32 devices in a mesh: member: 2 (over x), lon: 16 (over z, y, core).
Axes of the slice: x: 2, y: 2, z: 4, core: 2. Of those that a mesh axis runs over, the one named last changes fastest.
Arguments:
- right_side: float32 [512, 1024], P(('member', 'lon')), parts along dimension 0, may hold values from -72 to 72
- east_coef: float32 [256, 1024], P('lon'), may hold values from 0.5 to 2
- north_coef: float32 [256, 1024], P('lon'), may hold values from 0.5 to 2
- surface_term: float32 [256, 1024], P('lon'), may hold values from 0.02 to 1
- cell_mask: int32 [256, 1024], P('lon'), may hold values 0 or 1
- inverse_blocks: float32 [2048, 128, 128], P('lon'), may hold values from -0.2 to 0.2
- active_tiles: int32 [1536], replicated, may hold values from 0 to 2047, as said below
- low_bound: float32 [1], replicated, may hold values from 0.05 to 0.25
- high_bound: float32 [1], replicated, may hold values from 2 to 2.5
Outputs:
- solution_field: float32 [512, 1024], P(('member', 'lon')), parts along dimension 0
- residual: float32 [512, 1024], P(('member', 'lon')), parts along dimension 0
- norms: float32 [8], P('member'), parts along dimension 0
The draws below stay inside these ranges and needn't reach their ends.
There are 2 independent parts, one for each index of `member`. The reference program is written for one: setup_inputs(seed, part) draws one part's arguments, and reference() takes and returns one part's arrays. A program takes and returns all parts, laid end to end along the dimension named above; an argument that names none is the same for every part. Nothing has to cross between parts.
Inputs may be any that keep to these rules, and one draw needn't show every extreme that they name: `active_tiles`: sorted ascending and distinct. Tile g belongs to device g // 128 of lon. For each device i below 8, one of the devices i and i + 8 has all its 128 tiles listed and the other exactly 64 of them.
All inputs are finite; a program needn't handle non-finite values. No bound on the sum of `cell_mask` on one device may be relied on, other than what follows from the above.
Results may differ from the reference program's by a relative error of at most 0.0001.
Values sent between devices are 32-bit elements; how exact they have to be, the bound alone decides.
No kernel may reach another device: no remote copies, remote signals or barrier semaphores. Data moves between devices by JAX's collectives and lax.ppermute only.
A program may use at most 64 MiB of HBM per device.

```python
import math
import jax
import jax.numpy as jnp
from jax import lax

CX = 16
NY = 1024
TB = 128
ITERS = 4
NX = 256
TY = 8
TILES_DEV = 128
NTILES = 2048
ACTIVE = 1536
N_LON = 16


def draw_right_side(key, part):
    key = jax.random.fold_in(key, 5)
    first, second, third = jax.random.split(key, 3)
    col_scale = jnp.exp(jax.random.uniform(second, (NX, 1), jnp.float32, math.log(0.3), math.log(3.0)))
    row_scale = jnp.exp(jax.random.uniform(third, (1, NY), jnp.float32, math.log(0.3), math.log(3.0)))
    trend = 0.5 + 1.5 * jnp.arange(NX, dtype=jnp.float32)[:, None] / NX
    base = jnp.clip(jax.random.normal(first, (NX, NY), jnp.float32), -4.0, 4.0)
    return (base * col_scale * row_scale * trend).astype(jnp.float32)


def draw_inverse_blocks(key, part):
    key = jax.random.fold_in(key, 7)
    first, second, third = jax.random.split(key, 3)
    raw = jnp.clip(jax.random.normal(first, (NTILES, TB, TB), jnp.float32), -4.0, 4.0)
    sym = (raw + jnp.swapaxes(raw, 1, 2)) * 0.5 * (0.45 / math.sqrt(TB))
    ident = (jnp.arange(TB)[:, None] == jnp.arange(TB)[None, :]).astype(jnp.float32)
    diag_vals = 1.0 + 0.3 * jax.random.uniform(second, (NTILES, TB, 1), jnp.float32, -1.0, 1.0)
    tile_scale = 0.08 * jnp.exp(jax.random.uniform(third, (NTILES, 1, 1), jnp.float32, -0.3, 0.3))
    return (tile_scale * (sym * (1.0 - ident) + ident * diag_vals)).astype(jnp.float32)


def draw_active_tiles(key, part):
    key = jax.random.fold_in(key, 11)
    first, second = jax.random.split(key, 2)
    half_count = N_LON // 2
    pair_pick = jax.random.randint(first, (half_count,), 0, 2)
    full_flag = jnp.concatenate([pair_pick, 1 - pair_pick])
    device_keys = jax.random.split(second, N_LON)
    orders = jax.vmap(lambda one: jax.random.permutation(one, TILES_DEV))(device_keys)
    chosen = orders[:, :TILES_DEV // 2]
    picked = jnp.zeros((N_LON, TILES_DEV), jnp.int32).at[jnp.arange(N_LON)[:, None], chosen].set(1)
    keep = jnp.where(full_flag[:, None] == 1, 1, picked)
    flat = keep.reshape(-1)
    return jnp.nonzero(flat, size=ACTIVE)[0].astype(jnp.int32)


def touch_ends(array, own_key, smallest, largest):
    index_at = [jax.random.randint(jax.random.fold_in(own_key, axis), (), 0, length) for axis, length in enumerate(array.shape)]
    widest = array.shape.index(max(array.shape))
    neighbour = index_at[:widest] + [(index_at[widest] + 1) % array.shape[widest]] + index_at[widest + 1:]
    return array.at[tuple(index_at)].set(smallest).at[tuple(neighbour)].set(largest)


def block_levels(key, extent, pieces, least, high):
    level = 1.0
    for dim, shards_of in pieces:
        heights = jax.random.uniform(jax.random.fold_in(jax.random.fold_in(key, 6), dim), (shards_of,), jnp.float32, least / len(pieces), high / len(pieces))
        level = level * jnp.repeat(jnp.exp(heights), extent[dim] // shards_of).reshape((-1,) + (1,) * (len(extent) - 1 - dim))
    return level


def setup_inputs(seed: int = 0, part: int = 0) -> dict:
    seeds = jax.random.split(jax.random.key(seed), 10)
    part_keys = jax.random.split(jax.random.fold_in(seeds[9], part), 10)
    return {
        "right_side": draw_right_side(jax.random.fold_in(jax.random.fold_in(seeds[9], part), 71), part),
        "east_coef": jnp.clip(jnp.exp(math.log(2.0) - 1.3862944 * jax.random.uniform(seeds[1], (NX, NY), jnp.float32) ** block_levels(seeds[1], (NX, NY), ((0, 16),), -0.2, 0.2)), 0.5, 2.0),
        "north_coef": jnp.clip(jnp.exp(math.log(2.0) - 1.3862944 * jax.random.uniform(seeds[2], (NX, NY), jnp.float32) ** block_levels(seeds[2], (NX, NY), ((0, 16),), -0.2, 0.2)), 0.5, 2.0),
        "surface_term": jnp.clip(jnp.exp(math.log(1.0) - 3.912023 * jax.random.uniform(seeds[3], (NX, NY), jnp.float32) ** block_levels(seeds[3], (NX, NY), ((0, 16),), -0.2, 0.2)), 0.02, 1.0),
        "cell_mask": touch_ends((jax.random.randint(seeds[4], (NX, NY), 0, 8) < 7).astype(jnp.int32), jax.random.fold_in(seeds[4], 1), 0, 1),
        "inverse_blocks": draw_inverse_blocks(jax.random.fold_in(seeds[9], 71), part),
        "active_tiles": draw_active_tiles(jax.random.fold_in(seeds[9], 71), part),
        "low_bound": jnp.clip(jax.random.uniform(seeds[7], (1,), jnp.float32, 0.05, 0.25), 0.05, 0.25),
        "high_bound": jnp.clip(jax.random.uniform(seeds[8], (1,), jnp.float32, 2.0, 2.5), 2.0, 2.5),
    }


def tiles_of(field):
    return field.reshape(N_LON, CX, TILES_DEV, TY).transpose(0, 2, 1, 3).reshape(NTILES, TB)


def field_of(tiles):
    return tiles.reshape(N_LON, TILES_DEV, CX, TY).transpose(0, 2, 1, 3).reshape(NX, NY)


def reference(right_side, east_coef, north_coef, surface_term, cell_mask, inverse_blocks, active_tiles, low_bound, high_bound):
    flags = jnp.zeros((NTILES,), jnp.float32).at[active_tiles].set(1.0)
    tile_field = field_of(jnp.broadcast_to(flags[:, None], (NTILES, TB)))
    ocean = cell_mask.astype(jnp.float32) * tile_field
    zero_row = jnp.zeros((NX, 1), jnp.float32)
    east_faces = east_coef * ocean * jnp.roll(ocean, -1, axis=0)
    north_faces = north_coef * ocean * jnp.concatenate([ocean[:, 1:], zero_row], axis=1)
    west_faces = jnp.roll(east_faces, 1, axis=0)
    south_faces = jnp.concatenate([zero_row, north_faces[:, :-1]], axis=1)

    def operate(field):
        north_vals = jnp.concatenate([field[:, 1:], zero_row], axis=1)
        south_vals = jnp.concatenate([zero_row, field[:, :-1]], axis=1)
        total = surface_term * field
        total = total + east_faces * (field - jnp.roll(field, -1, axis=0))
        total = total + west_faces * (field - jnp.roll(field, 1, axis=0))
        total = total + north_faces * (field - north_vals)
        total = total + south_faces * (field - south_vals)
        return ocean * total

    def precondition(field):
        tiles = tiles_of(field)
        result = jnp.einsum("gij,gj->gi", inverse_blocks, tiles, precision=lax.Precision.HIGHEST)
        return ocean * field_of(result)

    center = (high_bound[0] + low_bound[0]) / 2.0
    radius = (high_bound[0] - low_bound[0]) / 2.0
    ratio = center / radius
    solution_field = jnp.zeros((NX, NY), jnp.float32)
    residual = ocean * right_side
    weight_prev = 1.0 / ratio
    direction = jnp.zeros((NX, NY), jnp.float32)
    norm_list = []
    for step in range(ITERS):
        search = precondition(residual)
        if step == 0:
            direction = search / center
        else:
            weight = 1.0 / (2.0 * ratio - weight_prev)
            direction = weight * weight_prev * direction + (2.0 * weight / radius) * search
            weight_prev = weight
        solution_field = solution_field + direction
        residual = residual - operate(direction)
        norm_list.append(jnp.sum(residual * residual) / (NX * NY))
    return solution_field, residual, jnp.stack(norm_list)
```

```python
import functools

import jax
import jax.numpy as jnp
from jax import lax
from jax.experimental import pallas as pl
from jax.experimental.pallas import tpu as pltpu
from jax.sharding import PartitionSpec as P

ITERS = 4
LANES = 128
SUBS = 8
F32 = jnp.float32
MIB = 2**20


def lane_blocks(rows):
    return rows // LANES


def roll(x, shift, axis):
    return pltpu.roll(x, shift % x.shape[axis], axis)


def repeat_row(row, times):
    return jnp.concatenate([row] * times, axis=1)


def gather_index():
    lane = lax.broadcasted_iota(jnp.int32, (SUBS, LANES), 1)
    sub = lax.broadcasted_iota(jnp.int32, (SUBS, LANES), 0)
    return (lane // SUBS) * SUBS + sub


def expand(field, block, index):
    part = field[:, block * LANES : (block + 1) * LANES]
    rows = [
        jnp.take_along_axis(jnp.broadcast_to(part[a : a + 1], (SUBS, LANES)), index, axis=1)
        for a in range(part.shape[0])
    ]
    return jnp.concatenate(rows, axis=0)


def blocks_product(bt_ref, field, out_ref):
    index = gather_index()
    columns, rows = field.shape
    for block in range(lane_blocks(rows)):
        spread = expand(field, block, index)
        for a in range(columns):
            out_ref[a : a + 1, block * LANES : (block + 1) * LANES] = jnp.sum(
                bt_ref[block, a] * spread, axis=0, keepdims=True
            )


def lane_partial(squares):
    total = jnp.sum(squares, axis=0, keepdims=True)
    parts = [total[:, i * LANES : (i + 1) * LANES] for i in range(total.shape[1] // LANES)]
    return functools.reduce(jnp.add, parts)


def tile_flags(active_ref, first, tiles):
    active = active_ref[...]
    before = jnp.sum((active < first).astype(jnp.int32))
    row = jnp.minimum(before // LANES, active_ref.shape[0] - 2)
    lane = lax.broadcasted_iota(jnp.int32, (LANES, tiles), 1) + first
    found = jnp.zeros((LANES, tiles), jnp.int32)
    for step in range(2):
        entries = jnp.broadcast_to(active_ref[pl.ds(row + step, 1), :], (LANES, LANES))
        found = found + (entries.T == lane).astype(jnp.int32)
    return (jnp.sum(found, axis=0, keepdims=True) > 0).astype(F32)


def first_kernel(
    device_ref, low_ref, high_ref, active_ref, right_ref, east_ref, north_ref, surface_ref, mask_ref, blocks_hbm,
    residual_ref, direction_ref, bt_ref, diag_ref, east_face_ref, north_face_ref, ocean_ref, coef_ref, up_ref, down_ref,
    raw, sems,
):
    columns, rows = right_ref.shape
    tiles = blocks_hbm.shape[0]
    count = lane_blocks(rows)
    step = tiles // count

    def fetch(i):
        part = pl.ds(i * step, step)
        return pltpu.make_async_copy(blocks_hbm.at[part], raw.at[part], sems.at[i])

    for i in range(count):
        fetch(i).start()
    low = jnp.full((1, LANES), low_ref[0], F32)
    high = jnp.full((1, LANES), high_ref[0], F32)
    center = (high + low) / 2.0
    radius = (high - low) / 2.0
    ratio = center / radius
    weight_prev = 1.0 / ratio
    coef_ref[0:1] = 1.0 / center
    for k in range(1, ITERS):
        weight = 1.0 / (2.0 * ratio - weight_prev)
        coef_ref[2 * k : 2 * k + 1] = weight * weight_prev
        coef_ref[2 * k + 1 : 2 * k + 2] = 2.0 * weight / radius
        weight_prev = weight
    flags = tile_flags(active_ref, device_ref[0] * tiles, tiles)
    lane = lax.broadcasted_iota(jnp.int32, (SUBS, LANES), 1)
    spread = [
        jnp.take_along_axis(jnp.broadcast_to(flags, (SUBS, tiles)), i * step + lane // SUBS, axis=1)
        for i in range(count)
    ]
    flag_lat = jnp.concatenate(spread, axis=1)[0:1]
    ocean = mask_ref[...].astype(F32) * flag_lat
    ocean_ref[...] = ocean
    lat = lax.broadcasted_iota(jnp.int32, (columns, rows), 1)
    lon = lax.broadcasted_iota(jnp.int32, (columns, rows), 0)
    east_ocean = east_ref[...] * ocean
    east_face = jnp.where(lon < columns - 1, east_ocean * roll(ocean, -1, 0), 0.0)
    north_face = jnp.where(lat < rows - 1, north_ref[...] * ocean * roll(ocean, -1, 1), 0.0)
    east_face_ref[...] = east_face
    north_face_ref[...] = north_face
    diag_ref[...] = surface_ref[...] * ocean + east_face + roll(east_face, 1, 0) + north_face + roll(north_face, 1, 1)
    residual = right_ref[...] * ocean
    residual_ref[...] = residual
    up_ref[1:2] = east_ocean[columns - 1 :]
    down_ref[1:2] = ocean[0:1]
    index = gather_index()
    for i in range(count):
        spread = expand(residual, i, index)
        fetch(i).wait()
        for a in range(columns):
            part = raw[i * step : (i + 1) * step, a * SUBS : (a + 1) * SUBS, :].reshape(LANES, LANES).T
            bt_ref[i, a] = part
            direction_ref[a : a + 1, i * LANES : (i + 1) * LANES] = jnp.sum(part * spread, axis=0, keepdims=True)
    direction = direction_ref[...] * ocean * repeat_row(coef_ref[0:1], count)
    direction_ref[...] = direction
    up_ref[0:1] = direction[columns - 1 :]
    down_ref[0:1] = direction[0:1]


def apply_operator(residual, direction, diag, east_face, north_face, west_term, east_term):
    flow = diag * direction
    flow = flow - east_face * roll(direction, -1, 0) - roll(east_face, 1, 0) * roll(direction, 1, 0)
    flow = flow - north_face * roll(direction, -1, 1) - roll(north_face, 1, 1) * roll(direction, 1, 1)
    lon = lax.broadcasted_iota(jnp.int32, residual.shape, 0)
    flow = jnp.where(lon == 0, flow - west_term, flow)
    flow = jnp.where(lon == residual.shape[0] - 1, flow - east_term, flow)
    return residual - flow


def search_step(bt_ref, residual, direction, ocean, coef_ref, k, search_ref, up_ref, down_ref, direction_out):
    count = lane_blocks(residual.shape[1])
    blocks_product(bt_ref, residual, search_ref)
    keep = repeat_row(coef_ref[2 * k : 2 * k + 1], count)
    gain = repeat_row(coef_ref[2 * k + 1 : 2 * k + 2], count)
    direction = keep * direction + gain * (ocean * search_ref[...])
    direction_out[...] = direction
    up_ref[...] = direction[-1:]
    down_ref[...] = direction[0:1]
    return direction


def second_kernel(
    west_ref, east_ref, residual_ref, direction_ref, diag_ref, east_face_ref, north_face_ref, ocean_ref, east_ocean_ref, coef_ref, bt_ref,
    residual_out, direction_out, solution_out, diag_out, faces_out, norms_out, up_ref, down_ref,
    search_ref,
):
    ocean = ocean_ref[...]
    direction = direction_ref[...]
    columns = ocean.shape[0]
    west_face = west_ref[1:2] * ocean[0:1]
    east_end = east_ocean_ref[1:2] * east_ref[1:2]
    faces_out[0:1] = west_face
    faces_out[1:2] = east_end
    lon = lax.broadcasted_iota(jnp.int32, ocean.shape, 0)
    diag = diag_ref[...]
    diag = jnp.where(lon == 0, diag + west_face, diag)
    diag = jnp.where(lon == columns - 1, diag + east_end, diag)
    diag_out[...] = diag
    residual = apply_operator(
        residual_ref[...], direction, diag, east_face_ref[...], north_face_ref[...],
        west_face * west_ref[0:1], east_end * east_ref[0:1],
    )
    residual_out[...] = residual
    norms_out[...] = jnp.zeros_like(norms_out)
    norms_out[0:1] = lane_partial(residual * residual)
    later = search_step(bt_ref, residual, direction, ocean, coef_ref, 1, search_ref, up_ref, down_ref, direction_out)
    solution_out[...] = direction + later


def middle_kernel(
    k,
    west_ref, east_ref, residual_ref, direction_ref, solution_ref, diag_ref, east_face_ref, north_face_ref, ocean_ref, faces_ref, coef_ref, norms_ref, bt_ref,
    residual_out, direction_out, solution_out, norms_out, up_ref, down_ref,
    search_ref,
):
    direction = direction_ref[...]
    residual = apply_operator(
        residual_ref[...], direction, diag_ref[...], east_face_ref[...], north_face_ref[...],
        faces_ref[0:1] * west_ref[...], faces_ref[1:2] * east_ref[...],
    )
    residual_out[...] = residual
    norms_out[...] = norms_ref[...]
    norms_out[k - 1 : k] = lane_partial(residual * residual)
    later = search_step(bt_ref, residual, direction, ocean_ref[...], coef_ref, k, search_ref, up_ref, down_ref, direction_out)
    solution_out[...] = solution_ref[...] + later


def last_kernel(
    west_ref, east_ref, residual_ref, direction_ref, diag_ref, east_face_ref, north_face_ref, faces_ref, norms_ref,
    residual_out, norms_out,
):
    residual = apply_operator(
        residual_ref[...], direction_ref[...], diag_ref[...], east_face_ref[...], north_face_ref[...],
        faces_ref[0:1] * west_ref[...], faces_ref[1:2] * east_ref[...],
    )
    residual_out[...] = residual
    norms_out[...] = norms_ref[...]
    norms_out[ITERS - 1 : ITERS] = lane_partial(residual * residual)


def vmem():
    return pl.BlockSpec(memory_space=pltpu.VMEM)


def smem():
    return pl.BlockSpec(memory_space=pltpu.SMEM)


def shape(*dims):
    return jax.ShapeDtypeStruct(dims, F32)


def call(body, in_specs, outs, scratch, limit):
    return pl.pallas_call(
        body,
        in_specs=in_specs,
        out_specs=[vmem()] * len(outs),
        out_shape=outs,
        scratch_shapes=scratch,
        compiler_params=pltpu.CompilerParams(vmem_limit_bytes=limit),
    )


def exchange(up, down):
    devices = lax.axis_size("lon")
    ahead = [(i, (i + 1) % devices) for i in range(devices)]
    back = [(j, i) for i, j in ahead]
    return lax.ppermute(up, "lon", ahead), lax.ppermute(down, "lon", back)


def reduce_stages(total):
    devices = lax.axis_size("lon")
    stride = 1
    while stride < devices:
        left = devices // stride
        radix = 4 if left % 4 == 0 else 2
        parts = [
            lax.ppermute(total, "lon", [(i, i ^ (s * stride)) for i in range(devices)])
            for s in range(1, radix)
        ]
        total = functools.reduce(jnp.add, parts, total)
        stride *= radix
    return total


def on_device(
    right_side, east_coef, north_coef, surface_term, cell_mask, inverse_blocks, active_tiles, low_bound, high_bound
):
    columns, rows = right_side.shape
    tiles = inverse_blocks.shape[0]
    count = lane_blocks(rows)
    cells_all = columns * lax.axis_size("lon") * rows
    device = lax.axis_index("lon").astype(jnp.int32).reshape(1)
    field = shape(columns, rows)
    norm_shape = shape(SUBS, LANES)
    row = shape(1, rows)
    two = shape(2, rows)
    bt_shape = shape(count, columns, LANES, LANES)
    residual, direction, bt, diag, east_face, north_face, ocean, coef, up, down = call(
        first_kernel,
        [smem()] * 3 + [vmem()] * 6 + [pl.BlockSpec(memory_space=pl.ANY)],
        [field, field, bt_shape, field, field, field, field, norm_shape, two, two],
        [pltpu.VMEM(inverse_blocks.shape, F32), pltpu.SemaphoreType.DMA((count,))],
        40 * MIB,
    )(
        device, low_bound, high_bound, active_tiles.reshape(-1, LANES), right_side, east_coef, north_coef, surface_term,
        cell_mask, inverse_blocks,
    )
    west, east = exchange(up, down)
    residual, direction, answer, diag, faces, norms, up2, down2 = call(
        second_kernel,
        [vmem()] * 11,
        [field, field, field, field, two, norm_shape, row, row],
        [pltpu.VMEM((columns, rows), F32)],
        24 * MIB,
    )(west, east, residual, direction, diag, east_face, north_face, ocean, up, coef, bt)
    for k in range(2, ITERS):
        west, east = exchange(up2, down2)
        residual, direction, answer, norms, up2, down2 = call(
            functools.partial(middle_kernel, k),
            [vmem()] * 13,
            [field, field, field, norm_shape, row, row],
            [pltpu.VMEM((columns, rows), F32)],
            24 * MIB,
        )(west, east, residual, direction, answer, diag, east_face, north_face, ocean, faces, coef, norms, bt)
    west, east = exchange(up2, down2)
    residual, norms = call(last_kernel, [vmem()] * 9, [field, norm_shape], [], 24 * MIB)(
        west, east, residual, direction, diag, east_face, north_face, faces, norms
    )
    norms = reduce_stages(norms)
    return answer, residual, jnp.sum(norms[:ITERS], axis=1) / cells_all


def solution(mesh):
    in_specs = (
        P(("member", "lon"), None),
        P("lon", None),
        P("lon", None),
        P("lon", None),
        P("lon", None),
        P("lon", None, None),
        P(),
        P(),
        P(),
    )
    out_specs = (P(("member", "lon"), None), P(("member", "lon"), None), P("member"))
    return jax.shard_map(on_device, mesh=mesh, in_specs=in_specs, out_specs=out_specs, check_vma=False)
```

```python
import functools

import jax
import jax.numpy as jnp
from jax import lax
from jax.experimental import pallas as pl
from jax.experimental.pallas import tpu as pltpu
from jax.sharding import PartitionSpec as P

ITERS = 4
LANES = 128
SUBS = 8
F32 = jnp.float32
MIB = 2**20


def lane_blocks(rows):
    return rows // LANES


def roll(x, shift, axis):
    return pltpu.roll(x, shift % x.shape[axis], axis)


def repeat_row(row, times):
    return jnp.concatenate([row] * times, axis=1)


def gather_index():
    lane = lax.broadcasted_iota(jnp.int32, (SUBS, LANES), 1)
    sub = lax.broadcasted_iota(jnp.int32, (SUBS, LANES), 0)
    return (lane // SUBS) * SUBS + sub


def expand(field, block, index):
    part = field[:, block * LANES : (block + 1) * LANES]
    rows = [
        jnp.take_along_axis(jnp.broadcast_to(part[a : a + 1], (SUBS, LANES)), index, axis=1)
        for a in range(part.shape[0])
    ]
    return jnp.concatenate(rows, axis=0)


def blocks_product(bt_ref, field, out_ref):
    index = gather_index()
    columns, rows = field.shape
    for block in range(lane_blocks(rows)):
        spread = expand(field, block, index)
        for a in range(columns):
            out_ref[a : a + 1, block * LANES : (block + 1) * LANES] = jnp.sum(
                bt_ref[block, a] * spread, axis=0, keepdims=True
            )


def even_device():
    return lax.rem(lax.axis_index("lon"), 2) == 0


def store_edges(inner_ref, outer_ref, row, even, first, last):
    inner_ref[row : row + 1] = jnp.where(even, last, first)
    outer_ref[row : row + 1] = jnp.where(even, first, last)


def halo_rows(inner_ref, outer_ref, row, even):
    inner, outer = inner_ref[row : row + 1], outer_ref[row : row + 1]
    return jnp.where(even, outer, inner), jnp.where(even, inner, outer)


def lane_partial(squares):
    total = jnp.sum(squares, axis=0, keepdims=True)
    parts = [total[:, i * LANES : (i + 1) * LANES] for i in range(total.shape[1] // LANES)]
    return functools.reduce(jnp.add, parts)


def tile_flags(active_ref, first, tiles):
    active = active_ref[...]
    before = jnp.sum((active < first).astype(jnp.int32))
    row = jnp.minimum(before // LANES, active_ref.shape[0] - 2)
    lane = lax.broadcasted_iota(jnp.int32, (LANES, tiles), 1) + first
    found = jnp.zeros((LANES, tiles), jnp.int32)
    for step in range(2):
        entries = jnp.broadcast_to(active_ref[pl.ds(row + step, 1), :], (LANES, LANES))
        found = found + (entries.T == lane).astype(jnp.int32)
    return (jnp.sum(found, axis=0, keepdims=True) > 0).astype(F32)


def transpose_kernel(blocks_hbm, bt_ref, raw, sems):
    count, columns = bt_ref.shape[:2]
    step = blocks_hbm.shape[0] // count

    def fetch(i):
        part = pl.ds(i * step, step)
        return pltpu.make_async_copy(blocks_hbm.at[part], raw.at[part], sems.at[i])

    for i in range(count):
        fetch(i).start()
    for i in range(count):
        fetch(i).wait()
        for a in range(columns):
            bt_ref[i, a] = raw[i * step : (i + 1) * step, a * SUBS : (a + 1) * SUBS, :].reshape(LANES, LANES).T


def first_kernel(
    low_ref, high_ref, active_ref, right_ref, east_ref, north_ref, surface_ref, mask_ref, bt_ref,
    residual_ref, direction_ref, diag_ref, east_face_ref, north_face_ref, ocean_ref, east_end_ref, coef_ref, inner_ref, outer_ref,
):
    columns, rows = right_ref.shape
    count = lane_blocks(rows)
    tiles = rows // SUBS
    even = even_device()
    low = jnp.broadcast_to(low_ref[...].reshape(1, 1), (1, LANES))
    high = jnp.broadcast_to(high_ref[...].reshape(1, 1), (1, LANES))
    center = (high + low) / 2.0
    radius = (high - low) / 2.0
    ratio = center / radius
    weight_prev = 1.0 / ratio
    coef_ref[0:1] = 1.0 / center
    for k in range(1, ITERS):
        weight = 1.0 / (2.0 * ratio - weight_prev)
        coef_ref[2 * k : 2 * k + 1] = weight * weight_prev
        coef_ref[2 * k + 1 : 2 * k + 2] = 2.0 * weight / radius
        weight_prev = weight
    flags = tile_flags(active_ref, lax.axis_index("lon") * tiles, tiles)
    lane = lax.broadcasted_iota(jnp.int32, (SUBS, LANES), 1)
    spread = [
        jnp.take_along_axis(jnp.broadcast_to(flags, (SUBS, tiles)), i * (LANES // SUBS) + lane // SUBS, axis=1)
        for i in range(count)
    ]
    flag_lat = jnp.concatenate(spread, axis=1)[0:1]
    ocean = mask_ref[...].astype(F32) * flag_lat
    ocean_ref[...] = ocean
    lat = lax.broadcasted_iota(jnp.int32, (columns, rows), 1)
    lon = lax.broadcasted_iota(jnp.int32, (columns, rows), 0)
    east_ocean = east_ref[...] * ocean
    east_face = jnp.where(lon < columns - 1, east_ocean * roll(ocean, -1, 0), 0.0)
    north_face = jnp.where(lat < rows - 1, north_ref[...] * ocean * roll(ocean, -1, 1), 0.0)
    east_face_ref[...] = east_face
    north_face_ref[...] = north_face
    diag_ref[...] = surface_ref[...] * ocean + east_face + roll(east_face, 1, 0) + north_face + roll(north_face, 1, 1)
    residual = right_ref[...] * ocean
    residual_ref[...] = residual
    east_end_ref[...] = east_ocean[columns - 1 :]
    store_edges(inner_ref, outer_ref, 1, even, ocean[0:1], east_ocean[columns - 1 :])
    blocks_product(bt_ref, residual, direction_ref)
    direction = direction_ref[...] * ocean * repeat_row(coef_ref[0:1], count)
    direction_ref[...] = direction
    store_edges(inner_ref, outer_ref, 0, even, direction[0:1], direction[columns - 1 :])


def apply_operator(residual, direction, diag, east_face, north_face, west_term, east_term):
    flow = diag * direction
    flow = flow - east_face * roll(direction, -1, 0) - roll(east_face, 1, 0) * roll(direction, 1, 0)
    flow = flow - north_face * roll(direction, -1, 1) - roll(north_face, 1, 1) * roll(direction, 1, 1)
    lon = lax.broadcasted_iota(jnp.int32, residual.shape, 0)
    flow = jnp.where(lon == 0, flow - west_term, flow)
    flow = jnp.where(lon == residual.shape[0] - 1, flow - east_term, flow)
    return residual - flow


def search_step(bt_ref, residual, direction, ocean, coef_ref, k, search_ref, inner_out, outer_out, direction_out):
    count = lane_blocks(residual.shape[1])
    blocks_product(bt_ref, residual, search_ref)
    keep = repeat_row(coef_ref[2 * k : 2 * k + 1], count)
    gain = repeat_row(coef_ref[2 * k + 1 : 2 * k + 2], count)
    direction = keep * direction + gain * (ocean * search_ref[...])
    direction_out[...] = direction
    store_edges(inner_out, outer_out, 0, even_device(), direction[0:1], direction[-1:])
    return direction


def second_kernel(
    inner_ref, outer_ref, residual_ref, direction_ref, diag_ref, east_face_ref, north_face_ref, ocean_ref, east_end_ref, coef_ref, bt_ref,
    residual_out, direction_out, solution_out, diag_out, faces_out, norms_out, inner_out, outer_out,
    search_ref,
):
    ocean = ocean_ref[...]
    direction = direction_ref[...]
    columns = ocean.shape[0]
    even = even_device()
    west, east = halo_rows(inner_ref, outer_ref, 0, even)
    west_static, east_static = halo_rows(inner_ref, outer_ref, 1, even)
    west_face = west_static * ocean[0:1]
    east_end = east_end_ref[...] * east_static
    faces_out[0:1] = west_face
    faces_out[1:2] = east_end
    lon = lax.broadcasted_iota(jnp.int32, ocean.shape, 0)
    diag = diag_ref[...]
    diag = jnp.where(lon == 0, diag + west_face, diag)
    diag = jnp.where(lon == columns - 1, diag + east_end, diag)
    diag_out[...] = diag
    residual = apply_operator(
        residual_ref[...], direction, diag, east_face_ref[...], north_face_ref[...],
        west_face * west, east_end * east,
    )
    residual_out[...] = residual
    norms_out[...] = jnp.zeros_like(norms_out)
    norms_out[0:1] = lane_partial(residual * residual)
    later = search_step(bt_ref, residual, direction, ocean, coef_ref, 1, search_ref, inner_out, outer_out, direction_out)
    solution_out[...] = direction + later


def middle_kernel(
    k,
    inner_ref, outer_ref, residual_ref, direction_ref, solution_ref, diag_ref, east_face_ref, north_face_ref, ocean_ref, faces_ref, coef_ref, norms_ref, bt_ref,
    residual_out, direction_out, solution_out, norms_out, inner_out, outer_out,
    search_ref,
):
    direction = direction_ref[...]
    west, east = halo_rows(inner_ref, outer_ref, 0, even_device())
    residual = apply_operator(
        residual_ref[...], direction, diag_ref[...], east_face_ref[...], north_face_ref[...],
        faces_ref[0:1] * west, faces_ref[1:2] * east,
    )
    residual_out[...] = residual
    norms_out[...] = norms_ref[...]
    norms_out[k - 1 : k] = lane_partial(residual * residual)
    later = search_step(bt_ref, residual, direction, ocean_ref[...], coef_ref, k, search_ref, inner_out, outer_out, direction_out)
    solution_out[...] = solution_ref[...] + later


def last_kernel(
    inner_ref, outer_ref, residual_ref, direction_ref, diag_ref, east_face_ref, north_face_ref, faces_ref, norms_ref,
    residual_out, norms_out,
):
    west, east = halo_rows(inner_ref, outer_ref, 0, even_device())
    residual = apply_operator(
        residual_ref[...], direction_ref[...], diag_ref[...], east_face_ref[...], north_face_ref[...],
        faces_ref[0:1] * west, faces_ref[1:2] * east,
    )
    residual_out[...] = residual
    norms_out[...] = norms_ref[...]
    norms_out[ITERS - 1 : ITERS] = lane_partial(residual * residual)


def vmem():
    return pl.BlockSpec(memory_space=pltpu.VMEM)


def shape(*dims):
    return jax.ShapeDtypeStruct(dims, F32)


def call(body, in_specs, outs, scratch, limit, cost=None):
    return pl.pallas_call(
        body,
        in_specs=in_specs,
        out_specs=[vmem()] * len(outs),
        out_shape=outs,
        scratch_shapes=scratch,
        compiler_params=pltpu.CompilerParams(vmem_limit_bytes=limit),
        cost_estimate=cost,
    )


def exchange(inner, outer):
    devices = lax.axis_size("lon")
    pairs = [(i, i ^ 1) for i in range(devices)]
    across = [(i, (i + 1 if i % 2 else i - 1) % devices) for i in range(devices)]
    return lax.ppermute(inner, "lon", pairs), lax.ppermute(outer, "lon", across)


def reduce_stages(total):
    devices = lax.axis_size("lon")
    stride = 1
    while stride < devices:
        left = devices // stride
        radix = 4 if left % 4 == 0 else 2
        parts = [
            lax.ppermute(total, "lon", [(i, i ^ (s * stride)) for i in range(devices)])
            for s in range(1, radix)
        ]
        total = functools.reduce(jnp.add, parts, total)
        stride *= radix
    return total


def on_device(
    right_side, east_coef, north_coef, surface_term, cell_mask, inverse_blocks, active_tiles, low_bound, high_bound
):
    columns, rows = right_side.shape
    tiles = inverse_blocks.shape[0]
    count = lane_blocks(rows)
    cells_all = columns * lax.axis_size("lon") * rows
    field = shape(columns, rows)
    norm_shape = shape(SUBS, LANES)
    row = shape(1, rows)
    two = shape(2, rows)
    bt_shape = shape(count, columns, LANES, LANES)
    (bt,) = call(
        transpose_kernel,
        [pl.BlockSpec(memory_space=pl.ANY)],
        [bt_shape],
        [pltpu.VMEM(inverse_blocks.shape, F32), pltpu.SemaphoreType.DMA((count,))],
        40 * MIB,
        pl.CostEstimate(flops=10**9, bytes_accessed=2 * inverse_blocks.size * 4, transcendentals=0),
    )(inverse_blocks)
    residual, direction, diag, east_face, north_face, ocean, east_end, coef, inner, outer = call(
        first_kernel,
        [vmem()] * 9,
        [field, field, field, field, field, field, row, norm_shape, two, two],
        [],
        24 * MIB,
    )(
        low_bound, high_bound, active_tiles.reshape(-1, LANES),
        right_side, east_coef, north_coef, surface_term, cell_mask, bt,
    )
    inner, outer = exchange(inner, outer)
    residual, direction, answer, diag, faces, norms, inner, outer = call(
        second_kernel,
        [vmem()] * 11,
        [field, field, field, field, two, norm_shape, row, row],
        [pltpu.VMEM((columns, rows), F32)],
        24 * MIB,
    )(inner, outer, residual, direction, diag, east_face, north_face, ocean, east_end, coef, bt)
    for k in range(2, ITERS):
        inner, outer = exchange(inner, outer)
        residual, direction, answer, norms, inner, outer = call(
            functools.partial(middle_kernel, k),
            [vmem()] * 13,
            [field, field, field, norm_shape, row, row],
            [pltpu.VMEM((columns, rows), F32)],
            24 * MIB,
        )(inner, outer, residual, direction, answer, diag, east_face, north_face, ocean, faces, coef, norms, bt)
    inner, outer = exchange(inner, outer)
    residual, norms = call(last_kernel, [vmem()] * 9, [field, norm_shape], [], 24 * MIB)(
        inner, outer, residual, direction, diag, east_face, north_face, faces, norms
    )
    norms = reduce_stages(norms)
    return answer, residual, jnp.sum(norms[:ITERS], axis=1) / cells_all


def solution(mesh):
    in_specs = (
        P(("member", "lon"), None),
        P("lon", None),
        P("lon", None),
        P("lon", None),
        P("lon", None),
        P("lon", None, None),
        P(),
        P(),
        P(),
    )
    out_specs = (P(("member", "lon"), None), P(("member", "lon"), None), P("member"))
    return jax.shard_map(on_device, mesh=mesh, in_specs=in_specs, out_specs=out_specs, check_vma=False)
```

```python
import functools

import jax
import jax.numpy as jnp
from jax import lax
from jax.experimental import pallas as pl
from jax.experimental.pallas import tpu as pltpu
from jax.sharding import PartitionSpec as P

ITERS = 4
LANES = 128
SUBS = 8
F32 = jnp.float32
MIB = 2**20


def lane_blocks(rows):
    return rows // LANES


def roll(x, shift, axis):
    return pltpu.roll(x, shift % x.shape[axis], axis)


def repeat_row(row, times):
    return jnp.concatenate([row] * times, axis=1)


def gather_index():
    lane = lax.broadcasted_iota(jnp.int32, (SUBS, LANES), 1)
    sub = lax.broadcasted_iota(jnp.int32, (SUBS, LANES), 0)
    return (lane // SUBS) * SUBS + sub


def expand(field, block, index):
    part = field[:, block * LANES : (block + 1) * LANES]
    rows = [
        jnp.take_along_axis(jnp.broadcast_to(part[a : a + 1], (SUBS, LANES)), index, axis=1)
        for a in range(part.shape[0])
    ]
    return jnp.concatenate(rows, axis=0)


def blocks_product(bt_ref, field, out_ref):
    index = gather_index()
    columns, rows = field.shape
    for block in range(lane_blocks(rows)):
        spread = expand(field, block, index)
        for a in range(columns):
            out_ref[a : a + 1, block * LANES : (block + 1) * LANES] = jnp.sum(
                bt_ref[block, a] * spread, axis=0, keepdims=True
            )


def even_device():
    return lax.rem(lax.axis_index("lon"), 2) == 0


def store_edges(inner_ref, outer_ref, row, even, first, last):
    inner_ref[row : row + 1] = jnp.where(even, last, first)
    outer_ref[row : row + 1] = jnp.where(even, first, last)


def halo_rows(inner_ref, outer_ref, row, even):
    inner, outer = inner_ref[row : row + 1], outer_ref[row : row + 1]
    return jnp.where(even, outer, inner), jnp.where(even, inner, outer)


def lane_partial(squares):
    total = jnp.sum(squares, axis=0, keepdims=True)
    parts = [total[:, i * LANES : (i + 1) * LANES] for i in range(total.shape[1] // LANES)]
    return functools.reduce(jnp.add, parts)


def tile_flags(active_ref, first, tiles):
    active = active_ref[...]
    before = jnp.sum((active < first).astype(jnp.int32))
    row = jnp.minimum(before // LANES, active_ref.shape[0] - 2)
    lane = lax.broadcasted_iota(jnp.int32, (LANES, tiles), 1) + first
    found = jnp.zeros((LANES, tiles), jnp.int32)
    for step in range(2):
        entries = jnp.broadcast_to(active_ref[pl.ds(row + step, 1), :], (LANES, LANES))
        found = found + (entries.T == lane).astype(jnp.int32)
    return (jnp.sum(found, axis=0, keepdims=True) > 0).astype(F32)


def transpose_kernel(blocks_hbm, bt_ref, raw, sems):
    count, columns = bt_ref.shape[:2]
    step = blocks_hbm.shape[0] // count

    def fetch(i):
        part = pl.ds(i * step, step)
        return pltpu.make_async_copy(blocks_hbm.at[part], raw.at[part], sems.at[i])

    for i in range(count):
        fetch(i).start()
    for i in range(count):
        fetch(i).wait()
        for a in range(columns):
            bt_ref[i, a] = raw[i * step : (i + 1) * step, a * SUBS : (a + 1) * SUBS, :].reshape(LANES, LANES).T


def first_kernel(
    active_ref, right_ref, east_ref, north_ref, surface_ref, mask_ref, bt_ref,
    residual_ref, search_ref, diag_ref, east_face_ref, north_face_ref, ocean_ref, east_end_ref, inner_ref, outer_ref,
):
    columns, rows = right_ref.shape
    count = lane_blocks(rows)
    tiles = rows // SUBS
    even = even_device()
    flags = tile_flags(active_ref, lax.axis_index("lon") * tiles, tiles)
    lane = lax.broadcasted_iota(jnp.int32, (SUBS, LANES), 1)
    spread = [
        jnp.take_along_axis(jnp.broadcast_to(flags, (SUBS, tiles)), i * (LANES // SUBS) + lane // SUBS, axis=1)
        for i in range(count)
    ]
    flag_lat = jnp.concatenate(spread, axis=1)[0:1]
    ocean = mask_ref[...].astype(F32) * flag_lat
    ocean_ref[...] = ocean
    lat = lax.broadcasted_iota(jnp.int32, (columns, rows), 1)
    lon = lax.broadcasted_iota(jnp.int32, (columns, rows), 0)
    east_ocean = east_ref[...] * ocean
    east_face = jnp.where(lon < columns - 1, east_ocean * roll(ocean, -1, 0), 0.0)
    north_face = jnp.where(lat < rows - 1, north_ref[...] * ocean * roll(ocean, -1, 1), 0.0)
    east_face_ref[...] = east_face
    north_face_ref[...] = north_face
    diag_ref[...] = surface_ref[...] * ocean + east_face + roll(east_face, 1, 0) + north_face + roll(north_face, 1, 1)
    residual = right_ref[...] * ocean
    residual_ref[...] = residual
    east_end_ref[...] = east_ocean[columns - 1 :]
    store_edges(inner_ref, outer_ref, 1, even, ocean[0:1], east_ocean[columns - 1 :])
    blocks_product(bt_ref, residual, search_ref)
    search = search_ref[...] * ocean
    search_ref[...] = search
    store_edges(inner_ref, outer_ref, 0, even, search[0:1], search[columns - 1 :])


def apply_operator(residual, direction, diag, east_face, north_face, west_term, east_term):
    flow = diag * direction
    flow = flow - east_face * roll(direction, -1, 0) - roll(east_face, 1, 0) * roll(direction, 1, 0)
    flow = flow - north_face * roll(direction, -1, 1) - roll(north_face, 1, 1) * roll(direction, 1, 1)
    lon = lax.broadcasted_iota(jnp.int32, residual.shape, 0)
    flow = jnp.where(lon == 0, flow - west_term, flow)
    flow = jnp.where(lon == residual.shape[0] - 1, flow - east_term, flow)
    return residual - flow


def search_step(bt_ref, residual, direction, ocean, coef_ref, k, search_ref):
    count = lane_blocks(residual.shape[1])
    blocks_product(bt_ref, residual, search_ref)
    keep = repeat_row(coef_ref[2 * k : 2 * k + 1], count)
    gain = repeat_row(coef_ref[2 * k + 1 : 2 * k + 2], count)
    return keep * direction + gain * (ocean * search_ref[...])


def store_coefficients(low_ref, high_ref, coef_ref):
    low = jnp.full((1, LANES), low_ref[0], F32)
    high = jnp.full((1, LANES), high_ref[0], F32)
    center = (high + low) / 2.0
    radius = (high - low) / 2.0
    ratio = center / radius
    weight_prev = 1.0 / ratio
    coef_ref[0:1] = 1.0 / center
    for k in range(1, ITERS):
        weight = 1.0 / (2.0 * ratio - weight_prev)
        coef_ref[2 * k : 2 * k + 1] = weight * weight_prev
        coef_ref[2 * k + 1 : 2 * k + 2] = 2.0 * weight / radius
        weight_prev = weight


def second_kernel(
    low_ref, high_ref, inner_ref, outer_ref, residual_ref, search_in, diag_ref, east_face_ref, north_face_ref, ocean_ref, east_end_ref, bt_ref,
    residual_out, direction_out, solution_out, diag_out, faces_out, norms_out, coef_out, inner_out, outer_out,
    search_ref,
):
    store_coefficients(low_ref, high_ref, coef_out)
    ocean = ocean_ref[...]
    columns, rows = ocean.shape
    scale = repeat_row(coef_out[0:1], lane_blocks(rows))
    direction = search_in[...] * scale
    even = even_device()
    west, east = halo_rows(inner_ref, outer_ref, 0, even)
    west_static, east_static = halo_rows(inner_ref, outer_ref, 1, even)
    west_face = west_static * ocean[0:1]
    east_end = east_end_ref[...] * east_static
    faces_out[0:1] = west_face
    faces_out[1:2] = east_end
    lon = lax.broadcasted_iota(jnp.int32, ocean.shape, 0)
    diag = diag_ref[...]
    diag = jnp.where(lon == 0, diag + west_face, diag)
    diag = jnp.where(lon == columns - 1, diag + east_end, diag)
    diag_out[...] = diag
    residual = apply_operator(
        residual_ref[...], direction, diag, east_face_ref[...], north_face_ref[...],
        west_face * (scale * west), east_end * (scale * east),
    )
    residual_out[...] = residual
    norms_out[...] = jnp.zeros_like(norms_out)
    norms_out[0:1, 0:LANES] = lane_partial(residual * residual)
    later = search_step(bt_ref, residual, direction, ocean, coef_out, 1, search_ref)
    direction_out[...] = later
    store_edges(inner_out, outer_out, 0, even, later[0:1], later[columns - 1 :])
    solution_out[...] = direction + later


def advance(k, west, east, residual_ref, direction_ref, solution_ref, diag_ref, east_face_ref, north_face_ref, ocean_ref, faces_ref, coef_ref, bt_ref, search_ref):
    direction = direction_ref[...]
    residual = apply_operator(
        residual_ref[...], direction, diag_ref[...], east_face_ref[...], north_face_ref[...],
        faces_ref[0:1] * west, faces_ref[1:2] * east,
    )
    later = search_step(bt_ref, residual, direction, ocean_ref[...], coef_ref, k, search_ref)
    return residual, later, solution_ref[...] + later


def store_norm(norms_out, norms_ref, k, squares):
    norms_out[...] = norms_ref[...]
    norms_out[0:1, k * LANES : (k + 1) * LANES] = lane_partial(squares)


def middle_kernel(
    k,
    inner_ref, outer_ref, residual_ref, direction_ref, solution_ref, diag_ref, east_face_ref, north_face_ref, ocean_ref, faces_ref, coef_ref, norms_ref, bt_ref,
    residual_out, direction_out, solution_out, norms_out, inner_out, outer_out,
    search_ref,
):
    even = even_device()
    west, east = halo_rows(inner_ref, outer_ref, 0, even)
    residual, later, answer = advance(
        k, west, east, residual_ref, direction_ref, solution_ref, diag_ref, east_face_ref, north_face_ref, ocean_ref, faces_ref, coef_ref, bt_ref, search_ref
    )
    residual_out[...] = residual
    store_norm(norms_out, norms_ref, k - 1, residual * residual)
    direction_out[...] = later
    store_edges(inner_out, outer_out, 0, even, later[0:1], later[-1:])
    solution_out[...] = answer


FIRST_RES, FIRST_DIR, LAST_RES, LAST_DIR, LAST_FACE, SUMS, PACK_ROWS = 0, 1, 2, 3, 4, 5, 8


def closing_kernel(
    inner_ref, outer_ref, residual_ref, direction_ref, solution_ref, diag_ref, east_face_ref, north_face_ref, ocean_ref, faces_ref, coef_ref, norms_ref, bt_ref,
    residual_out, solution_out, pack_out,
    search_ref,
):
    west, east = halo_rows(inner_ref, outer_ref, 0, even_device())
    residual, later, answer = advance(
        ITERS - 1, west, east, residual_ref, direction_ref, solution_ref, diag_ref, east_face_ref, north_face_ref, ocean_ref, faces_ref, coef_ref, bt_ref, search_ref
    )
    solution_out[...] = answer
    columns = residual.shape[0]
    sums = pack_out.at[SUMS : SUMS + 1]
    store_norm(sums, norms_ref, ITERS - 2, residual * residual)
    nothing = jnp.zeros_like(west)
    residual = apply_operator(residual, later, diag_ref[...], east_face_ref[...], north_face_ref[...], nothing, nothing)
    residual_out[...] = residual
    lon = lax.broadcasted_iota(jnp.int32, residual.shape, 0)
    inside = jnp.where((lon > 0) & (lon < columns - 1), residual, 0.0)
    sums[0:1, (ITERS - 1) * LANES : ITERS * LANES] = lane_partial(inside * inside)
    pack_out[FIRST_RES : FIRST_RES + 1] = residual[0:1]
    pack_out[FIRST_DIR : FIRST_DIR + 1] = later[0:1]
    pack_out[LAST_RES : LAST_RES + 1] = residual[columns - 1 :]
    pack_out[LAST_DIR : LAST_DIR + 1] = later[columns - 1 :]
    pack_out[LAST_FACE : LAST_FACE + 1] = faces_ref[1:2]
    pack_out[SUMS + 1 :] = jnp.zeros_like(pack_out[SUMS + 1 :])


def join_packs(size, radix, is_last, pack_ref, others, halo, packs):
    me = lax.axis_index("lon")
    mine = lax.rem(me // size, radix)
    packs[mine] = pack_ref[...]
    for s, other in enumerate(others, start=1):
        packs[mine ^ s] = other[...]

    def row(run, name):
        return packs[run % radix, name : name + 1, :]

    sums = functools.reduce(jnp.add, [row(run, SUMS) for run in range(radix)])
    total = None
    for run in range(radix if is_last else radix - 1):
        face = row(run, LAST_FACE)
        left = row(run, LAST_RES) + face * row(run + 1, FIRST_DIR)
        right = row(run + 1, FIRST_RES) + face * row(run, LAST_DIR)
        squares = lane_partial(left * left + right * right)
        total = squares if total is None else total + squares
    parts = [sums[:, i * LANES : (i + 1) * LANES] for i in range(sums.shape[1] // LANES)]
    parts[ITERS - 1] = parts[ITERS - 1] + total
    before = packs[lax.rem(mine + radix - 1, radix)][LAST_DIR : LAST_DIR + 1]
    after = packs[lax.rem(mine + 1, radix)][FIRST_DIR : FIRST_DIR + 1]
    place = lax.rem(me, size)
    west_now = place == 0
    east_now = place == size - 1
    if not is_last:
        west_now = west_now & (mine > 0)
        east_now = east_now & (mine < radix - 1)
    west, east = halo
    return parts, jnp.where(west_now, before, west), jnp.where(east_now, after, east)


def stage_kernel(size, radix, *refs):
    pack_ref, others, halo_ref = refs[0], refs[1:radix], refs[radix] if size > 1 else None
    pack_out, halo_out, packs = refs[-3:]
    nothing = jnp.zeros((1, pack_ref.shape[1]), F32)
    halo = (nothing, nothing) if halo_ref is None else (halo_ref[0:1], halo_ref[1:2])
    parts, west, east = join_packs(size, radix, False, pack_ref, others, halo, packs)
    pack_out[...] = packs[0]
    for name in (LAST_RES, LAST_DIR, LAST_FACE):
        pack_out[name : name + 1] = packs[radix - 1, name : name + 1, :]
    pack_out[SUMS : SUMS + 1] = jnp.concatenate(parts, axis=1)
    halo_out[0:1] = west
    halo_out[1:2] = east


def finish_kernel(size, radix, cells_all, *refs):
    pack_ref, others, halo_ref = refs[0], refs[1:radix], refs[radix]
    residual_ref, faces_ref, answer_ref = refs[radix + 1 : radix + 4]
    residual_out, answer_out, norms_out, packs = refs[radix + 4 :]
    parts, west, east = join_packs(size, radix, True, pack_ref, others, (halo_ref[0:1], halo_ref[1:2]), packs)
    answer_out[...] = answer_ref[...]
    residual = residual_ref[...]
    lon = lax.broadcasted_iota(jnp.int32, residual.shape, 0)
    residual = jnp.where(lon == 0, residual + faces_ref[0:1] * west, residual)
    residual = jnp.where(lon == residual.shape[0] - 1, residual + faces_ref[1:2] * east, residual)
    residual_out[...] = residual
    for k in range(ITERS):
        norms_out[k] = jnp.sum(parts[k]) / cells_all


def vmem():
    return pl.BlockSpec(memory_space=pltpu.VMEM)


def shape(*dims):
    return jax.ShapeDtypeStruct(dims, F32)


def smem():
    return pl.BlockSpec(memory_space=pltpu.SMEM)


def call(body, in_specs, outs, scratch, limit, cost=None, out_specs=None):
    return pl.pallas_call(
        body,
        in_specs=in_specs,
        out_specs=out_specs or [vmem()] * len(outs),
        out_shape=outs,
        scratch_shapes=scratch,
        compiler_params=pltpu.CompilerParams(vmem_limit_bytes=limit),
        cost_estimate=cost,
    )


def exchange(inner, outer):
    devices = lax.axis_size("lon")
    pairs = [(i, i ^ 1) for i in range(devices)]
    across = [(i, (i + 1 if i % 2 else i - 1) % devices) for i in range(devices)]
    return lax.ppermute(inner, "lon", pairs), lax.ppermute(outer, "lon", across)


def swap_runs(pack, size, radix):
    devices = lax.axis_size("lon")
    return [
        lax.ppermute(pack, "lon", [(i, i ^ (s * size)) for i in range(devices)]) for s in range(radix - 1, 0, -1)
    ][::-1]


def on_device(
    right_side, east_coef, north_coef, surface_term, cell_mask, inverse_blocks, active_tiles, low_bound, high_bound
):
    columns, rows = right_side.shape
    tiles = inverse_blocks.shape[0]
    count = lane_blocks(rows)
    field = shape(columns, rows)
    row = shape(1, rows)
    two = shape(2, rows)
    bt_shape = shape(count, columns, LANES, LANES)
    (bt,) = call(
        transpose_kernel,
        [pl.BlockSpec(memory_space=pl.ANY)],
        [bt_shape],
        [pltpu.VMEM(inverse_blocks.shape, F32), pltpu.SemaphoreType.DMA((count,))],
        40 * MIB,
        pl.CostEstimate(flops=10**9, bytes_accessed=2 * inverse_blocks.size * 4, transcendentals=0),
    )(inverse_blocks)
    residual, search, diag, east_face, north_face, ocean, east_end, inner, outer = call(
        first_kernel,
        [vmem()] * 7,
        [field, field, field, field, field, field, row, two, two],
        [],
        24 * MIB,
    )(active_tiles.reshape(-1, LANES), right_side, east_coef, north_coef, surface_term, cell_mask, bt)
    low_bound, high_bound, inner = lax.optimization_barrier((low_bound, high_bound, inner))
    inner, outer = exchange(inner, outer)
    residual, direction, answer, diag, faces, norms, coef, inner, outer = call(
        second_kernel,
        [smem()] * 2 + [vmem()] * 10,
        [field, field, field, field, two, row, shape(SUBS, LANES), row, row],
        [pltpu.VMEM((columns, rows), F32)],
        24 * MIB,
    )(low_bound, high_bound, inner, outer, residual, search, diag, east_face, north_face, ocean, east_end, bt)
    for k in range(2, ITERS - 1):
        inner, outer = exchange(inner, outer)
        residual, direction, answer, norms, inner, outer = call(
            functools.partial(middle_kernel, k),
            [vmem()] * 13,
            [field, field, field, row, row, row],
            [pltpu.VMEM((columns, rows), F32)],
            24 * MIB,
        )(inner, outer, residual, direction, answer, diag, east_face, north_face, ocean, faces, coef, norms, bt)
    inner, outer = exchange(inner, outer)
    pack_shape = shape(PACK_ROWS, rows)
    residual, answer, pack = call(
        closing_kernel,
        [vmem()] * 13,
        [field, field, pack_shape],
        [pltpu.VMEM((columns, rows), F32)],
        24 * MIB,
    )(inner, outer, residual, direction, answer, diag, east_face, north_face, ocean, faces, coef, norms, bt)
    devices = lax.axis_size("lon")
    size, halo = 1, []
    while True:
        radix = 4 if (devices // size) % 4 == 0 else 2
        others = swap_runs(pack, size, radix)
        packs = [pltpu.VMEM((radix, PACK_ROWS, rows), F32)]
        if size * radix == devices:
            break
        pack, *halo = call(
            functools.partial(stage_kernel, size, radix),
            [vmem()] * (radix + len(halo)),
            [pack_shape, two],
            packs,
            24 * MIB,
        )(pack, *others, *halo)
        size *= radix
    residual, answer, norms = call(
        functools.partial(finish_kernel, size, radix, float(columns * devices * rows)),
        [vmem()] * (radix + 4),
        [field, field, shape(ITERS)],
        packs,
        24 * MIB,
        out_specs=[vmem(), vmem(), smem()],
    )(pack, *others, *halo, residual, faces, answer)
    return answer, residual, norms


def solution(mesh):
    in_specs = (
        P(("member", "lon"), None),
        P("lon", None),
        P("lon", None),
        P("lon", None),
        P("lon", None),
        P("lon", None, None),
        P(),
        P(),
        P(),
    )
    out_specs = (P(("member", "lon"), None), P(("member", "lon"), None), P("member"))
    return jax.shard_map(on_device, mesh=mesh, in_specs=in_specs, out_specs=out_specs, check_vma=False)
```

```python
import functools

import jax
import jax.numpy as jnp
from jax import lax
from jax.experimental import pallas as pl
from jax.experimental.pallas import tpu as pltpu
from jax.sharding import PartitionSpec as P

ITERS = 4
LANES = 128
SUBS = 8
F32 = jnp.float32
MIB = 2**20


def lane_blocks(rows):
    return rows // LANES


def roll(x, shift, axis):
    return pltpu.roll(x, shift % x.shape[axis], axis)


def repeat_row(row, times):
    return jnp.concatenate([row] * times, axis=1)


def gather_index():
    lane = lax.broadcasted_iota(jnp.int32, (SUBS, LANES), 1)
    sub = lax.broadcasted_iota(jnp.int32, (SUBS, LANES), 0)
    return (lane // SUBS) * SUBS + sub


def expand(field, block, index):
    part = field[:, block * LANES : (block + 1) * LANES]
    rows = [
        jnp.take_along_axis(jnp.broadcast_to(part[a : a + 1], (SUBS, LANES)), index, axis=1)
        for a in range(part.shape[0])
    ]
    return jnp.concatenate(rows, axis=0)


def blocks_product(bt_ref, field, out_ref):
    index = gather_index()
    columns, rows = field.shape
    for block in range(lane_blocks(rows)):
        spread = expand(field, block, index)
        for a in range(columns):
            out_ref[a : a + 1, block * LANES : (block + 1) * LANES] = jnp.sum(
                bt_ref[block, a] * spread, axis=0, keepdims=True
            )


def even_device():
    return lax.rem(lax.axis_index("lon"), 2) == 0


def store_edges(inner_ref, outer_ref, row, even, first, last):
    inner_ref[row : row + 1] = jnp.where(even, last, first)
    outer_ref[row : row + 1] = jnp.where(even, first, last)


def halo_rows(inner_ref, outer_ref, row, even):
    inner, outer = inner_ref[row : row + 1], outer_ref[row : row + 1]
    return jnp.where(even, outer, inner), jnp.where(even, inner, outer)


def low_device():
    return lax.rem(lax.axis_index("lon"), 4) < 2


def lane_partial(squares):
    total = jnp.sum(squares, axis=0, keepdims=True)
    parts = [total[:, i * LANES : (i + 1) * LANES] for i in range(total.shape[1] // LANES)]
    return functools.reduce(jnp.add, parts)


def tile_flags(active_ref, first, tiles):
    active = active_ref[...]
    before = jnp.sum((active < first).astype(jnp.int32))
    row = jnp.minimum(before // LANES, active_ref.shape[0] - 2)
    lane = lax.broadcasted_iota(jnp.int32, (LANES, tiles), 1) + first
    found = jnp.zeros((LANES, tiles), jnp.int32)
    for step in range(2):
        entries = jnp.broadcast_to(active_ref[pl.ds(row + step, 1), :], (LANES, LANES))
        found = found + (entries.T == lane).astype(jnp.int32)
    return (jnp.sum(found, axis=0, keepdims=True) > 0).astype(F32)


def transpose_kernel(blocks_hbm, bt_ref, raw, sems):
    count, columns = bt_ref.shape[:2]
    step = blocks_hbm.shape[0] // count

    def fetch(i):
        part = pl.ds(i * step, step)
        return pltpu.make_async_copy(blocks_hbm.at[part], raw.at[part], sems.at[i])

    for i in range(count):
        fetch(i).start()
    for i in range(count):
        fetch(i).wait()
        for a in range(columns):
            bt_ref[i, a] = raw[i * step : (i + 1) * step, a * SUBS : (a + 1) * SUBS, :].reshape(LANES, LANES).T


PAIR_SEARCH, PAIR_FLOW, PAIR_FACE, PAIR_BACK_SEARCH, PAIR_BACK_FACE, PAIR_OWN, PAIR_OPPOSITE, PAIR_ROWS = 0, 1, 2, 3, 4, 8, 16, 24


def edge_products(bt_ref, field):
    columns, rows = field.shape
    index = gather_index()
    first, last = [], []
    for block in range(lane_blocks(rows)):
        spread = expand(field, block, index)
        first.append(jnp.sum(bt_ref[block, 0] * spread, axis=0, keepdims=True))
        last.append(jnp.sum(bt_ref[block, columns - 1] * spread, axis=0, keepdims=True))
    return jnp.concatenate(first, axis=1), jnp.concatenate(last, axis=1)


def first_kernel(
    active_ref, right_ref, east_ref, north_ref, surface_ref, mask_ref, bt_ref,
    residual_ref, search_ref, diag_ref, east_face_ref, north_face_ref, ocean_ref, east_end_ref, inner_ref, outer_ref, near_ref, far_ref,
):
    columns, rows = right_ref.shape
    count = lane_blocks(rows)
    tiles = rows // SUBS
    even = even_device()
    flags = tile_flags(active_ref, lax.axis_index("lon") * tiles, tiles)
    lane = lax.broadcasted_iota(jnp.int32, (SUBS, LANES), 1)
    spread = [
        jnp.take_along_axis(jnp.broadcast_to(flags, (SUBS, tiles)), i * (LANES // SUBS) + lane // SUBS, axis=1)
        for i in range(count)
    ]
    flag_lat = jnp.concatenate(spread, axis=1)[0:1]
    ocean = mask_ref[...].astype(F32) * flag_lat
    ocean_ref[...] = ocean
    lat = lax.broadcasted_iota(jnp.int32, (columns, rows), 1)
    lon = lax.broadcasted_iota(jnp.int32, (columns, rows), 0)
    east_ocean = east_ref[...] * ocean
    east_face = jnp.where(lon < columns - 1, east_ocean * roll(ocean, -1, 0), 0.0)
    north_face = jnp.where(lat < rows - 1, north_ref[...] * ocean * roll(ocean, -1, 1), 0.0)
    east_face_ref[...] = east_face
    north_face_ref[...] = north_face
    diag = surface_ref[...] * ocean + east_face + roll(east_face, 1, 0) + north_face + roll(north_face, 1, 1)
    diag_ref[...] = diag
    residual = right_ref[...] * ocean
    residual_ref[...] = residual
    east_end = east_ocean[columns - 1 :]
    east_end_ref[...] = east_end
    blocks_product(bt_ref, residual, search_ref)
    search = search_ref[...] * ocean
    search_ref[...] = search
    nothing = jnp.zeros_like(east_end)
    flow = apply_operator(jnp.zeros_like(search), -search, diag, east_face, north_face, nothing, nothing)
    edges = edge_products(bt_ref, flow)
    fields = (
        (PAIR_SEARCH, search[0:1], search[columns - 1 :]),
        (PAIR_FLOW, edges[0] * ocean[0:1], edges[1] * ocean[columns - 1 :]),
        (PAIR_FACE, ocean[0:1], east_end),
        (PAIR_BACK_SEARCH, search[columns - 1 :], search[0:1]),
        (PAIR_BACK_FACE, east_end, ocean[0:1]),
    )
    for row, west, east in fields:
        store_edges(inner_ref, outer_ref, row, even, west, east)
    for ref, edge in ((inner_ref, jnp.where(even, columns - 1, 0)), (outer_ref, jnp.where(even, 0, columns - 1))):
        ref[len(fields) : SUBS] = jnp.zeros((SUBS - len(fields), rows), F32)
        for i in range(count):
            lanes = slice(i * LANES, (i + 1) * LANES)
            ref[PAIR_OWN : PAIR_OWN + SUBS, lanes] = bt_ref[i, edge, pl.ds(pl.multiple_of(edge * SUBS, SUBS), SUBS), :]
            back = columns - 1 - edge
            ref[PAIR_OPPOSITE : PAIR_OPPOSITE + SUBS, lanes] = bt_ref[i, edge, pl.ds(pl.multiple_of(back * SUBS, SUBS), SUBS), :]
    low = low_device()
    for row, west, east in ((0, search[0:1], search[columns - 1 :]), (1, ocean[0:1], east_end)):
        near_ref[row : row + 1] = jnp.where(low, east, west)
        far_ref[row : row + 1] = jnp.where(low, west, east)


def apply_operator(residual, direction, diag, east_face, north_face, west_term, east_term):
    flow = diag * direction
    flow = flow - east_face * roll(direction, -1, 0) - roll(east_face, 1, 0) * roll(direction, 1, 0)
    flow = flow - north_face * roll(direction, -1, 1) - roll(north_face, 1, 1) * roll(direction, 1, 1)
    lon = lax.broadcasted_iota(jnp.int32, residual.shape, 0)
    flow = jnp.where(lon == 0, flow - west_term, flow)
    flow = jnp.where(lon == residual.shape[0] - 1, flow - east_term, flow)
    return residual - flow


def search_step(bt_ref, residual, direction, ocean, coef_ref, k, search_ref):
    count = lane_blocks(residual.shape[1])
    blocks_product(bt_ref, residual, search_ref)
    keep = repeat_row(coef_ref[2 * k : 2 * k + 1], count)
    gain = repeat_row(coef_ref[2 * k + 1 : 2 * k + 2], count)
    return keep * direction + gain * (ocean * search_ref[...])


def store_coefficients(low_ref, high_ref, coef_ref):
    low = jnp.full((1, LANES), low_ref[0], F32)
    high = jnp.full((1, LANES), high_ref[0], F32)
    center = (high + low) / 2.0
    radius = (high - low) / 2.0
    ratio = center / radius
    weight_prev = 1.0 / ratio
    coef_ref[0:1] = 1.0 / center
    for k in range(1, ITERS):
        weight = 1.0 / (2.0 * ratio - weight_prev)
        coef_ref[2 * k : 2 * k + 1] = weight * weight_prev
        coef_ref[2 * k + 1 : 2 * k + 2] = 2.0 * weight / radius
        weight_prev = weight


def neighbour_direction(own, opposite, search, flow, own_push, opposite_push, coef_ref):
    rows = search.shape[1]
    count = lane_blocks(rows)
    index = gather_index()
    parts = []
    for block in range(count):
        lanes = slice(block * LANES, (block + 1) * LANES)
        product = own[:, lanes] * expand(own_push, block, index) + opposite[:, lanes] * expand(opposite_push, block, index)
        parts.append(jnp.sum(product, axis=0, keepdims=True))
    scale, keep, gain = (repeat_row(coef_ref[n : n + 1], count) for n in (0, 2, 3))
    return keep * (scale * search) + gain * (search - scale * flow + jnp.concatenate(parts, axis=1))


def second_kernel(
    low_ref, high_ref, inner_ref, outer_ref, near_ref, far_ref, residual_ref, search_in, diag_ref, east_face_ref, north_face_ref, ocean_ref, east_end_ref, bt_ref,
    residual_out, direction_out, solution_out, diag_out, faces_out, norms_out, coef_out, inner_out, outer_out,
    search_ref,
):
    store_coefficients(low_ref, high_ref, coef_out)
    ocean = ocean_ref[...]
    columns, rows = ocean.shape
    scale = repeat_row(coef_out[0:1], lane_blocks(rows))
    search = search_in[...]
    even, low = even_device(), low_device()
    sides = [halo_rows(inner_ref, outer_ref, row, even) for row in range(PAIR_BACK_FACE + 1)]
    beyond = [
        (jnp.where(low, far, near), jnp.where(low, near, far))
        for near, far in ((near_ref[row : row + 1], far_ref[row : row + 1]) for row in range(2))
    ]
    here = (search[0:1], search[columns - 1 :])
    static = (ocean[0:1], east_end_ref[...])
    faces, halos, later_halos = [], [], []
    for side in range(2):
        there, flow, face, back, back_face = (pair[side] for pair in sides)
        face = static[side] * face
        own_push = face * (scale * (here[side] - there))
        opposite_push = back_face * beyond[1][side] * (scale * (beyond[0][side] - back))
        from_inner = even if side == 1 else jnp.logical_not(even)
        own, opposite = (
            jnp.where(from_inner, inner_ref[row : row + SUBS], outer_ref[row : row + SUBS]) for row in (PAIR_OWN, PAIR_OPPOSITE)
        )
        faces.append(face)
        halos.append(face * (scale * there))
        later_halos.append(face * neighbour_direction(own, opposite, there, flow, own_push, opposite_push, coef_out))
    faces_out[0:1] = faces[0]
    faces_out[1:2] = faces[1]
    lon = lax.broadcasted_iota(jnp.int32, ocean.shape, 0)
    diag = diag_ref[...]
    diag = jnp.where(lon == 0, diag + faces[0], diag)
    diag = jnp.where(lon == columns - 1, diag + faces[1], diag)
    diag_out[...] = diag
    east_face, north_face = east_face_ref[...], north_face_ref[...]
    direction = search * scale
    residual = apply_operator(residual_ref[...], direction, diag, east_face, north_face, halos[0], halos[1])
    norms_out[...] = jnp.zeros_like(norms_out)
    norms_out[0:1, 0:LANES] = lane_partial(residual * residual)
    later = search_step(bt_ref, residual, direction, ocean, coef_out, 1, search_ref)
    answer = direction + later
    residual = apply_operator(residual, later, diag, east_face, north_face, later_halos[0], later_halos[1])
    norms_out[0:1, LANES : 2 * LANES] = lane_partial(residual * residual)
    residual_out[...] = residual
    later = search_step(bt_ref, residual, later, ocean, coef_out, 2, search_ref)
    direction_out[...] = later
    store_edges(inner_out, outer_out, 0, even, later[0:1], later[columns - 1 :])
    solution_out[...] = answer + later


def advance(k, west, east, residual_ref, direction_ref, solution_ref, diag_ref, east_face_ref, north_face_ref, ocean_ref, faces_ref, coef_ref, bt_ref, search_ref):
    direction = direction_ref[...]
    residual = apply_operator(
        residual_ref[...], direction, diag_ref[...], east_face_ref[...], north_face_ref[...],
        faces_ref[0:1] * west, faces_ref[1:2] * east,
    )
    later = search_step(bt_ref, residual, direction, ocean_ref[...], coef_ref, k, search_ref)
    return residual, later, solution_ref[...] + later


def store_norm(norms_out, norms_ref, k, squares):
    norms_out[...] = norms_ref[...]
    norms_out[0:1, k * LANES : (k + 1) * LANES] = lane_partial(squares)


def middle_kernel(
    k,
    inner_ref, outer_ref, residual_ref, direction_ref, solution_ref, diag_ref, east_face_ref, north_face_ref, ocean_ref, faces_ref, coef_ref, norms_ref, bt_ref,
    residual_out, direction_out, solution_out, norms_out, inner_out, outer_out,
    search_ref,
):
    even = even_device()
    west, east = halo_rows(inner_ref, outer_ref, 0, even)
    residual, later, answer = advance(
        k, west, east, residual_ref, direction_ref, solution_ref, diag_ref, east_face_ref, north_face_ref, ocean_ref, faces_ref, coef_ref, bt_ref, search_ref
    )
    residual_out[...] = residual
    store_norm(norms_out, norms_ref, k - 1, residual * residual)
    direction_out[...] = later
    store_edges(inner_out, outer_out, 0, even, later[0:1], later[-1:])
    solution_out[...] = answer


FIRST_RES, FIRST_DIR, LAST_RES, LAST_DIR, LAST_FACE, SUMS, PACK_ROWS = 0, 1, 2, 3, 4, 5, 8


def closing_kernel(
    inner_ref, outer_ref, residual_ref, direction_ref, solution_ref, diag_ref, east_face_ref, north_face_ref, ocean_ref, faces_ref, coef_ref, norms_ref, bt_ref,
    residual_out, solution_out, pack_out,
    search_ref,
):
    west, east = halo_rows(inner_ref, outer_ref, 0, even_device())
    residual, later, answer = advance(
        ITERS - 1, west, east, residual_ref, direction_ref, solution_ref, diag_ref, east_face_ref, north_face_ref, ocean_ref, faces_ref, coef_ref, bt_ref, search_ref
    )
    solution_out[...] = answer
    columns = residual.shape[0]
    sums = pack_out.at[SUMS : SUMS + 1]
    store_norm(sums, norms_ref, ITERS - 2, residual * residual)
    nothing = jnp.zeros_like(west)
    residual = apply_operator(residual, later, diag_ref[...], east_face_ref[...], north_face_ref[...], nothing, nothing)
    residual_out[...] = residual
    lon = lax.broadcasted_iota(jnp.int32, residual.shape, 0)
    inside = jnp.where((lon > 0) & (lon < columns - 1), residual, 0.0)
    sums[0:1, (ITERS - 1) * LANES : ITERS * LANES] = lane_partial(inside * inside)
    pack_out[FIRST_RES : FIRST_RES + 1] = residual[0:1]
    pack_out[FIRST_DIR : FIRST_DIR + 1] = later[0:1]
    pack_out[LAST_RES : LAST_RES + 1] = residual[columns - 1 :]
    pack_out[LAST_DIR : LAST_DIR + 1] = later[columns - 1 :]
    pack_out[LAST_FACE : LAST_FACE + 1] = faces_ref[1:2]
    pack_out[SUMS + 1 :] = jnp.zeros_like(pack_out[SUMS + 1 :])


def join_packs(size, radix, is_last, pack_ref, others, halo, packs):
    me = lax.axis_index("lon")
    mine = lax.rem(me // size, radix)
    packs[mine] = pack_ref[...]
    for s, other in enumerate(others, start=1):
        packs[mine ^ s] = other[...]

    def row(run, name):
        return packs[run % radix, name : name + 1, :]

    sums = functools.reduce(jnp.add, [row(run, SUMS) for run in range(radix)])
    total = None
    for run in range(radix if is_last else radix - 1):
        face = row(run, LAST_FACE)
        left = row(run, LAST_RES) + face * row(run + 1, FIRST_DIR)
        right = row(run + 1, FIRST_RES) + face * row(run, LAST_DIR)
        squares = lane_partial(left * left + right * right)
        total = squares if total is None else total + squares
    parts = [sums[:, i * LANES : (i + 1) * LANES] for i in range(sums.shape[1] // LANES)]
    parts[ITERS - 1] = parts[ITERS - 1] + total
    before = packs[lax.rem(mine + radix - 1, radix)][LAST_DIR : LAST_DIR + 1]
    after = packs[lax.rem(mine + 1, radix)][FIRST_DIR : FIRST_DIR + 1]
    place = lax.rem(me, size)
    west_now = place == 0
    east_now = place == size - 1
    if not is_last:
        west_now = west_now & (mine > 0)
        east_now = east_now & (mine < radix - 1)
    west, east = halo
    return parts, jnp.where(west_now, before, west), jnp.where(east_now, after, east)


def stage_kernel(size, radix, *refs):
    pack_ref, others, halo_ref = refs[0], refs[1:radix], refs[radix] if size > 1 else None
    pack_out, halo_out, packs = refs[-3:]
    nothing = jnp.zeros((1, pack_ref.shape[1]), F32)
    halo = (nothing, nothing) if halo_ref is None else (halo_ref[0:1], halo_ref[1:2])
    parts, west, east = join_packs(size, radix, False, pack_ref, others, halo, packs)
    pack_out[...] = packs[0]
    for name in (LAST_RES, LAST_DIR, LAST_FACE):
        pack_out[name : name + 1] = packs[radix - 1, name : name + 1, :]
    pack_out[SUMS : SUMS + 1] = jnp.concatenate(parts, axis=1)
    halo_out[0:1] = west
    halo_out[1:2] = east


def finish_kernel(size, radix, cells_all, *refs):
    pack_ref, others, halo_ref = refs[0], refs[1:radix], refs[radix]
    residual_ref, faces_ref, answer_ref = refs[radix + 1 : radix + 4]
    residual_out, answer_out, norms_out, packs = refs[radix + 4 :]
    parts, west, east = join_packs(size, radix, True, pack_ref, others, (halo_ref[0:1], halo_ref[1:2]), packs)
    answer_out[...] = answer_ref[...]
    residual = residual_ref[...]
    lon = lax.broadcasted_iota(jnp.int32, residual.shape, 0)
    residual = jnp.where(lon == 0, residual + faces_ref[0:1] * west, residual)
    residual = jnp.where(lon == residual.shape[0] - 1, residual + faces_ref[1:2] * east, residual)
    residual_out[...] = residual
    for k in range(ITERS):
        norms_out[k] = jnp.sum(parts[k]) / cells_all


def vmem():
    return pl.BlockSpec(memory_space=pltpu.VMEM)


def shape(*dims):
    return jax.ShapeDtypeStruct(dims, F32)


def smem():
    return pl.BlockSpec(memory_space=pltpu.SMEM)


def call(body, in_specs, outs, scratch, limit, cost=None, out_specs=None):
    return pl.pallas_call(
        body,
        in_specs=in_specs,
        out_specs=out_specs or [vmem()] * len(outs),
        out_shape=outs,
        scratch_shapes=scratch,
        compiler_params=pltpu.CompilerParams(vmem_limit_bytes=limit),
        cost_estimate=cost,
    )


def exchange(inner, outer):
    devices = lax.axis_size("lon")
    pairs = [(i, i ^ 1) for i in range(devices)]
    across = [(i, (i + 1 if i % 2 else i - 1) % devices) for i in range(devices)]
    return lax.ppermute(inner, "lon", pairs), lax.ppermute(outer, "lon", across)


def exchange_beyond(near, far):
    devices = lax.axis_size("lon")
    within = [(i, i ^ 2) for i in range(devices)]
    across = [(i, (i + 2 if i % 4 >= 2 else i - 2) % devices) for i in range(devices)]
    return lax.ppermute(near, "lon", within), lax.ppermute(far, "lon", across)


def swap_runs(pack, size, radix):
    devices = lax.axis_size("lon")
    return [
        lax.ppermute(pack, "lon", [(i, i ^ (s * size)) for i in range(devices)]) for s in range(radix - 1, 0, -1)
    ][::-1]


def on_device(
    right_side, east_coef, north_coef, surface_term, cell_mask, inverse_blocks, active_tiles, low_bound, high_bound
):
    columns, rows = right_side.shape
    tiles = inverse_blocks.shape[0]
    count = lane_blocks(rows)
    field = shape(columns, rows)
    row = shape(1, rows)
    two = shape(2, rows)
    bt_shape = shape(count, columns, LANES, LANES)
    (bt,) = call(
        transpose_kernel,
        [pl.BlockSpec(memory_space=pl.ANY)],
        [bt_shape],
        [pltpu.VMEM(inverse_blocks.shape, F32), pltpu.SemaphoreType.DMA((count,))],
        40 * MIB,
        pl.CostEstimate(flops=10**9, bytes_accessed=2 * inverse_blocks.size * 4, transcendentals=0),
    )(inverse_blocks)
    pair_shape = shape(PAIR_ROWS, rows)
    residual, search, diag, east_face, north_face, ocean, east_end, inner, outer, near, far = call(
        first_kernel,
        [vmem()] * 7,
        [field, field, field, field, field, field, row, pair_shape, pair_shape, two, two],
        [],
        24 * MIB,
    )(active_tiles.reshape(-1, LANES), right_side, east_coef, north_coef, surface_term, cell_mask, bt)
    low_bound, high_bound, inner = lax.optimization_barrier((low_bound, high_bound, inner))
    inner, outer = exchange(inner, outer)
    near, far = exchange_beyond(near, far)
    residual, direction, answer, diag, faces, norms, coef, inner, outer = call(
        second_kernel,
        [smem()] * 2 + [vmem()] * 12,
        [field, field, field, field, two, row, shape(SUBS, LANES), row, row],
        [pltpu.VMEM((columns, rows), F32)],
        24 * MIB,
    )(low_bound, high_bound, inner, outer, near, far, residual, search, diag, east_face, north_face, ocean, east_end, bt)
    for k in range(3, ITERS - 1):
        inner, outer = exchange(inner, outer)
        residual, direction, answer, norms, inner, outer = call(
            functools.partial(middle_kernel, k),
            [vmem()] * 13,
            [field, field, field, row, row, row],
            [pltpu.VMEM((columns, rows), F32)],
            24 * MIB,
        )(inner, outer, residual, direction, answer, diag, east_face, north_face, ocean, faces, coef, norms, bt)
    inner, outer = exchange(inner, outer)
    pack_shape = shape(PACK_ROWS, rows)
    residual, answer, pack = call(
        closing_kernel,
        [vmem()] * 13,
        [field, field, pack_shape],
        [pltpu.VMEM((columns, rows), F32)],
        24 * MIB,
    )(inner, outer, residual, direction, answer, diag, east_face, north_face, ocean, faces, coef, norms, bt)
    devices = lax.axis_size("lon")
    size, halo = 1, []
    while True:
        radix = 4 if (devices // size) % 4 == 0 else 2
        others = swap_runs(pack, size, radix)
        packs = [pltpu.VMEM((radix, PACK_ROWS, rows), F32)]
        if size * radix == devices:
            break
        pack, *halo = call(
            functools.partial(stage_kernel, size, radix),
            [vmem()] * (radix + len(halo)),
            [pack_shape, two],
            packs,
            24 * MIB,
        )(pack, *others, *halo)
        size *= radix
    residual, answer, norms = call(
        functools.partial(finish_kernel, size, radix, float(columns * devices * rows)),
        [vmem()] * (radix + 4),
        [field, field, shape(ITERS)],
        packs,
        24 * MIB,
        out_specs=[vmem(), vmem(), smem()],
    )(pack, *others, *halo, residual, faces, answer)
    return answer, residual, norms


def solution(mesh):
    in_specs = (
        P(("member", "lon"), None),
        P("lon", None),
        P("lon", None),
        P("lon", None),
        P("lon", None),
        P("lon", None, None),
        P(),
        P(),
        P(),
    )
    out_specs = (P(("member", "lon"), None), P(("member", "lon"), None), P("member"))
    return jax.shard_map(on_device, mesh=mesh, in_specs=in_specs, out_specs=out_specs, check_vma=False)
```

```python
import functools

import jax
import jax.numpy as jnp
from jax import lax
from jax.experimental import pallas as pl
from jax.experimental.pallas import tpu as pltpu
from jax.sharding import PartitionSpec as P

ITERS = 4
LANES = 128
SUBS = 8
F32 = jnp.float32
MIB = 2**20


def lane_blocks(rows):
    return rows // LANES


def roll(x, shift, axis):
    return pltpu.roll(x, shift % x.shape[axis], axis)


def repeat_row(row, times):
    return jnp.concatenate([row] * times, axis=1)


def gather_index():
    lane = lax.broadcasted_iota(jnp.int32, (SUBS, LANES), 1)
    sub = lax.broadcasted_iota(jnp.int32, (SUBS, LANES), 0)
    return (lane // SUBS) * SUBS + sub


def expand(field, block, index):
    part = field[:, block * LANES : (block + 1) * LANES]
    rows = [
        jnp.take_along_axis(jnp.broadcast_to(part[a : a + 1], (SUBS, LANES)), index, axis=1)
        for a in range(part.shape[0])
    ]
    return jnp.concatenate(rows, axis=0)


def blocks_product(bt_ref, field, out_ref):
    index = gather_index()
    columns, rows = field.shape
    for block in range(lane_blocks(rows)):
        spread = expand(field, block, index)
        for a in range(columns):
            out_ref[a : a + 1, block * LANES : (block + 1) * LANES] = jnp.sum(
                bt_ref[block, a] * spread, axis=0, keepdims=True
            )


def even_device():
    return lax.rem(lax.axis_index("lon"), 2) == 0


def store_edges(inner_ref, outer_ref, row, even, first, last):
    inner_ref[row : row + 1] = jnp.where(even, last, first)
    outer_ref[row : row + 1] = jnp.where(even, first, last)


def halo_rows(inner_ref, outer_ref, row, even):
    inner, outer = inner_ref[row : row + 1], outer_ref[row : row + 1]
    return jnp.where(even, outer, inner), jnp.where(even, inner, outer)


def low_device():
    return lax.rem(lax.axis_index("lon"), 4) < 2


def lane_partial(squares):
    total = jnp.sum(squares, axis=0, keepdims=True)
    parts = [total[:, i * LANES : (i + 1) * LANES] for i in range(total.shape[1] // LANES)]
    return functools.reduce(jnp.add, parts)


def tile_flags(active_ref, first, tiles):
    active = active_ref[...]
    before = jnp.sum((active < first).astype(jnp.int32))
    row = jnp.minimum(before // LANES, active_ref.shape[0] - 2)
    lane = lax.broadcasted_iota(jnp.int32, (LANES, tiles), 1) + first
    found = jnp.zeros((LANES, tiles), jnp.int32)
    for step in range(2):
        entries = jnp.broadcast_to(active_ref[pl.ds(row + step, 1), :], (LANES, LANES))
        found = found + (entries.T == lane).astype(jnp.int32)
    return (jnp.sum(found, axis=0, keepdims=True) > 0).astype(F32)


def transpose_kernel(blocks_hbm, bt_ref, raw, sems):
    count, columns = bt_ref.shape[:2]
    step = blocks_hbm.shape[0] // count

    def fetch(i):
        part = pl.ds(i * step, step)
        return pltpu.make_async_copy(blocks_hbm.at[part], raw.at[part], sems.at[i])

    for i in range(count):
        fetch(i).start()
    for i in range(count):
        fetch(i).wait()
        for a in range(columns):
            bt_ref[i, a] = raw[i * step : (i + 1) * step, a * SUBS : (a + 1) * SUBS, :].reshape(LANES, LANES).T


PAIR_SEARCH, PAIR_FLOW, PAIR_FACE, PAIR_BACK_SEARCH, PAIR_BACK_FACE, PAIR_OWN, PAIR_OPPOSITE, PAIR_ROWS = 0, 1, 2, 3, 4, 8, 16, 24


def edge_products(bt_ref, field):
    columns, rows = field.shape
    index = gather_index()
    first, last = [], []
    for block in range(lane_blocks(rows)):
        spread = expand(field, block, index)
        first.append(jnp.sum(bt_ref[block, 0] * spread, axis=0, keepdims=True))
        last.append(jnp.sum(bt_ref[block, columns - 1] * spread, axis=0, keepdims=True))
    return jnp.concatenate(first, axis=1), jnp.concatenate(last, axis=1)


def first_kernel(
    active_ref, right_ref, east_ref, north_ref, surface_ref, mask_ref, bt_ref,
    residual_ref, search_ref, diag_ref, east_face_ref, north_face_ref, ocean_ref, east_end_ref, flow_ref, inner_ref, outer_ref, near_ref, far_ref,
):
    columns, rows = right_ref.shape
    count = lane_blocks(rows)
    tiles = rows // SUBS
    even = even_device()
    flags = tile_flags(active_ref, lax.axis_index("lon") * tiles, tiles)
    lane = lax.broadcasted_iota(jnp.int32, (SUBS, LANES), 1)
    spread = [
        jnp.take_along_axis(jnp.broadcast_to(flags, (SUBS, tiles)), i * (LANES // SUBS) + lane // SUBS, axis=1)
        for i in range(count)
    ]
    flag_lat = jnp.concatenate(spread, axis=1)[0:1]
    ocean = mask_ref[...].astype(F32) * flag_lat
    ocean_ref[...] = ocean
    lat = lax.broadcasted_iota(jnp.int32, (columns, rows), 1)
    lon = lax.broadcasted_iota(jnp.int32, (columns, rows), 0)
    east_ocean = east_ref[...] * ocean
    east_face = jnp.where(lon < columns - 1, east_ocean * roll(ocean, -1, 0), 0.0)
    north_face = jnp.where(lat < rows - 1, north_ref[...] * ocean * roll(ocean, -1, 1), 0.0)
    east_face_ref[...] = east_face
    north_face_ref[...] = north_face
    diag = surface_ref[...] * ocean + east_face + roll(east_face, 1, 0) + north_face + roll(north_face, 1, 1)
    diag_ref[...] = diag
    residual = right_ref[...] * ocean
    residual_ref[...] = residual
    east_end = east_ocean[columns - 1 :]
    east_end_ref[...] = east_end
    blocks_product(bt_ref, residual, search_ref)
    search = search_ref[...] * ocean
    search_ref[...] = search
    nothing = jnp.zeros_like(east_end)
    flow = apply_operator(jnp.zeros_like(search), -search, diag, east_face, north_face, nothing, nothing)
    flow_ref[...] = flow
    edges = edge_products(bt_ref, flow)
    fields = (
        (PAIR_SEARCH, search[0:1], search[columns - 1 :]),
        (PAIR_FLOW, edges[0] * ocean[0:1], edges[1] * ocean[columns - 1 :]),
        (PAIR_FACE, ocean[0:1], east_end),
        (PAIR_BACK_SEARCH, search[columns - 1 :], search[0:1]),
        (PAIR_BACK_FACE, east_end, ocean[0:1]),
    )
    for row, west, east in fields:
        store_edges(inner_ref, outer_ref, row, even, west, east)
    for ref, edge in ((inner_ref, jnp.where(even, columns - 1, 0)), (outer_ref, jnp.where(even, 0, columns - 1))):
        ref[len(fields) : SUBS] = jnp.zeros((SUBS - len(fields), rows), F32)
        for i in range(count):
            lanes = slice(i * LANES, (i + 1) * LANES)
            ref[PAIR_OWN : PAIR_OWN + SUBS, lanes] = bt_ref[i, edge, pl.ds(pl.multiple_of(edge * SUBS, SUBS), SUBS), :]
            back = columns - 1 - edge
            ref[PAIR_OPPOSITE : PAIR_OPPOSITE + SUBS, lanes] = bt_ref[i, edge, pl.ds(pl.multiple_of(back * SUBS, SUBS), SUBS), :]
    low = low_device()
    for row, west, east in ((0, search[0:1], search[columns - 1 :]), (1, ocean[0:1], east_end)):
        near_ref[row : row + 1] = jnp.where(low, east, west)
        far_ref[row : row + 1] = jnp.where(low, west, east)


def apply_operator(residual, direction, diag, east_face, north_face, west_term, east_term):
    flow = diag * direction
    flow = flow - east_face * roll(direction, -1, 0) - roll(east_face, 1, 0) * roll(direction, 1, 0)
    flow = flow - north_face * roll(direction, -1, 1) - roll(north_face, 1, 1) * roll(direction, 1, 1)
    lon = lax.broadcasted_iota(jnp.int32, residual.shape, 0)
    flow = jnp.where(lon == 0, flow - west_term, flow)
    flow = jnp.where(lon == residual.shape[0] - 1, flow - east_term, flow)
    return residual - flow


def search_step(bt_ref, residual, direction, ocean, coef_ref, k, search_ref):
    count = lane_blocks(residual.shape[1])
    blocks_product(bt_ref, residual, search_ref)
    keep = repeat_row(coef_ref[2 * k : 2 * k + 1], count)
    gain = repeat_row(coef_ref[2 * k + 1 : 2 * k + 2], count)
    return keep * direction + gain * (ocean * search_ref[...])


def store_coefficients(low_ref, high_ref, coef_ref):
    low = jnp.full((1, LANES), low_ref[0], F32)
    high = jnp.full((1, LANES), high_ref[0], F32)
    center = (high + low) / 2.0
    radius = (high - low) / 2.0
    ratio = center / radius
    weight_prev = 1.0 / ratio
    coef_ref[0:1] = 1.0 / center
    for k in range(1, ITERS):
        weight = 1.0 / (2.0 * ratio - weight_prev)
        coef_ref[2 * k : 2 * k + 1] = weight * weight_prev
        coef_ref[2 * k + 1 : 2 * k + 2] = 2.0 * weight / radius
        weight_prev = weight


def neighbour_direction(own, opposite, search, flow, own_push, opposite_push, coef_ref):
    rows = search.shape[1]
    count = lane_blocks(rows)
    index = gather_index()
    parts = []
    for block in range(count):
        lanes = slice(block * LANES, (block + 1) * LANES)
        product = own[:, lanes] * expand(own_push, block, index) + opposite[:, lanes] * expand(opposite_push, block, index)
        parts.append(jnp.sum(product, axis=0, keepdims=True))
    scale, keep, gain = (repeat_row(coef_ref[n : n + 1], count) for n in (0, 2, 3))
    return keep * (scale * search) + gain * (search - scale * flow + jnp.concatenate(parts, axis=1))


def side_products(bt_ref, first, last):
    count, columns = bt_ref.shape[:2]
    index = gather_index()
    blocks = []
    for block in range(count):
        west, east = expand(first, block, index), expand(last, block, index)
        rows = [
            jnp.sum(bt_ref[block, a, :SUBS] * west + bt_ref[block, a, LANES - SUBS :] * east, axis=0, keepdims=True)
            for a in range(columns)
        ]
        blocks.append(jnp.concatenate(rows, axis=0))
    return jnp.concatenate(blocks, axis=1)


def add_sides(field, first, last):
    lon = lax.broadcasted_iota(jnp.int32, field.shape, 0)
    field = jnp.where(lon == 0, field + first, field)
    return jnp.where(lon == field.shape[0] - 1, field + last, field)


def product_kernel(bt_ref, field_ref, out_ref):
    blocks_product(bt_ref, field_ref[...], out_ref)


def second_kernel(
    low_ref, high_ref, inner_ref, outer_ref, near_ref, far_ref, residual_ref, search_ref, flow_ref, product_ref, diag_ref, east_face_ref, north_face_ref, ocean_ref, east_end_ref, bt_ref,
    residual_out, direction_out, diag_out, faces_out, norms_out, coef_out, inner_out, outer_out,
):
    store_coefficients(low_ref, high_ref, coef_out)
    ocean = ocean_ref[...]
    columns, rows = ocean.shape
    count = lane_blocks(rows)
    scale, keep, gain, keep_next, gain_next = (repeat_row(coef_out[n : n + 1], count) for n in (0, 2, 3, 4, 5))
    search = search_ref[...]
    even, low = even_device(), low_device()
    sides = [halo_rows(inner_ref, outer_ref, row, even) for row in range(PAIR_BACK_FACE + 1)]
    beyond = [
        (jnp.where(low, far, near), jnp.where(low, near, far))
        for near, far in ((near_ref[row : row + 1], far_ref[row : row + 1]) for row in range(2))
    ]
    here = (search[0:1], search[columns - 1 :])
    static = (ocean[0:1], east_end_ref[...])
    faces, pushes, later_halos = [], [], []
    for side in range(2):
        there, flow, face, back, back_face = (pair[side] for pair in sides)
        face = static[side] * face
        own_push = face * (scale * (here[side] - there))
        opposite_push = back_face * beyond[1][side] * (scale * (beyond[0][side] - back))
        from_inner = even if side == 1 else jnp.logical_not(even)
        own, opposite = (
            jnp.where(from_inner, inner_ref[row : row + SUBS], outer_ref[row : row + SUBS]) for row in (PAIR_OWN, PAIR_OPPOSITE)
        )
        faces.append(face)
        pushes.append(-own_push)
        later_halos.append(face * neighbour_direction(own, opposite, there, flow, own_push, opposite_push, coef_out))
    faces_out[0:1] = faces[0]
    faces_out[1:2] = faces[1]
    diag = add_sides(diag_ref[...], faces[0], faces[1])
    diag_out[...] = diag
    residual = add_sides(residual_ref[...] - scale * flow_ref[...], pushes[0], pushes[1])
    norms_out[...] = jnp.zeros_like(norms_out)
    norms_out[0:1, 0:LANES] = lane_partial(residual * residual)
    product = side_products(bt_ref, pushes[0], pushes[1]) - scale * product_ref[...]
    direction = keep * (scale * search) + gain * (search + ocean * product)
    direction_out[...] = direction
    residual = apply_operator(residual, direction, diag, east_face_ref[...], north_face_ref[...], later_halos[0], later_halos[1])
    residual_out[...] = residual
    first, last = edge_products(bt_ref, residual)
    store_edges(
        inner_out, outer_out, 0, even,
        keep_next * direction[0:1] + gain_next * (ocean[0:1] * first),
        keep_next * direction[columns - 1 :] + gain_next * (ocean[columns - 1 :] * last),
    )


def store_norm(norms_out, norms_ref, k, squares):
    norms_out[...] = norms_ref[...]
    norms_out[0:1, k * LANES : (k + 1) * LANES] = lane_partial(squares)


def ahead_kernel(
    residual_ref, direction_ref, search_ref, diag_ref, east_face_ref, north_face_ref, ocean_ref, coef_ref, norms_ref, bt_ref,
    residual_out, direction_out, solution_out, product_out, norms_out,
):
    residual = residual_ref[...]
    direction = direction_ref[...]
    store_norm(norms_out, norms_ref, 1, residual * residual)
    later = search_step(bt_ref, residual, direction, ocean_ref[...], coef_ref, 2, product_out)
    direction_out[...] = later
    scale = repeat_row(coef_ref[0:1], lane_blocks(residual.shape[1]))
    solution_out[...] = scale * search_ref[...] + direction + later
    nothing = jnp.zeros((1, residual.shape[1]), F32)
    residual = apply_operator(residual, later, diag_ref[...], east_face_ref[...], north_face_ref[...], nothing, nothing)
    residual_out[...] = residual
    blocks_product(bt_ref, residual, product_out)


FIRST_RES, FIRST_DIR, LAST_RES, LAST_DIR, LAST_FACE, SUMS, PACK_ROWS = 0, 1, 2, 3, 4, 5, 8


def closing_kernel(
    inner_ref, outer_ref, residual_ref, direction_ref, solution_ref, product_ref, diag_ref, east_face_ref, north_face_ref, ocean_ref, faces_ref, coef_ref, norms_ref, bt_ref,
    residual_out, solution_out, pack_out,
):
    west, east = halo_rows(inner_ref, outer_ref, 0, even_device())
    west, east = faces_ref[0:1] * west, faces_ref[1:2] * east
    residual = add_sides(residual_ref[...], west, east)
    keep, gain = (repeat_row(coef_ref[n : n + 1], lane_blocks(residual.shape[1])) for n in (2 * ITERS - 2, 2 * ITERS - 1))
    product = product_ref[...] + side_products(bt_ref, west, east)
    later = keep * direction_ref[...] + gain * (ocean_ref[...] * product)
    solution_out[...] = solution_ref[...] + later
    columns = residual.shape[0]
    sums = pack_out.at[SUMS : SUMS + 1]
    store_norm(sums, norms_ref, ITERS - 2, residual * residual)
    nothing = jnp.zeros_like(west)
    residual = apply_operator(residual, later, diag_ref[...], east_face_ref[...], north_face_ref[...], nothing, nothing)
    residual_out[...] = residual
    lon = lax.broadcasted_iota(jnp.int32, residual.shape, 0)
    inside = jnp.where((lon > 0) & (lon < columns - 1), residual, 0.0)
    sums[0:1, (ITERS - 1) * LANES : ITERS * LANES] = lane_partial(inside * inside)
    pack_out[FIRST_RES : FIRST_RES + 1] = residual[0:1]
    pack_out[FIRST_DIR : FIRST_DIR + 1] = later[0:1]
    pack_out[LAST_RES : LAST_RES + 1] = residual[columns - 1 :]
    pack_out[LAST_DIR : LAST_DIR + 1] = later[columns - 1 :]
    pack_out[LAST_FACE : LAST_FACE + 1] = faces_ref[1:2]
    pack_out[SUMS + 1 :] = jnp.zeros_like(pack_out[SUMS + 1 :])


def join_packs(size, radix, is_last, pack_ref, others, halo, packs):
    me = lax.axis_index("lon")
    mine = lax.rem(me // size, radix)
    packs[mine] = pack_ref[...]
    for s, other in enumerate(others, start=1):
        packs[mine ^ s] = other[...]

    def row(run, name):
        return packs[run % radix, name : name + 1, :]

    sums = functools.reduce(jnp.add, [row(run, SUMS) for run in range(radix)])
    total = None
    for run in range(radix if is_last else radix - 1):
        face = row(run, LAST_FACE)
        left = row(run, LAST_RES) + face * row(run + 1, FIRST_DIR)
        right = row(run + 1, FIRST_RES) + face * row(run, LAST_DIR)
        squares = lane_partial(left * left + right * right)
        total = squares if total is None else total + squares
    parts = [sums[:, i * LANES : (i + 1) * LANES] for i in range(sums.shape[1] // LANES)]
    parts[ITERS - 1] = parts[ITERS - 1] + total
    before = packs[lax.rem(mine + radix - 1, radix)][LAST_DIR : LAST_DIR + 1]
    after = packs[lax.rem(mine + 1, radix)][FIRST_DIR : FIRST_DIR + 1]
    place = lax.rem(me, size)
    west_now = place == 0
    east_now = place == size - 1
    if not is_last:
        west_now = west_now & (mine > 0)
        east_now = east_now & (mine < radix - 1)
    west, east = halo
    return parts, jnp.where(west_now, before, west), jnp.where(east_now, after, east)


def stage_kernel(size, radix, *refs):
    pack_ref, others, halo_ref = refs[0], refs[1:radix], refs[radix] if size > 1 else None
    pack_out, halo_out, packs = refs[-3:]
    nothing = jnp.zeros((1, pack_ref.shape[1]), F32)
    halo = (nothing, nothing) if halo_ref is None else (halo_ref[0:1], halo_ref[1:2])
    parts, west, east = join_packs(size, radix, False, pack_ref, others, halo, packs)
    pack_out[...] = packs[0]
    for name in (LAST_RES, LAST_DIR, LAST_FACE):
        pack_out[name : name + 1] = packs[radix - 1, name : name + 1, :]
    pack_out[SUMS : SUMS + 1] = jnp.concatenate(parts, axis=1)
    halo_out[0:1] = west
    halo_out[1:2] = east


def finish_kernel(size, radix, cells_all, *refs):
    pack_ref, others, halo_ref = refs[0], refs[1:radix], refs[radix]
    residual_ref, faces_ref, answer_ref = refs[radix + 1 : radix + 4]
    residual_out, answer_out, norms_out, packs = refs[radix + 4 :]
    parts, west, east = join_packs(size, radix, True, pack_ref, others, (halo_ref[0:1], halo_ref[1:2]), packs)
    answer_out[...] = answer_ref[...]
    residual = residual_ref[...]
    lon = lax.broadcasted_iota(jnp.int32, residual.shape, 0)
    residual = jnp.where(lon == 0, residual + faces_ref[0:1] * west, residual)
    residual = jnp.where(lon == residual.shape[0] - 1, residual + faces_ref[1:2] * east, residual)
    residual_out[...] = residual
    for k in range(ITERS):
        norms_out[k] = jnp.sum(parts[k]) / cells_all


def vmem():
    return pl.BlockSpec(memory_space=pltpu.VMEM)


def shape(*dims):
    return jax.ShapeDtypeStruct(dims, F32)


def smem():
    return pl.BlockSpec(memory_space=pltpu.SMEM)


def call(body, in_specs, outs, scratch, limit, cost=None, out_specs=None):
    return pl.pallas_call(
        body,
        in_specs=in_specs,
        out_specs=out_specs or [vmem()] * len(outs),
        out_shape=outs,
        scratch_shapes=scratch,
        compiler_params=pltpu.CompilerParams(vmem_limit_bytes=limit),
        cost_estimate=cost,
    )


def exchange(inner, outer):
    devices = lax.axis_size("lon")
    pairs = [(i, i ^ 1) for i in range(devices)]
    across = [(i, (i + 1 if i % 2 else i - 1) % devices) for i in range(devices)]
    return lax.ppermute(inner, "lon", pairs), lax.ppermute(outer, "lon", across)


def exchange_beyond(near, far):
    devices = lax.axis_size("lon")
    within = [(i, i ^ 2) for i in range(devices)]
    across = [(i, (i + 2 if i % 4 >= 2 else i - 2) % devices) for i in range(devices)]
    return lax.ppermute(near, "lon", within), lax.ppermute(far, "lon", across)


def swap_runs(pack, size, radix):
    devices = lax.axis_size("lon")
    return [
        lax.ppermute(pack, "lon", [(i, i ^ (s * size)) for i in range(devices)]) for s in range(radix - 1, 0, -1)
    ][::-1]


def on_device(
    right_side, east_coef, north_coef, surface_term, cell_mask, inverse_blocks, active_tiles, low_bound, high_bound
):
    columns, rows = right_side.shape
    tiles = inverse_blocks.shape[0]
    count = lane_blocks(rows)
    field = shape(columns, rows)
    row = shape(1, rows)
    two = shape(2, rows)
    bt_shape = shape(count, columns, LANES, LANES)
    (bt,) = call(
        transpose_kernel,
        [pl.BlockSpec(memory_space=pl.ANY)],
        [bt_shape],
        [pltpu.VMEM(inverse_blocks.shape, F32), pltpu.SemaphoreType.DMA((count,))],
        40 * MIB,
        pl.CostEstimate(flops=10**9, bytes_accessed=2 * inverse_blocks.size * 4, transcendentals=0),
    )(inverse_blocks)
    pair_shape = shape(PAIR_ROWS, rows)
    residual, search, diag, east_face, north_face, ocean, east_end, flow, inner, outer, near, far = call(
        first_kernel,
        [vmem()] * 7,
        [field, field, field, field, field, field, row, field, pair_shape, pair_shape, two, two],
        [],
        24 * MIB,
    )(active_tiles.reshape(-1, LANES), right_side, east_coef, north_coef, surface_term, cell_mask, bt)
    low_bound, high_bound, inner = lax.optimization_barrier((low_bound, high_bound, inner))
    inner, outer = exchange(inner, outer)
    near, far = exchange_beyond(near, far)
    work = pl.CostEstimate(flops=2 * bt.size, bytes_accessed=4 * bt.size, transcendentals=0)
    (product,) = call(product_kernel, [vmem()] * 2, [field], [], 24 * MIB, work)(bt, flow)
    residual, direction, diag, faces, norms, coef, inner, outer = call(
        second_kernel,
        [smem()] * 2 + [vmem()] * 14,
        [field, field, field, two, row, shape(SUBS, LANES), row, row],
        [],
        24 * MIB,
    )(
        low_bound, high_bound, inner, outer, near, far, residual, search, flow, product, diag, east_face, north_face,
        ocean, east_end, bt,
    )
    inner, outer = exchange(inner, outer)
    residual, direction, answer, product, norms = call(
        ahead_kernel,
        [vmem()] * 10,
        [field, field, field, field, row],
        [],
        24 * MIB,
        work,
    )(residual, direction, search, diag, east_face, north_face, ocean, coef, norms, bt)
    pack_shape = shape(PACK_ROWS, rows)
    residual, answer, pack = call(closing_kernel, [vmem()] * 14, [field, field, pack_shape], [], 24 * MIB)(
        inner, outer, residual, direction, answer, product, diag, east_face, north_face, ocean, faces, coef, norms, bt
    )
    devices = lax.axis_size("lon")
    size, halo = 1, []
    while True:
        radix = 4 if (devices // size) % 4 == 0 else 2
        others = swap_runs(pack, size, radix)
        packs = [pltpu.VMEM((radix, PACK_ROWS, rows), F32)]
        if size * radix == devices:
            break
        pack, *halo = call(
            functools.partial(stage_kernel, size, radix),
            [vmem()] * (radix + len(halo)),
            [pack_shape, two],
            packs,
            24 * MIB,
        )(pack, *others, *halo)
        size *= radix
    residual, answer, norms = call(
        functools.partial(finish_kernel, size, radix, float(columns * devices * rows)),
        [vmem()] * (radix + 4),
        [field, field, shape(ITERS)],
        packs,
        24 * MIB,
        out_specs=[vmem(), vmem(), smem()],
    )(pack, *others, *halo, residual, faces, answer)
    return answer, residual, norms


def solution(mesh):
    in_specs = (
        P(("member", "lon"), None),
        P("lon", None),
        P("lon", None),
        P("lon", None),
        P("lon", None),
        P("lon", None, None),
        P(),
        P(),
        P(),
    )
    out_specs = (P(("member", "lon"), None), P(("member", "lon"), None), P("member"))
    return jax.shard_map(on_device, mesh=mesh, in_specs=in_specs, out_specs=out_specs, check_vma=False)
```

```python
import functools

import jax
import jax.numpy as jnp
from jax import lax
from jax.experimental import pallas as pl
from jax.experimental.pallas import tpu as pltpu
from jax.sharding import PartitionSpec as P

ITERS = 4
LANES = 128
SUBS = 8
F32 = jnp.float32
MIB = 2**20


def lane_blocks(rows):
    return rows // LANES


def roll(x, shift, axis):
    return pltpu.roll(x, shift % x.shape[axis], axis)


def repeat_row(row, times):
    return jnp.concatenate([row] * times, axis=1)


def gather_index():
    lane = lax.broadcasted_iota(jnp.int32, (SUBS, LANES), 1)
    sub = lax.broadcasted_iota(jnp.int32, (SUBS, LANES), 0)
    return (lane // SUBS) * SUBS + sub


def expand(field, block, index):
    part = field[:, block * LANES : (block + 1) * LANES]
    rows = [
        jnp.take_along_axis(jnp.broadcast_to(part[a : a + 1], (SUBS, LANES)), index, axis=1)
        for a in range(part.shape[0])
    ]
    return jnp.concatenate(rows, axis=0)


def blocks_product(bt_ref, field, out_ref):
    index = gather_index()
    columns, rows = field.shape
    for block in range(lane_blocks(rows)):
        spread = expand(field, block, index)
        for a in range(columns):
            out_ref[a : a + 1, block * LANES : (block + 1) * LANES] = jnp.sum(
                bt_ref[block, a] * spread, axis=0, keepdims=True
            )


def even_device():
    return lax.rem(lax.axis_index("lon"), 2) == 0


def store_edges(inner_ref, outer_ref, row, even, first, last):
    inner_ref[row : row + 1] = jnp.where(even, last, first)
    outer_ref[row : row + 1] = jnp.where(even, first, last)


def halo_rows(inner_ref, outer_ref, row, even):
    inner, outer = inner_ref[row : row + 1], outer_ref[row : row + 1]
    return jnp.where(even, outer, inner), jnp.where(even, inner, outer)


def low_device():
    return lax.rem(lax.axis_index("lon"), 4) < 2


def lane_partial(squares):
    total = jnp.sum(squares, axis=0, keepdims=True)
    parts = [total[:, i * LANES : (i + 1) * LANES] for i in range(total.shape[1] // LANES)]
    return functools.reduce(jnp.add, parts)


def tile_flags(active_ref, first, tiles):
    active = active_ref[...]
    before = jnp.sum((active < first).astype(jnp.int32))
    row = jnp.minimum(before // LANES, active_ref.shape[0] - 2)
    lane = lax.broadcasted_iota(jnp.int32, (LANES, tiles), 1) + first
    found = jnp.zeros((LANES, tiles), jnp.int32)
    for step in range(2):
        entries = jnp.broadcast_to(active_ref[pl.ds(row + step, 1), :], (LANES, LANES))
        found = found + (entries.T == lane).astype(jnp.int32)
    return (jnp.sum(found, axis=0, keepdims=True) > 0).astype(F32)


def transpose_kernel(blocks_hbm, bt_ref, raw, sems):
    count, columns = bt_ref.shape[:2]
    step = blocks_hbm.shape[0] // count

    def fetch(i):
        part = pl.ds(i * step, step)
        return pltpu.make_async_copy(blocks_hbm.at[part], raw.at[part], sems.at[i])

    for i in range(count):
        fetch(i).start()
    for i in range(count):
        fetch(i).wait()
        for a in range(columns):
            bt_ref[i, a] = raw[i * step : (i + 1) * step, a * SUBS : (a + 1) * SUBS, :].reshape(LANES, LANES).T


PAIR_SEARCH, PAIR_FLOW, PAIR_FACE, PAIR_BACK_SEARCH, PAIR_BACK_FACE, PAIR_OWN, PAIR_OPPOSITE, PAIR_ROWS = 0, 1, 2, 3, 4, 8, 16, 24


def edge_products(bt_ref, field):
    columns, rows = field.shape
    index = gather_index()
    first, last = [], []
    for block in range(lane_blocks(rows)):
        spread = expand(field, block, index)
        first.append(jnp.sum(bt_ref[block, 0] * spread, axis=0, keepdims=True))
        last.append(jnp.sum(bt_ref[block, columns - 1] * spread, axis=0, keepdims=True))
    return jnp.concatenate(first, axis=1), jnp.concatenate(last, axis=1)


def first_kernel(
    active_ref, right_ref, east_ref, north_ref, surface_ref, mask_ref, bt_ref,
    residual_ref, search_ref, diag_ref, east_face_ref, north_face_ref, ocean_ref, east_end_ref, flow_ref, inner_ref, outer_ref, near_ref, far_ref,
):
    columns, rows = right_ref.shape
    count = lane_blocks(rows)
    tiles = rows // SUBS
    even = even_device()
    flags = tile_flags(active_ref, lax.axis_index("lon") * tiles, tiles)
    lane = lax.broadcasted_iota(jnp.int32, (SUBS, LANES), 1)
    spread = [
        jnp.take_along_axis(jnp.broadcast_to(flags, (SUBS, tiles)), i * (LANES // SUBS) + lane // SUBS, axis=1)
        for i in range(count)
    ]
    flag_lat = jnp.concatenate(spread, axis=1)[0:1]
    ocean = mask_ref[...].astype(F32) * flag_lat
    ocean_ref[...] = ocean
    lat = lax.broadcasted_iota(jnp.int32, (columns, rows), 1)
    lon = lax.broadcasted_iota(jnp.int32, (columns, rows), 0)
    east_ocean = east_ref[...] * ocean
    east_face = jnp.where(lon < columns - 1, east_ocean * roll(ocean, -1, 0), 0.0)
    north_face = jnp.where(lat < rows - 1, north_ref[...] * ocean * roll(ocean, -1, 1), 0.0)
    east_face_ref[...] = east_face
    north_face_ref[...] = north_face
    diag = surface_ref[...] * ocean + east_face + roll(east_face, 1, 0) + north_face + roll(north_face, 1, 1)
    diag_ref[...] = diag
    residual = right_ref[...] * ocean
    residual_ref[...] = residual
    east_end = east_ocean[columns - 1 :]
    east_end_ref[...] = east_end
    blocks_product(bt_ref, residual, search_ref)
    search = search_ref[...] * ocean
    search_ref[...] = search
    nothing = jnp.zeros_like(east_end)
    flow = apply_operator(jnp.zeros_like(search), -search, diag, east_face, north_face, nothing, nothing)
    flow_ref[...] = flow
    edges = edge_products(bt_ref, flow)
    fields = (
        (PAIR_SEARCH, search[0:1], search[columns - 1 :]),
        (PAIR_FLOW, edges[0] * ocean[0:1], edges[1] * ocean[columns - 1 :]),
        (PAIR_FACE, ocean[0:1], east_end),
        (PAIR_BACK_SEARCH, search[columns - 1 :], search[0:1]),
        (PAIR_BACK_FACE, east_end, ocean[0:1]),
    )
    for row, west, east in fields:
        store_edges(inner_ref, outer_ref, row, even, west, east)
    for ref, edge in ((inner_ref, jnp.where(even, columns - 1, 0)), (outer_ref, jnp.where(even, 0, columns - 1))):
        ref[len(fields) : SUBS] = jnp.zeros((SUBS - len(fields), rows), F32)
        for i in range(count):
            lanes = slice(i * LANES, (i + 1) * LANES)
            ref[PAIR_OWN : PAIR_OWN + SUBS, lanes] = bt_ref[i, edge, pl.ds(pl.multiple_of(edge * SUBS, SUBS), SUBS), :]
            back = columns - 1 - edge
            ref[PAIR_OPPOSITE : PAIR_OPPOSITE + SUBS, lanes] = bt_ref[i, edge, pl.ds(pl.multiple_of(back * SUBS, SUBS), SUBS), :]
    low = low_device()
    for row, west, east in ((0, search[0:1], search[columns - 1 :]), (1, ocean[0:1], east_end)):
        near_ref[row : row + 1] = jnp.where(low, east, west)
        far_ref[row : row + 1] = jnp.where(low, west, east)


def apply_operator(residual, direction, diag, east_face, north_face, west_term, east_term):
    flow = diag * direction
    flow = flow - east_face * roll(direction, -1, 0) - roll(east_face, 1, 0) * roll(direction, 1, 0)
    flow = flow - north_face * roll(direction, -1, 1) - roll(north_face, 1, 1) * roll(direction, 1, 1)
    lon = lax.broadcasted_iota(jnp.int32, residual.shape, 0)
    flow = jnp.where(lon == 0, flow - west_term, flow)
    flow = jnp.where(lon == residual.shape[0] - 1, flow - east_term, flow)
    return residual - flow


def search_step(bt_ref, residual, direction, ocean, coef_ref, k, search_ref):
    count = lane_blocks(residual.shape[1])
    blocks_product(bt_ref, residual, search_ref)
    keep = repeat_row(coef_ref[2 * k : 2 * k + 1], count)
    gain = repeat_row(coef_ref[2 * k + 1 : 2 * k + 2], count)
    return keep * direction + gain * (ocean * search_ref[...])


def store_coefficients(low_ref, high_ref, coef_ref):
    low = jnp.full((1, LANES), low_ref[0], F32)
    high = jnp.full((1, LANES), high_ref[0], F32)
    center = (high + low) / 2.0
    radius = (high - low) / 2.0
    ratio = center / radius
    weight_prev = 1.0 / ratio
    coef_ref[0:1] = 1.0 / center
    for k in range(1, ITERS):
        weight = 1.0 / (2.0 * ratio - weight_prev)
        coef_ref[2 * k : 2 * k + 1] = weight * weight_prev
        coef_ref[2 * k + 1 : 2 * k + 2] = 2.0 * weight / radius
        weight_prev = weight


def neighbour_direction(own, opposite, search, flow, own_push, opposite_push, coef_ref):
    rows = search.shape[1]
    count = lane_blocks(rows)
    index = gather_index()
    parts = []
    for block in range(count):
        lanes = slice(block * LANES, (block + 1) * LANES)
        product = own[:, lanes] * expand(own_push, block, index) + opposite[:, lanes] * expand(opposite_push, block, index)
        parts.append(jnp.sum(product, axis=0, keepdims=True))
    scale, keep, gain = (repeat_row(coef_ref[n : n + 1], count) for n in (0, 2, 3))
    return keep * (scale * search) + gain * (search - scale * flow + jnp.concatenate(parts, axis=1))


def side_products(bt_ref, first, last):
    count, columns = bt_ref.shape[:2]
    index = gather_index()
    blocks = []
    for block in range(count):
        west, east = expand(first, block, index), expand(last, block, index)
        rows = [
            jnp.sum(bt_ref[block, a, :SUBS] * west + bt_ref[block, a, LANES - SUBS :] * east, axis=0, keepdims=True)
            for a in range(columns)
        ]
        blocks.append(jnp.concatenate(rows, axis=0))
    return jnp.concatenate(blocks, axis=1)


def add_sides(field, first, last):
    lon = lax.broadcasted_iota(jnp.int32, field.shape, 0)
    field = jnp.where(lon == 0, field + first, field)
    return jnp.where(lon == field.shape[0] - 1, field + last, field)


def product_kernel(bt_ref, field_ref, out_ref):
    blocks_product(bt_ref, field_ref[...], out_ref)


def second_kernel(
    low_ref, high_ref, far_ref, outer_ref, near_ref, inner_ref, residual_ref, search_ref, flow_ref, product_ref, diag_ref, east_face_ref, north_face_ref, ocean_ref, east_end_ref, bt_ref,
    residual_out, direction_out, diag_out, faces_out, norms_out, coef_out, inner_out, outer_out,
):
    store_coefficients(low_ref, high_ref, coef_out)
    ocean = ocean_ref[...]
    columns, rows = ocean.shape
    count = lane_blocks(rows)
    scale, keep, gain, keep_next, gain_next = (repeat_row(coef_out[n : n + 1], count) for n in (0, 2, 3, 4, 5))
    search = search_ref[...]
    even, low = even_device(), low_device()
    sides = [halo_rows(inner_ref, outer_ref, row, even) for row in range(PAIR_BACK_FACE + 1)]
    beyond = [
        (jnp.where(low, far, near), jnp.where(low, near, far))
        for near, far in ((near_ref[row : row + 1], far_ref[row : row + 1]) for row in range(2))
    ]
    here = (search[0:1], search[columns - 1 :])
    static = (ocean[0:1], east_end_ref[...])
    faces, pushes, later_halos = [], [], []
    for side in range(2):
        there, flow, face, back, back_face = (pair[side] for pair in sides)
        face = static[side] * face
        own_push = face * (scale * (here[side] - there))
        opposite_push = back_face * beyond[1][side] * (scale * (beyond[0][side] - back))
        from_inner = even if side == 1 else jnp.logical_not(even)
        own, opposite = (
            jnp.where(from_inner, inner_ref[row : row + SUBS], outer_ref[row : row + SUBS]) for row in (PAIR_OWN, PAIR_OPPOSITE)
        )
        faces.append(face)
        pushes.append(-own_push)
        later_halos.append(face * neighbour_direction(own, opposite, there, flow, own_push, opposite_push, coef_out))
    faces_out[0:1] = faces[0]
    faces_out[1:2] = faces[1]
    diag = add_sides(diag_ref[...], faces[0], faces[1])
    diag_out[...] = diag
    residual = add_sides(residual_ref[...] - scale * flow_ref[...], pushes[0], pushes[1])
    norms_out[...] = jnp.zeros_like(norms_out)
    norms_out[0:1, 0:LANES] = lane_partial(residual * residual)
    product = side_products(bt_ref, pushes[0], pushes[1]) - scale * product_ref[...]
    direction = keep * (scale * search) + gain * (search + ocean * product)
    direction_out[...] = direction
    residual = apply_operator(residual, direction, diag, east_face_ref[...], north_face_ref[...], later_halos[0], later_halos[1])
    residual_out[...] = residual
    first, last = edge_products(bt_ref, residual)
    store_edges(
        inner_out, outer_out, 0, even,
        keep_next * direction[0:1] + gain_next * (ocean[0:1] * first),
        keep_next * direction[columns - 1 :] + gain_next * (ocean[columns - 1 :] * last),
    )


def store_norm(norms_out, norms_ref, k, squares):
    norms_out[...] = norms_ref[...]
    norms_out[0:1, k * LANES : (k + 1) * LANES] = lane_partial(squares)


def ahead_kernel(
    residual_ref, direction_ref, search_ref, diag_ref, east_face_ref, north_face_ref, ocean_ref, coef_ref, norms_ref, bt_ref,
    residual_out, direction_out, solution_out, product_out, norms_out,
):
    residual = residual_ref[...]
    direction = direction_ref[...]
    store_norm(norms_out, norms_ref, 1, residual * residual)
    later = search_step(bt_ref, residual, direction, ocean_ref[...], coef_ref, 2, product_out)
    direction_out[...] = later
    scale = repeat_row(coef_ref[0:1], lane_blocks(residual.shape[1]))
    solution_out[...] = scale * search_ref[...] + direction + later
    nothing = jnp.zeros((1, residual.shape[1]), F32)
    residual = apply_operator(residual, later, diag_ref[...], east_face_ref[...], north_face_ref[...], nothing, nothing)
    residual_out[...] = residual
    blocks_product(bt_ref, residual, product_out)


FIRST_RES, FIRST_DIR, LAST_RES, LAST_DIR, LAST_FACE, SUMS, PACK_ROWS = 0, 1, 2, 3, 4, 5, 8


def closing_kernel(
    outer_ref, inner_ref, residual_ref, direction_ref, solution_ref, product_ref, diag_ref, east_face_ref, north_face_ref, ocean_ref, faces_ref, coef_ref, norms_ref, bt_ref,
    residual_out, solution_out, pack_out,
):
    west, east = halo_rows(inner_ref, outer_ref, 0, even_device())
    west, east = faces_ref[0:1] * west, faces_ref[1:2] * east
    residual = add_sides(residual_ref[...], west, east)
    keep, gain = (repeat_row(coef_ref[n : n + 1], lane_blocks(residual.shape[1])) for n in (2 * ITERS - 2, 2 * ITERS - 1))
    product = product_ref[...] + side_products(bt_ref, west, east)
    later = keep * direction_ref[...] + gain * (ocean_ref[...] * product)
    solution_out[...] = solution_ref[...] + later
    columns = residual.shape[0]
    sums = pack_out.at[SUMS : SUMS + 1]
    store_norm(sums, norms_ref, ITERS - 2, residual * residual)
    nothing = jnp.zeros_like(west)
    residual = apply_operator(residual, later, diag_ref[...], east_face_ref[...], north_face_ref[...], nothing, nothing)
    residual_out[...] = residual
    lon = lax.broadcasted_iota(jnp.int32, residual.shape, 0)
    inside = jnp.where((lon > 0) & (lon < columns - 1), residual, 0.0)
    sums[0:1, (ITERS - 1) * LANES : ITERS * LANES] = lane_partial(inside * inside)
    pack_out[FIRST_RES : FIRST_RES + 1] = residual[0:1]
    pack_out[FIRST_DIR : FIRST_DIR + 1] = later[0:1]
    pack_out[LAST_RES : LAST_RES + 1] = residual[columns - 1 :]
    pack_out[LAST_DIR : LAST_DIR + 1] = later[columns - 1 :]
    pack_out[LAST_FACE : LAST_FACE + 1] = faces_ref[1:2]
    pack_out[SUMS + 1 :] = jnp.zeros_like(pack_out[SUMS + 1 :])


def swap_order(size, radix):
    return (1,) if radix == 2 else (1, 2, 3) if size == 1 else (1, 3, 2)


def join_packs(size, radix, is_last, pack_ref, others, halo, packs):
    me = lax.axis_index("lon")
    mine = lax.rem(me // size, radix)
    packs[mine] = pack_ref[...]
    for s, other in zip(swap_order(size, radix), others):
        packs[mine ^ s] = other[...]

    def row(run, name):
        return packs[run % radix, name : name + 1, :]

    sums = functools.reduce(jnp.add, [row(run, SUMS) for run in range(radix)])
    total = None
    for run in range(radix if is_last else radix - 1):
        face = row(run, LAST_FACE)
        left = row(run, LAST_RES) + face * row(run + 1, FIRST_DIR)
        right = row(run + 1, FIRST_RES) + face * row(run, LAST_DIR)
        squares = lane_partial(left * left + right * right)
        total = squares if total is None else total + squares
    parts = [sums[:, i * LANES : (i + 1) * LANES] for i in range(sums.shape[1] // LANES)]
    parts[ITERS - 1] = parts[ITERS - 1] + total
    before = packs[lax.rem(mine + radix - 1, radix)][LAST_DIR : LAST_DIR + 1]
    after = packs[lax.rem(mine + 1, radix)][FIRST_DIR : FIRST_DIR + 1]
    place = lax.rem(me, size)
    west_now = place == 0
    east_now = place == size - 1
    if not is_last:
        west_now = west_now & (mine > 0)
        east_now = east_now & (mine < radix - 1)
    west, east = halo
    return parts, jnp.where(west_now, before, west), jnp.where(east_now, after, east)


def stage_kernel(size, radix, *refs):
    pack_ref, others, halo_ref = refs[0], refs[1:radix], refs[radix] if size > 1 else None
    pack_out, halo_out, packs = refs[-3:]
    nothing = jnp.zeros((1, pack_ref.shape[1]), F32)
    halo = (nothing, nothing) if halo_ref is None else (halo_ref[0:1], halo_ref[1:2])
    parts, west, east = join_packs(size, radix, False, pack_ref, others, halo, packs)
    pack_out[...] = packs[0]
    for name in (LAST_RES, LAST_DIR, LAST_FACE):
        pack_out[name : name + 1] = packs[radix - 1, name : name + 1, :]
    pack_out[SUMS : SUMS + 1] = jnp.concatenate(parts, axis=1)
    halo_out[0:1] = west
    halo_out[1:2] = east


def finish_kernel(size, radix, cells_all, *refs):
    pack_ref, others, halo_ref = refs[0], refs[1:radix], refs[radix]
    residual_ref, faces_ref, answer_ref = refs[radix + 1 : radix + 4]
    residual_out, answer_out, norms_out, packs = refs[radix + 4 :]
    parts, west, east = join_packs(size, radix, True, pack_ref, others, (halo_ref[0:1], halo_ref[1:2]), packs)
    answer_out[...] = answer_ref[...]
    residual = residual_ref[...]
    lon = lax.broadcasted_iota(jnp.int32, residual.shape, 0)
    residual = jnp.where(lon == 0, residual + faces_ref[0:1] * west, residual)
    residual = jnp.where(lon == residual.shape[0] - 1, residual + faces_ref[1:2] * east, residual)
    residual_out[...] = residual
    for k in range(ITERS):
        norms_out[k] = jnp.sum(parts[k]) / cells_all


def vmem():
    return pl.BlockSpec(memory_space=pltpu.VMEM)


def shape(*dims):
    return jax.ShapeDtypeStruct(dims, F32)


def smem():
    return pl.BlockSpec(memory_space=pltpu.SMEM)


def call(body, in_specs, outs, scratch, limit, cost=None, out_specs=None):
    return pl.pallas_call(
        body,
        in_specs=in_specs,
        out_specs=out_specs or [vmem()] * len(outs),
        out_shape=outs,
        scratch_shapes=scratch,
        compiler_params=pltpu.CompilerParams(vmem_limit_bytes=limit),
        cost_estimate=cost,
    )


def exchange(inner, outer):
    devices = lax.axis_size("lon")
    pairs = [(i, i ^ 1) for i in range(devices)]
    across = [(i, (i + 1 if i % 2 else i - 1) % devices) for i in range(devices)]
    return lax.ppermute(inner, "lon", pairs), lax.ppermute(outer, "lon", across)


def exchange_beyond(near, far):
    devices = lax.axis_size("lon")
    within = [(i, i ^ 2) for i in range(devices)]
    across = [(i, (i + 2 if i % 4 >= 2 else i - 2) % devices) for i in range(devices)]
    return lax.ppermute(near, "lon", within), lax.ppermute(far, "lon", across)


def swap_runs(pack, size, radix):
    devices = lax.axis_size("lon")
    return [
        lax.ppermute(pack, "lon", [(i, i ^ (s * size)) for i in range(devices)]) for s in swap_order(size, radix)
    ]


def on_device(
    right_side, east_coef, north_coef, surface_term, cell_mask, inverse_blocks, active_tiles, low_bound, high_bound
):
    columns, rows = right_side.shape
    tiles = inverse_blocks.shape[0]
    count = lane_blocks(rows)
    field = shape(columns, rows)
    row = shape(1, rows)
    two = shape(2, rows)
    bt_shape = shape(count, columns, LANES, LANES)
    (bt,) = call(
        transpose_kernel,
        [pl.BlockSpec(memory_space=pl.ANY)],
        [bt_shape],
        [pltpu.VMEM(inverse_blocks.shape, F32), pltpu.SemaphoreType.DMA((count,))],
        40 * MIB,
        pl.CostEstimate(flops=10**9, bytes_accessed=2 * inverse_blocks.size * 4, transcendentals=0),
    )(inverse_blocks)
    pair_shape = shape(PAIR_ROWS, rows)
    residual, search, diag, east_face, north_face, ocean, east_end, flow, inner, outer, near, far = call(
        first_kernel,
        [vmem()] * 7,
        [field, field, field, field, field, field, row, field, pair_shape, pair_shape, two, two],
        [],
        24 * MIB,
    )(active_tiles.reshape(-1, LANES), right_side, east_coef, north_coef, surface_term, cell_mask, bt)
    low_bound, high_bound, outer = lax.optimization_barrier((low_bound, high_bound, outer))
    inner, outer = exchange(inner, outer)
    near, far = exchange_beyond(near, far)
    work = pl.CostEstimate(flops=2 * bt.size, bytes_accessed=4 * bt.size, transcendentals=0)
    (product,) = call(product_kernel, [vmem()] * 2, [field], [], 24 * MIB, work)(bt, flow)
    residual, direction, diag, faces, norms, coef, inner, outer = call(
        second_kernel,
        [smem()] * 2 + [vmem()] * 14,
        [field, field, field, two, row, shape(SUBS, LANES), row, row],
        [],
        24 * MIB,
    )(
        low_bound, high_bound, far, outer, near, inner, residual, search, flow, product, diag, east_face, north_face,
        ocean, east_end, bt,
    )
    inner, outer = exchange(inner, outer)
    residual, direction, answer, product, norms = call(
        ahead_kernel,
        [vmem()] * 10,
        [field, field, field, field, row],
        [],
        24 * MIB,
        work,
    )(residual, direction, search, diag, east_face, north_face, ocean, coef, norms, bt)
    pack_shape = shape(PACK_ROWS, rows)
    residual, answer, pack = call(closing_kernel, [vmem()] * 14, [field, field, pack_shape], [], 24 * MIB)(
        outer, inner, residual, direction, answer, product, diag, east_face, north_face, ocean, faces, coef, norms, bt
    )
    devices = lax.axis_size("lon")
    size, halo = 1, []
    while True:
        radix = 4 if (devices // size) % 4 == 0 else 2
        others = swap_runs(pack, size, radix)
        packs = [pltpu.VMEM((radix, PACK_ROWS, rows), F32)]
        if size * radix == devices:
            break
        pack, *halo = call(
            functools.partial(stage_kernel, size, radix),
            [vmem()] * (radix + len(halo)),
            [pack_shape, two],
            packs,
            24 * MIB,
        )(pack, *others, *halo)
        size *= radix
    residual, answer, norms = call(
        functools.partial(finish_kernel, size, radix, float(columns * devices * rows)),
        [vmem()] * (radix + 4),
        [field, field, shape(ITERS)],
        packs,
        24 * MIB,
        out_specs=[vmem(), vmem(), smem()],
    )(pack, *others, *halo, residual, faces, answer)
    return answer, residual, norms


def solution(mesh):
    in_specs = (
        P(("member", "lon"), None),
        P("lon", None),
        P("lon", None),
        P("lon", None),
        P("lon", None),
        P("lon", None, None),
        P(),
        P(),
        P(),
    )
    out_specs = (P(("member", "lon"), None), P(("member", "lon"), None), P("member"))
    return jax.shard_map(on_device, mesh=mesh, in_specs=in_specs, out_specs=out_specs, check_vma=False)
```

```python
import functools

import jax
import jax.numpy as jnp
from jax import lax
from jax.experimental import pallas as pl
from jax.experimental.pallas import tpu as pltpu
from jax.sharding import PartitionSpec as P

ITERS = 4
LANES = 128
SUBS = 8
F32 = jnp.float32
MIB = 2**20


def lane_blocks(rows):
    return rows // LANES


def roll(x, shift, axis):
    return pltpu.roll(x, shift % x.shape[axis], axis)


def repeat_row(row, times):
    return jnp.concatenate([row] * times, axis=1)


def gather_index():
    lane = lax.broadcasted_iota(jnp.int32, (SUBS, LANES), 1)
    sub = lax.broadcasted_iota(jnp.int32, (SUBS, LANES), 0)
    return (lane // SUBS) * SUBS + sub


def expand(field, block, index):
    part = field[:, block * LANES : (block + 1) * LANES]
    rows = [
        jnp.take_along_axis(jnp.broadcast_to(part[a : a + 1], (SUBS, LANES)), index, axis=1)
        for a in range(part.shape[0])
    ]
    return jnp.concatenate(rows, axis=0)


def fold(parts):
    sub = lax.broadcasted_iota(jnp.int32, (SUBS, LANES), 0)
    half = SUBS // 2
    while half:
        upper = (sub & half) == 0
        parts = [
            jnp.where(upper, low, high) + jnp.where(upper, roll(low, -half, 0), roll(high, half, 0))
            for low, high in zip(parts[:half], parts[half:])
        ]
        half //= 2
    return parts[0]


def row_sums(product):
    return functools.reduce(jnp.add, [product[i : i + SUBS] for i in range(0, product.shape[0], SUBS)])


def blocks_product(bt_ref, field, out_ref):
    index = gather_index()
    columns, rows = field.shape
    for block in range(lane_blocks(rows)):
        spread = expand(field, block, index)
        for first in range(0, columns, SUBS):
            parts = [row_sums(bt_ref[block, a] * spread) for a in range(first, first + SUBS)]
            out_ref[first : first + SUBS, block * LANES : (block + 1) * LANES] = fold(parts)


def even_device():
    return lax.rem(lax.axis_index("lon"), 2) == 0


def store_edges(inner_ref, outer_ref, row, even, first, last):
    inner_ref[row : row + 1] = jnp.where(even, last, first)
    outer_ref[row : row + 1] = jnp.where(even, first, last)


def halo_rows(inner_ref, outer_ref, row, even):
    inner, outer = inner_ref[row : row + 1], outer_ref[row : row + 1]
    return jnp.where(even, outer, inner), jnp.where(even, inner, outer)


def low_device():
    return lax.rem(lax.axis_index("lon"), 4) < 2


def lane_partial(squares):
    total = jnp.sum(squares, axis=0, keepdims=True)
    parts = [total[:, i * LANES : (i + 1) * LANES] for i in range(total.shape[1] // LANES)]
    return functools.reduce(jnp.add, parts)


def tile_flags(active_ref, first, tiles):
    active = active_ref[...]
    before = jnp.sum((active < first).astype(jnp.int32))
    row = jnp.minimum(before // LANES, active_ref.shape[0] - 2)
    lane = lax.broadcasted_iota(jnp.int32, (LANES, tiles), 1) + first
    found = jnp.zeros((LANES, tiles), jnp.int32)
    for step in range(2):
        entries = jnp.broadcast_to(active_ref[pl.ds(row + step, 1), :], (LANES, LANES))
        found = found + (entries.T == lane).astype(jnp.int32)
    return (jnp.sum(found, axis=0, keepdims=True) > 0).astype(F32)


def transpose_kernel(blocks_hbm, bt_ref, raw, sems):
    count, columns = bt_ref.shape[:2]
    step = blocks_hbm.shape[0] // count

    def fetch(i):
        part = pl.ds(i * step, step)
        return pltpu.make_async_copy(blocks_hbm.at[part], raw.at[part], sems.at[i])

    for i in range(count):
        fetch(i).start()
    for i in range(count):
        fetch(i).wait()
        for a in range(columns):
            bt_ref[i, a] = raw[i * step : (i + 1) * step, a * SUBS : (a + 1) * SUBS, :].reshape(LANES, LANES).T


PAIR_SEARCH, PAIR_FLOW, PAIR_FACE, PAIR_BACK_SEARCH, PAIR_BACK_FACE, PAIR_OWN, PAIR_OPPOSITE, PAIR_ROWS = 0, 1, 2, 3, 4, 8, 16, 24


def edge_products(bt_ref, field):
    columns, rows = field.shape
    index = gather_index()
    first, last = [], []
    for block in range(lane_blocks(rows)):
        spread = expand(field, block, index)
        first.append(jnp.sum(bt_ref[block, 0] * spread, axis=0, keepdims=True))
        last.append(jnp.sum(bt_ref[block, columns - 1] * spread, axis=0, keepdims=True))
    return jnp.concatenate(first, axis=1), jnp.concatenate(last, axis=1)


def first_kernel(
    active_ref, right_ref, east_ref, north_ref, surface_ref, mask_ref, bt_ref,
    residual_ref, search_ref, diag_ref, east_face_ref, north_face_ref, ocean_ref, east_end_ref, flow_ref, inner_ref, outer_ref, near_ref, far_ref,
):
    columns, rows = right_ref.shape
    count = lane_blocks(rows)
    tiles = rows // SUBS
    even = even_device()
    flags = tile_flags(active_ref, lax.axis_index("lon") * tiles, tiles)
    right = right_ref[...] * mask_ref[...].astype(F32)
    blocks_product(bt_ref, right, search_ref)
    lane = lax.broadcasted_iota(jnp.int32, (SUBS, LANES), 1)
    spread = [
        jnp.take_along_axis(jnp.broadcast_to(flags, (SUBS, tiles)), i * (LANES // SUBS) + lane // SUBS, axis=1)
        for i in range(count)
    ]
    flag_lat = jnp.concatenate(spread, axis=1)[0:1]
    ocean = mask_ref[...].astype(F32) * flag_lat
    ocean_ref[...] = ocean
    lat = lax.broadcasted_iota(jnp.int32, (columns, rows), 1)
    lon = lax.broadcasted_iota(jnp.int32, (columns, rows), 0)
    east_ocean = east_ref[...] * ocean
    east_face = jnp.where(lon < columns - 1, east_ocean * roll(ocean, -1, 0), 0.0)
    north_face = jnp.where(lat < rows - 1, north_ref[...] * ocean * roll(ocean, -1, 1), 0.0)
    east_face_ref[...] = east_face
    north_face_ref[...] = north_face
    diag = surface_ref[...] * ocean + east_face + roll(east_face, 1, 0) + north_face + roll(north_face, 1, 1)
    diag_ref[...] = diag
    residual = right_ref[...] * ocean
    residual_ref[...] = residual
    east_end = east_ocean[columns - 1 :]
    east_end_ref[...] = east_end
    search = search_ref[...] * ocean
    search_ref[...] = search
    nothing = jnp.zeros_like(east_end)
    flow = apply_operator(jnp.zeros_like(search), -search, diag, east_face, north_face, nothing, nothing)
    flow_ref[...] = flow
    edges = edge_products(bt_ref, flow)
    fields = (
        (PAIR_SEARCH, search[0:1], search[columns - 1 :]),
        (PAIR_FLOW, edges[0] * ocean[0:1], edges[1] * ocean[columns - 1 :]),
        (PAIR_FACE, ocean[0:1], east_end),
        (PAIR_BACK_SEARCH, search[columns - 1 :], search[0:1]),
        (PAIR_BACK_FACE, east_end, ocean[0:1]),
    )
    for row, west, east in fields:
        store_edges(inner_ref, outer_ref, row, even, west, east)
    for ref, edge in ((inner_ref, jnp.where(even, columns - 1, 0)), (outer_ref, jnp.where(even, 0, columns - 1))):
        ref[len(fields) : SUBS] = jnp.zeros((SUBS - len(fields), rows), F32)
        for i in range(count):
            lanes = slice(i * LANES, (i + 1) * LANES)
            ref[PAIR_OWN : PAIR_OWN + SUBS, lanes] = bt_ref[i, edge, pl.ds(pl.multiple_of(edge * SUBS, SUBS), SUBS), :]
            back = columns - 1 - edge
            ref[PAIR_OPPOSITE : PAIR_OPPOSITE + SUBS, lanes] = bt_ref[i, edge, pl.ds(pl.multiple_of(back * SUBS, SUBS), SUBS), :]
    low = low_device()
    for row, west, east in ((0, search[0:1], search[columns - 1 :]), (1, ocean[0:1], east_end)):
        near_ref[row : row + 1] = jnp.where(low, east, west)
        far_ref[row : row + 1] = jnp.where(low, west, east)


def apply_operator(residual, direction, diag, east_face, north_face, west_term, east_term):
    flow = diag * direction
    flow = flow - east_face * roll(direction, -1, 0) - roll(east_face, 1, 0) * roll(direction, 1, 0)
    flow = flow - north_face * roll(direction, -1, 1) - roll(north_face, 1, 1) * roll(direction, 1, 1)
    lon = lax.broadcasted_iota(jnp.int32, residual.shape, 0)
    flow = jnp.where(lon == 0, flow - west_term, flow)
    flow = jnp.where(lon == residual.shape[0] - 1, flow - east_term, flow)
    return residual - flow


def search_step(bt_ref, residual, direction, ocean, coef_ref, k, search_ref):
    count = lane_blocks(residual.shape[1])
    blocks_product(bt_ref, residual, search_ref)
    keep = repeat_row(coef_ref[2 * k : 2 * k + 1], count)
    gain = repeat_row(coef_ref[2 * k + 1 : 2 * k + 2], count)
    return keep * direction + gain * (ocean * search_ref[...])


def store_coefficients(low_ref, high_ref, coef_ref):
    low = jnp.full((1, LANES), low_ref[0], F32)
    high = jnp.full((1, LANES), high_ref[0], F32)
    center = (high + low) / 2.0
    radius = (high - low) / 2.0
    ratio = center / radius
    weight_prev = 1.0 / ratio
    coef_ref[0:1] = 1.0 / center
    for k in range(1, ITERS):
        weight = 1.0 / (2.0 * ratio - weight_prev)
        coef_ref[2 * k : 2 * k + 1] = weight * weight_prev
        coef_ref[2 * k + 1 : 2 * k + 2] = 2.0 * weight / radius
        weight_prev = weight


def neighbour_direction(own, opposite, search, flow, own_push, opposite_push, coef_ref):
    rows = search.shape[1]
    count = lane_blocks(rows)
    index = gather_index()
    parts = []
    for block in range(count):
        lanes = slice(block * LANES, (block + 1) * LANES)
        product = own[:, lanes] * expand(own_push, block, index) + opposite[:, lanes] * expand(opposite_push, block, index)
        parts.append(jnp.sum(product, axis=0, keepdims=True))
    scale, keep, gain = (repeat_row(coef_ref[n : n + 1], count) for n in (0, 2, 3))
    return keep * (scale * search) + gain * (search - scale * flow + jnp.concatenate(parts, axis=1))


def side_products(bt_ref, first, last):
    count, columns = bt_ref.shape[:2]
    index = gather_index()
    blocks = []
    for block in range(count):
        west, east = expand(first, block, index), expand(last, block, index)
        parts = [bt_ref[block, a, :SUBS] * west + bt_ref[block, a, LANES - SUBS :] * east for a in range(columns)]
        rows = [fold(parts[a : a + SUBS]) for a in range(0, columns, SUBS)]
        blocks.append(jnp.concatenate(rows, axis=0))
    return jnp.concatenate(blocks, axis=1)


def add_sides(field, first, last):
    lon = lax.broadcasted_iota(jnp.int32, field.shape, 0)
    field = jnp.where(lon == 0, field + first, field)
    return jnp.where(lon == field.shape[0] - 1, field + last, field)


def product_kernel(bt_ref, field_ref, out_ref):
    blocks_product(bt_ref, field_ref[...], out_ref)


def second_kernel(
    low_ref, high_ref, far_ref, outer_ref, near_ref, inner_ref, residual_ref, search_ref, flow_ref, product_ref, diag_ref, east_face_ref, north_face_ref, ocean_ref, east_end_ref, bt_ref,
    residual_out, direction_out, diag_out, faces_out, norms_out, coef_out, inner_out, outer_out,
):
    store_coefficients(low_ref, high_ref, coef_out)
    ocean = ocean_ref[...]
    columns, rows = ocean.shape
    count = lane_blocks(rows)
    scale, keep, gain, keep_next, gain_next = (repeat_row(coef_out[n : n + 1], count) for n in (0, 2, 3, 4, 5))
    search = search_ref[...]
    even, low = even_device(), low_device()
    sides = [halo_rows(inner_ref, outer_ref, row, even) for row in range(PAIR_BACK_FACE + 1)]
    beyond = [
        (jnp.where(low, far, near), jnp.where(low, near, far))
        for near, far in ((near_ref[row : row + 1], far_ref[row : row + 1]) for row in range(2))
    ]
    here = (search[0:1], search[columns - 1 :])
    static = (ocean[0:1], east_end_ref[...])
    faces, pushes, later_halos = [], [], []
    for side in range(2):
        there, flow, face, back, back_face = (pair[side] for pair in sides)
        face = static[side] * face
        own_push = face * (scale * (here[side] - there))
        opposite_push = back_face * beyond[1][side] * (scale * (beyond[0][side] - back))
        from_inner = even if side == 1 else jnp.logical_not(even)
        own, opposite = (
            jnp.where(from_inner, inner_ref[row : row + SUBS], outer_ref[row : row + SUBS]) for row in (PAIR_OWN, PAIR_OPPOSITE)
        )
        faces.append(face)
        pushes.append(-own_push)
        later_halos.append(face * neighbour_direction(own, opposite, there, flow, own_push, opposite_push, coef_out))
    faces_out[0:1] = faces[0]
    faces_out[1:2] = faces[1]
    diag = add_sides(diag_ref[...], faces[0], faces[1])
    diag_out[...] = diag
    residual = add_sides(residual_ref[...] - scale * flow_ref[...], pushes[0], pushes[1])
    norms_out[...] = jnp.zeros_like(norms_out)
    norms_out[0:1, 0:LANES] = lane_partial(residual * residual)
    product = side_products(bt_ref, pushes[0], pushes[1]) - scale * product_ref[...]
    direction = keep * (scale * search) + gain * (search + ocean * product)
    direction_out[...] = direction
    residual = apply_operator(residual, direction, diag, east_face_ref[...], north_face_ref[...], later_halos[0], later_halos[1])
    residual_out[...] = residual
    first, last = edge_products(bt_ref, residual)
    store_edges(
        inner_out, outer_out, 0, even,
        keep_next * direction[0:1] + gain_next * (ocean[0:1] * first),
        keep_next * direction[columns - 1 :] + gain_next * (ocean[columns - 1 :] * last),
    )


def store_norm(norms_out, norms_ref, k, squares):
    norms_out[...] = norms_ref[...]
    norms_out[0:1, k * LANES : (k + 1) * LANES] = lane_partial(squares)


def ahead_kernel(
    residual_ref, direction_ref, search_ref, diag_ref, east_face_ref, north_face_ref, ocean_ref, coef_ref, norms_ref, bt_ref,
    residual_out, direction_out, solution_out, product_out, norms_out,
):
    residual = residual_ref[...]
    direction = direction_ref[...]
    store_norm(norms_out, norms_ref, 1, residual * residual)
    later = search_step(bt_ref, residual, direction, ocean_ref[...], coef_ref, 2, product_out)
    direction_out[...] = later
    scale = repeat_row(coef_ref[0:1], lane_blocks(residual.shape[1]))
    solution_out[...] = scale * search_ref[...] + direction + later
    nothing = jnp.zeros((1, residual.shape[1]), F32)
    residual = apply_operator(residual, later, diag_ref[...], east_face_ref[...], north_face_ref[...], nothing, nothing)
    residual_out[...] = residual
    blocks_product(bt_ref, residual, product_out)


FIRST_RES, FIRST_DIR, LAST_RES, LAST_DIR, LAST_FACE, SUMS, PACK_ROWS = 0, 1, 2, 3, 4, 5, 8


def closing_kernel(
    outer_ref, inner_ref, residual_ref, direction_ref, solution_ref, product_ref, diag_ref, east_face_ref, north_face_ref, ocean_ref, faces_ref, coef_ref, norms_ref, bt_ref,
    residual_out, solution_out, pack_out,
):
    west, east = halo_rows(inner_ref, outer_ref, 0, even_device())
    west, east = faces_ref[0:1] * west, faces_ref[1:2] * east
    residual = add_sides(residual_ref[...], west, east)
    keep, gain = (repeat_row(coef_ref[n : n + 1], lane_blocks(residual.shape[1])) for n in (2 * ITERS - 2, 2 * ITERS - 1))
    product = product_ref[...] + side_products(bt_ref, west, east)
    later = keep * direction_ref[...] + gain * (ocean_ref[...] * product)
    solution_out[...] = solution_ref[...] + later
    columns = residual.shape[0]
    sums = pack_out.at[SUMS : SUMS + 1]
    store_norm(sums, norms_ref, ITERS - 2, residual * residual)
    nothing = jnp.zeros_like(west)
    residual = apply_operator(residual, later, diag_ref[...], east_face_ref[...], north_face_ref[...], nothing, nothing)
    residual_out[...] = residual
    lon = lax.broadcasted_iota(jnp.int32, residual.shape, 0)
    inside = jnp.where((lon > 0) & (lon < columns - 1), residual, 0.0)
    sums[0:1, (ITERS - 1) * LANES : ITERS * LANES] = lane_partial(inside * inside)
    pack_out[FIRST_RES : FIRST_RES + 1] = residual[0:1]
    pack_out[FIRST_DIR : FIRST_DIR + 1] = later[0:1]
    pack_out[LAST_RES : LAST_RES + 1] = residual[columns - 1 :]
    pack_out[LAST_DIR : LAST_DIR + 1] = later[columns - 1 :]
    pack_out[LAST_FACE : LAST_FACE + 1] = faces_ref[1:2]
    pack_out[SUMS + 1 :] = jnp.zeros_like(pack_out[SUMS + 1 :])


def swap_order(size, radix):
    return (1,) if radix == 2 else (1, 2, 3) if size == 1 else (1, 3, 2)


def join_packs(size, radix, is_last, pack_ref, others, halo, packs):
    me = lax.axis_index("lon")
    mine = lax.rem(me // size, radix)
    packs[mine] = pack_ref[...]
    for s, other in zip(swap_order(size, radix), others):
        packs[mine ^ s] = other[...]

    def row(run, name):
        return packs[run % radix, name : name + 1, :]

    sums = functools.reduce(jnp.add, [row(run, SUMS) for run in range(radix)])
    total = None
    for run in range(radix if is_last else radix - 1):
        face = row(run, LAST_FACE)
        left = row(run, LAST_RES) + face * row(run + 1, FIRST_DIR)
        right = row(run + 1, FIRST_RES) + face * row(run, LAST_DIR)
        squares = lane_partial(left * left + right * right)
        total = squares if total is None else total + squares
    parts = [sums[:, i * LANES : (i + 1) * LANES] for i in range(sums.shape[1] // LANES)]
    parts[ITERS - 1] = parts[ITERS - 1] + total
    before = packs[lax.rem(mine + radix - 1, radix)][LAST_DIR : LAST_DIR + 1]
    after = packs[lax.rem(mine + 1, radix)][FIRST_DIR : FIRST_DIR + 1]
    place = lax.rem(me, size)
    west_now = place == 0
    east_now = place == size - 1
    if not is_last:
        west_now = west_now & (mine > 0)
        east_now = east_now & (mine < radix - 1)
    west, east = halo
    return parts, jnp.where(west_now, before, west), jnp.where(east_now, after, east)


def stage_kernel(size, radix, *refs):
    pack_ref, others, halo_ref = refs[0], refs[1:radix], refs[radix] if size > 1 else None
    pack_out, halo_out, packs = refs[-3:]
    nothing = jnp.zeros((1, pack_ref.shape[1]), F32)
    halo = (nothing, nothing) if halo_ref is None else (halo_ref[0:1], halo_ref[1:2])
    parts, west, east = join_packs(size, radix, False, pack_ref, others, halo, packs)
    pack_out[...] = packs[0]
    for name in (LAST_RES, LAST_DIR, LAST_FACE):
        pack_out[name : name + 1] = packs[radix - 1, name : name + 1, :]
    pack_out[SUMS : SUMS + 1] = jnp.concatenate(parts, axis=1)
    halo_out[0:1] = west
    halo_out[1:2] = east


def finish_kernel(size, radix, cells_all, *refs):
    pack_ref, others, halo_ref = refs[0], refs[1:radix], refs[radix]
    residual_ref, faces_ref, answer_ref = refs[radix + 1 : radix + 4]
    residual_out, answer_out, norms_out, packs = refs[radix + 4 :]
    parts, west, east = join_packs(size, radix, True, pack_ref, others, (halo_ref[0:1], halo_ref[1:2]), packs)
    answer_out[...] = answer_ref[...]
    residual = residual_ref[...]
    lon = lax.broadcasted_iota(jnp.int32, residual.shape, 0)
    residual = jnp.where(lon == 0, residual + faces_ref[0:1] * west, residual)
    residual = jnp.where(lon == residual.shape[0] - 1, residual + faces_ref[1:2] * east, residual)
    residual_out[...] = residual
    for k in range(ITERS):
        norms_out[k] = jnp.sum(parts[k]) / cells_all


def vmem():
    return pl.BlockSpec(memory_space=pltpu.VMEM)


def shape(*dims):
    return jax.ShapeDtypeStruct(dims, F32)


def smem():
    return pl.BlockSpec(memory_space=pltpu.SMEM)


def call(body, in_specs, outs, scratch, limit, cost=None, out_specs=None):
    return pl.pallas_call(
        body,
        in_specs=in_specs,
        out_specs=out_specs or [vmem()] * len(outs),
        out_shape=outs,
        scratch_shapes=scratch,
        compiler_params=pltpu.CompilerParams(vmem_limit_bytes=limit),
        cost_estimate=cost,
    )


def exchange(inner, outer):
    devices = lax.axis_size("lon")
    pairs = [(i, i ^ 1) for i in range(devices)]
    across = [(i, (i + 1 if i % 2 else i - 1) % devices) for i in range(devices)]
    return lax.ppermute(inner, "lon", pairs), lax.ppermute(outer, "lon", across)


def exchange_beyond(near, far):
    devices = lax.axis_size("lon")
    within = [(i, i ^ 2) for i in range(devices)]
    across = [(i, (i + 2 if i % 4 >= 2 else i - 2) % devices) for i in range(devices)]
    return lax.ppermute(near, "lon", within), lax.ppermute(far, "lon", across)


def swap_runs(pack, size, radix):
    devices = lax.axis_size("lon")
    return [
        lax.ppermute(pack, "lon", [(i, i ^ (s * size)) for i in range(devices)]) for s in swap_order(size, radix)
    ]


def on_device(
    right_side, east_coef, north_coef, surface_term, cell_mask, inverse_blocks, active_tiles, low_bound, high_bound
):
    columns, rows = right_side.shape
    tiles = inverse_blocks.shape[0]
    count = lane_blocks(rows)
    field = shape(columns, rows)
    row = shape(1, rows)
    two = shape(2, rows)
    bt_shape = shape(count, columns, LANES, LANES)
    (bt,) = call(
        transpose_kernel,
        [pl.BlockSpec(memory_space=pl.ANY)],
        [bt_shape],
        [pltpu.VMEM(inverse_blocks.shape, F32), pltpu.SemaphoreType.DMA((count,))],
        40 * MIB,
        pl.CostEstimate(flops=10**9, bytes_accessed=2 * inverse_blocks.size * 4, transcendentals=0),
    )(inverse_blocks)
    pair_shape = shape(PAIR_ROWS, rows)
    residual, search, diag, east_face, north_face, ocean, east_end, flow, inner, outer, near, far = call(
        first_kernel,
        [vmem()] * 7,
        [field, field, field, field, field, field, row, field, pair_shape, pair_shape, two, two],
        [],
        24 * MIB,
    )(active_tiles.reshape(-1, LANES), right_side, east_coef, north_coef, surface_term, cell_mask, bt)
    low_bound, high_bound, outer = lax.optimization_barrier((low_bound, high_bound, outer))
    inner, outer = exchange(inner, outer)
    near, far = exchange_beyond(near, far)
    work = pl.CostEstimate(flops=2 * bt.size, bytes_accessed=4 * bt.size, transcendentals=0)
    (product,) = call(product_kernel, [vmem()] * 2, [field], [], 24 * MIB, work)(bt, flow)
    residual, direction, diag, faces, norms, coef, inner, outer = call(
        second_kernel,
        [smem()] * 2 + [vmem()] * 14,
        [field, field, field, two, row, shape(SUBS, LANES), row, row],
        [],
        24 * MIB,
    )(
        low_bound, high_bound, far, outer, near, inner, residual, search, flow, product, diag, east_face, north_face,
        ocean, east_end, bt,
    )
    inner, outer = exchange(inner, outer)
    residual, direction, answer, product, norms = call(
        ahead_kernel,
        [vmem()] * 10,
        [field, field, field, field, row],
        [],
        24 * MIB,
        work,
    )(residual, direction, search, diag, east_face, north_face, ocean, coef, norms, bt)
    pack_shape = shape(PACK_ROWS, rows)
    residual, answer, pack = call(closing_kernel, [vmem()] * 14, [field, field, pack_shape], [], 24 * MIB)(
        outer, inner, residual, direction, answer, product, diag, east_face, north_face, ocean, faces, coef, norms, bt
    )
    devices = lax.axis_size("lon")
    size, halo = 1, []
    while True:
        radix = 4 if (devices // size) % 4 == 0 else 2
        others = swap_runs(pack, size, radix)
        packs = [pltpu.VMEM((radix, PACK_ROWS, rows), F32)]
        if size * radix == devices:
            break
        pack, *halo = call(
            functools.partial(stage_kernel, size, radix),
            [vmem()] * (radix + len(halo)),
            [pack_shape, two],
            packs,
            24 * MIB,
        )(pack, *others, *halo)
        size *= radix
    residual, answer, norms = call(
        functools.partial(finish_kernel, size, radix, float(columns * devices * rows)),
        [vmem()] * (radix + 4),
        [field, field, shape(ITERS)],
        packs,
        24 * MIB,
        out_specs=[vmem(), vmem(), smem()],
    )(pack, *others, *halo, residual, faces, answer)
    return answer, residual, norms


def solution(mesh):
    in_specs = (
        P(("member", "lon"), None),
        P("lon", None),
        P("lon", None),
        P("lon", None),
        P("lon", None),
        P("lon", None, None),
        P(),
        P(),
        P(),
    )
    out_specs = (P(("member", "lon"), None), P(("member", "lon"), None), P("member"))
    return jax.shard_map(on_device, mesh=mesh, in_specs=in_specs, out_specs=out_specs, check_vma=False)
```

```python
import functools

import jax
import jax.numpy as jnp
from jax import lax
from jax.experimental import pallas as pl
from jax.experimental.pallas import tpu as pltpu
from jax.sharding import PartitionSpec as P

ITERS = 4
LANES = 128
SUBS = 8
F32 = jnp.float32
MIB = 2**20


def lane_blocks(rows):
    return rows // LANES


def roll(x, shift, axis):
    return pltpu.roll(x, shift % x.shape[axis], axis)


def repeat_row(row, times):
    return jnp.concatenate([row] * times, axis=1)


def gather_index():
    lane = lax.broadcasted_iota(jnp.int32, (SUBS, LANES), 1)
    sub = lax.broadcasted_iota(jnp.int32, (SUBS, LANES), 0)
    return (lane // SUBS) * SUBS + sub


def expand(field, block, index):
    part = field[:, block * LANES : (block + 1) * LANES]
    rows = [
        jnp.take_along_axis(jnp.broadcast_to(part[a : a + 1], (SUBS, LANES)), index, axis=1)
        for a in range(part.shape[0])
    ]
    return jnp.concatenate(rows, axis=0)


def fold(parts):
    sub = lax.broadcasted_iota(jnp.int32, (SUBS, LANES), 0)
    half = SUBS // 2
    while half:
        upper = (sub & half) == 0
        parts = [
            jnp.where(upper, low, high) + jnp.where(upper, roll(low, -half, 0), roll(high, half, 0))
            for low, high in zip(parts[:half], parts[half:])
        ]
        half //= 2
    return parts[0]


def row_sums(product):
    return functools.reduce(jnp.add, [product[i : i + SUBS] for i in range(0, product.shape[0], SUBS)])


def blocks_product(bt_ref, field, out_ref):
    index = gather_index()
    columns, rows = field.shape
    for block in range(lane_blocks(rows)):
        spread = expand(field, block, index)
        for first in range(0, columns, SUBS):
            parts = [row_sums(bt_ref[block, a] * spread) for a in range(first, first + SUBS)]
            out_ref[first : first + SUBS, block * LANES : (block + 1) * LANES] = fold(parts)


def even_device():
    return lax.rem(lax.axis_index("lon"), 2) == 0


def store_edges(inner_ref, outer_ref, row, even, first, last):
    inner_ref[row : row + 1] = jnp.where(even, last, first)
    outer_ref[row : row + 1] = jnp.where(even, first, last)


def halo_rows(inner_ref, outer_ref, row, even):
    inner, outer = inner_ref[row : row + 1], outer_ref[row : row + 1]
    return jnp.where(even, outer, inner), jnp.where(even, inner, outer)


def low_device():
    return lax.rem(lax.axis_index("lon"), 4) < 2


def lane_partial(squares):
    total = jnp.sum(squares, axis=0, keepdims=True)
    parts = [total[:, i * LANES : (i + 1) * LANES] for i in range(total.shape[1] // LANES)]
    return functools.reduce(jnp.add, parts)


def tile_flags(active_ref, first, tiles):
    active = active_ref[...]
    before = jnp.sum((active < first).astype(jnp.int32))
    row = jnp.minimum(before // LANES, active_ref.shape[0] - 2)
    lane = lax.broadcasted_iota(jnp.int32, (LANES, tiles), 1) + first
    found = jnp.zeros((LANES, tiles), jnp.int32)
    for step in range(2):
        entries = jnp.broadcast_to(active_ref[pl.ds(row + step, 1), :], (LANES, LANES))
        found = found + (entries.T == lane).astype(jnp.int32)
    return (jnp.sum(found, axis=0, keepdims=True) > 0).astype(F32)


def transpose_kernel(blocks_hbm, bt_ref, raw, sems):
    count, columns = bt_ref.shape[:2]
    step = blocks_hbm.shape[0] // count

    def fetch(i):
        part = pl.ds(i * step, step)
        return pltpu.make_async_copy(blocks_hbm.at[part], raw.at[part], sems.at[i])

    for i in range(count):
        fetch(i).start()
    for i in range(count):
        fetch(i).wait()
        for a in range(columns):
            bt_ref[i, a] = raw[i * step : (i + 1) * step, a * SUBS : (a + 1) * SUBS, :].reshape(LANES, LANES).T


PAIR_SEARCH, PAIR_FLOW, PAIR_FACE, PAIR_BACK_SEARCH, PAIR_BACK_FACE, PAIR_OWN, PAIR_OPPOSITE, PAIR_ROWS = 0, 1, 2, 3, 4, 8, 16, 24


def edge_products(bt_ref, field):
    columns, rows = field.shape
    index = gather_index()
    first, last = [], []
    for block in range(lane_blocks(rows)):
        spread = expand(field, block, index)
        first.append(jnp.sum(bt_ref[block, 0] * spread, axis=0, keepdims=True))
        last.append(jnp.sum(bt_ref[block, columns - 1] * spread, axis=0, keepdims=True))
    return jnp.concatenate(first, axis=1), jnp.concatenate(last, axis=1)


def first_kernel(
    active_ref, right_ref, east_ref, north_ref, surface_ref, mask_ref, bt_ref,
    residual_ref, search_ref, diag_ref, east_face_ref, north_face_ref, ocean_ref, east_end_ref, flow_ref, inner_ref, outer_ref, near_ref, far_ref,
):
    columns, rows = right_ref.shape
    count = lane_blocks(rows)
    tiles = rows // SUBS
    even = even_device()
    flags = tile_flags(active_ref, lax.axis_index("lon") * tiles, tiles)
    right = right_ref[...] * mask_ref[...].astype(F32)
    blocks_product(bt_ref, right, search_ref)
    lane = lax.broadcasted_iota(jnp.int32, (SUBS, LANES), 1)
    spread = [
        jnp.take_along_axis(jnp.broadcast_to(flags, (SUBS, tiles)), i * (LANES // SUBS) + lane // SUBS, axis=1)
        for i in range(count)
    ]
    flag_lat = jnp.concatenate(spread, axis=1)[0:1]
    ocean = mask_ref[...].astype(F32) * flag_lat
    ocean_ref[...] = ocean
    lat = lax.broadcasted_iota(jnp.int32, (columns, rows), 1)
    lon = lax.broadcasted_iota(jnp.int32, (columns, rows), 0)
    east_ocean = east_ref[...] * ocean
    east_face = jnp.where(lon < columns - 1, east_ocean * roll(ocean, -1, 0), 0.0)
    north_face = jnp.where(lat < rows - 1, north_ref[...] * ocean * roll(ocean, -1, 1), 0.0)
    east_face_ref[...] = east_face
    north_face_ref[...] = north_face
    diag = surface_ref[...] * ocean + east_face + roll(east_face, 1, 0) + north_face + roll(north_face, 1, 1)
    diag_ref[...] = diag
    residual = right_ref[...] * ocean
    residual_ref[...] = residual
    east_end = east_ocean[columns - 1 :]
    east_end_ref[...] = east_end
    search = search_ref[...] * ocean
    search_ref[...] = search
    nothing = jnp.zeros_like(east_end)
    flow = apply_operator(jnp.zeros_like(search), -search, diag, east_face, north_face, nothing, nothing)
    flow_ref[...] = flow
    edges = edge_products(bt_ref, flow)
    fields = (
        (PAIR_SEARCH, search[0:1], search[columns - 1 :]),
        (PAIR_FLOW, edges[0] * ocean[0:1], edges[1] * ocean[columns - 1 :]),
        (PAIR_FACE, ocean[0:1], east_end),
        (PAIR_BACK_SEARCH, search[columns - 1 :], search[0:1]),
        (PAIR_BACK_FACE, east_end, ocean[0:1]),
    )
    for row, west, east in fields:
        store_edges(inner_ref, outer_ref, row, even, west, east)
    for ref, edge in ((inner_ref, jnp.where(even, columns - 1, 0)), (outer_ref, jnp.where(even, 0, columns - 1))):
        ref[len(fields) : SUBS] = jnp.zeros((SUBS - len(fields), rows), F32)
        for i in range(count):
            lanes = slice(i * LANES, (i + 1) * LANES)
            ref[PAIR_OWN : PAIR_OWN + SUBS, lanes] = bt_ref[i, edge, pl.ds(pl.multiple_of(edge * SUBS, SUBS), SUBS), :]
            back = columns - 1 - edge
            ref[PAIR_OPPOSITE : PAIR_OPPOSITE + SUBS, lanes] = bt_ref[i, edge, pl.ds(pl.multiple_of(back * SUBS, SUBS), SUBS), :]
    low = low_device()
    for row, west, east in ((0, search[0:1], search[columns - 1 :]), (1, ocean[0:1], east_end)):
        near_ref[row : row + 1] = jnp.where(low, east, west)
        far_ref[row : row + 1] = jnp.where(low, west, east)


def apply_operator(residual, direction, diag, east_face, north_face, west_term, east_term):
    flow = diag * direction
    flow = flow - east_face * roll(direction, -1, 0) - roll(east_face, 1, 0) * roll(direction, 1, 0)
    flow = flow - north_face * roll(direction, -1, 1) - roll(north_face, 1, 1) * roll(direction, 1, 1)
    lon = lax.broadcasted_iota(jnp.int32, residual.shape, 0)
    flow = jnp.where(lon == 0, flow - west_term, flow)
    flow = jnp.where(lon == residual.shape[0] - 1, flow - east_term, flow)
    return residual - flow


def search_step(bt_ref, residual, direction, ocean, coef_ref, k, search_ref):
    count = lane_blocks(residual.shape[1])
    blocks_product(bt_ref, residual, search_ref)
    keep = repeat_row(coef_ref[2 * k : 2 * k + 1], count)
    gain = repeat_row(coef_ref[2 * k + 1 : 2 * k + 2], count)
    return keep * direction + gain * (ocean * search_ref[...])


def store_coefficients(low_ref, high_ref, coef_ref):
    low = jnp.full((1, LANES), low_ref[0], F32)
    high = jnp.full((1, LANES), high_ref[0], F32)
    center = (high + low) / 2.0
    radius = (high - low) / 2.0
    ratio = center / radius
    weight_prev = 1.0 / ratio
    coef_ref[0:1] = 1.0 / center
    for k in range(1, ITERS):
        weight = 1.0 / (2.0 * ratio - weight_prev)
        coef_ref[2 * k : 2 * k + 1] = weight * weight_prev
        coef_ref[2 * k + 1 : 2 * k + 2] = 2.0 * weight / radius
        weight_prev = weight


def neighbour_direction(own, opposite, search, flow, own_push, opposite_push, coef_ref):
    rows = search.shape[1]
    count = lane_blocks(rows)
    index = gather_index()
    parts = []
    for block in range(count):
        lanes = slice(block * LANES, (block + 1) * LANES)
        product = own[:, lanes] * expand(own_push, block, index) + opposite[:, lanes] * expand(opposite_push, block, index)
        parts.append(jnp.sum(product, axis=0, keepdims=True))
    scale, keep, gain = (repeat_row(coef_ref[n : n + 1], count) for n in (0, 2, 3))
    return keep * (scale * search) + gain * (search - scale * flow + jnp.concatenate(parts, axis=1))


def side_products(bt_ref, first, last):
    count, columns = bt_ref.shape[:2]
    index = gather_index()
    blocks = []
    for block in range(count):
        west, east = expand(first, block, index), expand(last, block, index)
        parts = [bt_ref[block, a, :SUBS] * west + bt_ref[block, a, LANES - SUBS :] * east for a in range(columns)]
        rows = [fold(parts[a : a + SUBS]) for a in range(0, columns, SUBS)]
        blocks.append(jnp.concatenate(rows, axis=0))
    return jnp.concatenate(blocks, axis=1)


def add_sides(field, first, last):
    lon = lax.broadcasted_iota(jnp.int32, field.shape, 0)
    field = jnp.where(lon == 0, field + first, field)
    return jnp.where(lon == field.shape[0] - 1, field + last, field)


def product_kernel(bt_ref, field_ref, out_ref):
    blocks_product(bt_ref, field_ref[...], out_ref)


def second_kernel(
    low_ref, high_ref, far_ref, outer_ref, near_ref, inner_ref, residual_ref, search_ref, flow_ref, product_ref, diag_ref, east_face_ref, north_face_ref, ocean_ref, east_end_ref, bt_ref,
    residual_out, direction_out, diag_out, faces_out, norms_out, coef_out, inner_out, outer_out,
):
    store_coefficients(low_ref, high_ref, coef_out)
    ocean = ocean_ref[...]
    columns, rows = ocean.shape
    count = lane_blocks(rows)
    scale, keep, gain, keep_next, gain_next = (repeat_row(coef_out[n : n + 1], count) for n in (0, 2, 3, 4, 5))
    search = search_ref[...]
    even, low = even_device(), low_device()
    sides = [halo_rows(inner_ref, outer_ref, row, even) for row in range(PAIR_BACK_FACE + 1)]
    beyond = [
        (jnp.where(low, far, near), jnp.where(low, near, far))
        for near, far in ((near_ref[row : row + 1], far_ref[row : row + 1]) for row in range(2))
    ]
    here = (search[0:1], search[columns - 1 :])
    static = (ocean[0:1], east_end_ref[...])
    faces, pushes, later_halos = [], [], []
    for side in range(2):
        there, flow, face, back, back_face = (pair[side] for pair in sides)
        face = static[side] * face
        own_push = face * (scale * (here[side] - there))
        opposite_push = back_face * beyond[1][side] * (scale * (beyond[0][side] - back))
        from_inner = even if side == 1 else jnp.logical_not(even)
        own, opposite = (
            jnp.where(from_inner, inner_ref[row : row + SUBS], outer_ref[row : row + SUBS]) for row in (PAIR_OWN, PAIR_OPPOSITE)
        )
        faces.append(face)
        pushes.append(-own_push)
        later_halos.append(face * neighbour_direction(own, opposite, there, flow, own_push, opposite_push, coef_out))
    faces_out[0:1] = faces[0]
    faces_out[1:2] = faces[1]
    diag = add_sides(diag_ref[...], faces[0], faces[1])
    diag_out[...] = diag
    residual = add_sides(residual_ref[...] - scale * flow_ref[...], pushes[0], pushes[1])
    norms_out[...] = jnp.zeros_like(norms_out)
    norms_out[0:1, 0:LANES] = lane_partial(residual * residual)
    product = side_products(bt_ref, pushes[0], pushes[1]) - scale * product_ref[...]
    direction = keep * (scale * search) + gain * (search + ocean * product)
    direction_out[...] = direction
    residual = apply_operator(residual, direction, diag, east_face_ref[...], north_face_ref[...], later_halos[0], later_halos[1])
    residual_out[...] = residual
    first, last = edge_products(bt_ref, residual)
    store_edges(
        inner_out, outer_out, 0, even,
        keep_next * direction[0:1] + gain_next * (ocean[0:1] * first),
        keep_next * direction[columns - 1 :] + gain_next * (ocean[columns - 1 :] * last),
    )


def store_norm(norms_out, norms_ref, k, squares):
    norms_out[...] = norms_ref[...]
    norms_out[0:1, k * LANES : (k + 1) * LANES] = lane_partial(squares)


def ahead_kernel(
    residual_ref, direction_ref, search_ref, diag_ref, east_face_ref, north_face_ref, ocean_ref, coef_ref, norms_ref, bt_ref,
    residual_out, direction_out, solution_out, product_out, norms_out,
):
    residual = residual_ref[...]
    direction = direction_ref[...]
    store_norm(norms_out, norms_ref, 1, residual * residual)
    later = search_step(bt_ref, residual, direction, ocean_ref[...], coef_ref, 2, product_out)
    direction_out[...] = later
    scale = repeat_row(coef_ref[0:1], lane_blocks(residual.shape[1]))
    solution_out[...] = scale * search_ref[...] + direction + later
    nothing = jnp.zeros((1, residual.shape[1]), F32)
    residual = apply_operator(residual, later, diag_ref[...], east_face_ref[...], north_face_ref[...], nothing, nothing)
    residual_out[...] = residual
    blocks_product(bt_ref, residual, product_out)


FIRST_RES, FIRST_PUSH, LAST_RES, LAST_PUSH, SUMS, PACK_PARTS = 0, 1, 2, 3, 4, 5


def store_row(pack_ref, part, row):
    for i in range(pack_ref.shape[1]):
        pack_ref[part, i : i + 1, :] = row[:, i * LANES : (i + 1) * LANES]


def closing_kernel(
    outer_ref, inner_ref, residual_ref, direction_ref, solution_ref, product_ref, diag_ref, east_face_ref, north_face_ref, ocean_ref, faces_ref, coef_ref, norms_ref, bt_ref,
    residual_out, solution_out, pack_out,
):
    west, east = halo_rows(inner_ref, outer_ref, 0, even_device())
    west, east = faces_ref[0:1] * west, faces_ref[1:2] * east
    residual = add_sides(residual_ref[...], west, east)
    keep, gain = (repeat_row(coef_ref[n : n + 1], lane_blocks(residual.shape[1])) for n in (2 * ITERS - 2, 2 * ITERS - 1))
    product = product_ref[...] + side_products(bt_ref, west, east)
    later = keep * direction_ref[...] + gain * (ocean_ref[...] * product)
    solution_out[...] = solution_ref[...] + later
    columns = residual.shape[0]
    pack_out[SUMS] = jnp.zeros(pack_out.shape[1:], F32)
    for k in range(ITERS - 2):
        pack_out[SUMS, k : k + 1, :] = norms_ref[0:1, k * LANES : (k + 1) * LANES]
    pack_out[SUMS, ITERS - 2 : ITERS - 1, :] = lane_partial(residual * residual)
    nothing = jnp.zeros_like(west)
    residual = apply_operator(residual, later, diag_ref[...], east_face_ref[...], north_face_ref[...], nothing, nothing)
    residual_out[...] = residual
    lon = lax.broadcasted_iota(jnp.int32, residual.shape, 0)
    inside = jnp.where((lon > 0) & (lon < columns - 1), residual, 0.0)
    pack_out[SUMS, ITERS - 1 : ITERS, :] = lane_partial(inside * inside)
    store_row(pack_out, FIRST_RES, residual[0:1])
    store_row(pack_out, FIRST_PUSH, faces_ref[0:1] * later[0:1])
    store_row(pack_out, LAST_RES, residual[columns - 1 :])
    store_row(pack_out, LAST_PUSH, faces_ref[1:2] * later[columns - 1 :])


def swap_order(size, radix):
    return (1,) if radix == 2 else (1, 2, 3) if size == 1 else (1, 3, 2)


def join_packs(size, radix, is_last, pack_ref, others, halo, packs):
    me = lax.axis_index("lon")
    mine = lax.rem(me // size, radix)
    packs[mine] = pack_ref[...]
    for s, other in zip(swap_order(size, radix), others):
        packs[mine ^ s] = other[...]

    def part(run, name):
        return packs[run % radix, name]

    sums = functools.reduce(jnp.add, [part(run, SUMS) for run in range(radix)])
    squares = []
    for run in range(radix if is_last else radix - 1):
        left = part(run, LAST_RES) + part(run + 1, FIRST_PUSH)
        right = part(run + 1, FIRST_RES) + part(run, LAST_PUSH)
        squares.append(left * left + right * right)
    total = jnp.sum(functools.reduce(jnp.add, squares), axis=0, keepdims=True)
    sub = lax.broadcasted_iota(jnp.int32, sums.shape, 0)
    sums = jnp.where(sub == ITERS - 1, sums + total, sums)
    before = packs[lax.rem(mine + radix - 1, radix), LAST_PUSH]
    after = packs[lax.rem(mine + 1, radix), FIRST_PUSH]
    place = lax.rem(me, size)
    west_now = place == 0
    east_now = place == size - 1
    if not is_last:
        west_now = west_now & (mine > 0)
        east_now = east_now & (mine < radix - 1)
    west, east = halo
    return sums, jnp.where(west_now, before, west), jnp.where(east_now, after, east)


def stage_kernel(size, radix, *refs):
    pack_ref, others, halo_ref = refs[0], refs[1:radix], refs[radix] if size > 1 else None
    pack_out, halo_out, packs = refs[-3:]
    nothing = jnp.zeros(pack_ref.shape[1:], F32)
    halo = (nothing, nothing) if halo_ref is None else (halo_ref[0], halo_ref[1])
    sums, west, east = join_packs(size, radix, False, pack_ref, others, halo, packs)
    pack_out[...] = packs[0]
    for name in (LAST_RES, LAST_PUSH):
        pack_out[name] = packs[radix - 1, name]
    pack_out[SUMS] = sums
    halo_out[0] = west
    halo_out[1] = east


def finish_kernel(size, radix, cells_all, *refs):
    pack_ref, others, halo_ref = refs[0], refs[1:radix], refs[radix]
    residual_ref, answer_ref = refs[radix + 1 : radix + 3]
    residual_out, answer_out, norms_out, packs = refs[radix + 3 :]
    sums, *pushes = join_packs(size, radix, True, pack_ref, others, (halo_ref[0], halo_ref[1]), packs)
    answer_out[...] = answer_ref[...]
    west, east = (
        jnp.concatenate([push[i : i + 1] for i in range(push.shape[0])], axis=1) for push in pushes
    )
    residual_out[...] = add_sides(residual_ref[...], west, east)
    for k in range(ITERS):
        norms_out[k] = jnp.sum(sums[k : k + 1]) / cells_all


def vmem():
    return pl.BlockSpec(memory_space=pltpu.VMEM)


def shape(*dims):
    return jax.ShapeDtypeStruct(dims, F32)


def smem():
    return pl.BlockSpec(memory_space=pltpu.SMEM)


def call(body, in_specs, outs, scratch, limit, cost=None, out_specs=None):
    return pl.pallas_call(
        body,
        in_specs=in_specs,
        out_specs=out_specs or [vmem()] * len(outs),
        out_shape=outs,
        scratch_shapes=scratch,
        compiler_params=pltpu.CompilerParams(vmem_limit_bytes=limit),
        cost_estimate=cost,
    )


def exchange(inner, outer):
    devices = lax.axis_size("lon")
    pairs = [(i, i ^ 1) for i in range(devices)]
    across = [(i, (i + 1 if i % 2 else i - 1) % devices) for i in range(devices)]
    return lax.ppermute(inner, "lon", pairs), lax.ppermute(outer, "lon", across)


def exchange_beyond(near, far):
    devices = lax.axis_size("lon")
    within = [(i, i ^ 2) for i in range(devices)]
    across = [(i, (i + 2 if i % 4 >= 2 else i - 2) % devices) for i in range(devices)]
    return lax.ppermute(near, "lon", within), lax.ppermute(far, "lon", across)


def swap_runs(pack, size, radix):
    devices = lax.axis_size("lon")
    return [
        lax.ppermute(pack, "lon", [(i, i ^ (s * size)) for i in range(devices)]) for s in swap_order(size, radix)
    ]


def on_device(
    right_side, east_coef, north_coef, surface_term, cell_mask, inverse_blocks, active_tiles, low_bound, high_bound
):
    columns, rows = right_side.shape
    tiles = inverse_blocks.shape[0]
    count = lane_blocks(rows)
    field = shape(columns, rows)
    row = shape(1, rows)
    two = shape(2, rows)
    bt_shape = shape(count, columns, LANES, LANES)
    (bt,) = call(
        transpose_kernel,
        [pl.BlockSpec(memory_space=pl.ANY)],
        [bt_shape],
        [pltpu.VMEM(inverse_blocks.shape, F32), pltpu.SemaphoreType.DMA((count,))],
        40 * MIB,
        pl.CostEstimate(flops=10**9, bytes_accessed=2 * inverse_blocks.size * 4, transcendentals=0),
    )(inverse_blocks)
    pair_shape = shape(PAIR_ROWS, rows)
    residual, search, diag, east_face, north_face, ocean, east_end, flow, inner, outer, near, far = call(
        first_kernel,
        [vmem()] * 7,
        [field, field, field, field, field, field, row, field, pair_shape, pair_shape, two, two],
        [],
        24 * MIB,
    )(active_tiles.reshape(-1, LANES), right_side, east_coef, north_coef, surface_term, cell_mask, bt)
    low_bound, high_bound, outer = lax.optimization_barrier((low_bound, high_bound, outer))
    inner, outer = exchange(inner, outer)
    near, far = exchange_beyond(near, far)
    work = pl.CostEstimate(flops=2 * bt.size, bytes_accessed=4 * bt.size, transcendentals=0)
    (product,) = call(product_kernel, [vmem()] * 2, [field], [], 24 * MIB, work)(bt, flow)
    residual, direction, diag, faces, norms, coef, inner, outer = call(
        second_kernel,
        [smem()] * 2 + [vmem()] * 14,
        [field, field, field, two, row, shape(SUBS, LANES), row, row],
        [],
        24 * MIB,
    )(
        low_bound, high_bound, far, outer, near, inner, residual, search, flow, product, diag, east_face, north_face,
        ocean, east_end, bt,
    )
    inner, outer = exchange(inner, outer)
    residual, direction, answer, product, norms = call(
        ahead_kernel,
        [vmem()] * 10,
        [field, field, field, field, row],
        [],
        24 * MIB,
        work,
    )(residual, direction, search, diag, east_face, north_face, ocean, coef, norms, bt)
    pack_shape = shape(PACK_PARTS, count, LANES)
    residual, answer, pack = call(closing_kernel, [vmem()] * 14, [field, field, pack_shape], [], 24 * MIB)(
        outer, inner, residual, direction, answer, product, diag, east_face, north_face, ocean, faces, coef, norms, bt
    )
    devices = lax.axis_size("lon")
    size, halo = 1, []
    while True:
        radix = 4 if (devices // size) % 4 == 0 else 2
        others = swap_runs(pack, size, radix)
        packs = [pltpu.VMEM((radix, PACK_PARTS, count, LANES), F32)]
        if size * radix == devices:
            break
        pack, *halo = call(
            functools.partial(stage_kernel, size, radix),
            [vmem()] * (radix + len(halo)),
            [pack_shape, shape(2, count, LANES)],
            packs,
            24 * MIB,
        )(pack, *others, *halo)
        size *= radix
    residual, answer, norms = call(
        functools.partial(finish_kernel, size, radix, float(columns * devices * rows)),
        [vmem()] * (radix + 3),
        [field, field, shape(ITERS)],
        packs,
        24 * MIB,
        out_specs=[vmem(), vmem(), smem()],
    )(pack, *others, *halo, residual, answer)
    return answer, residual, norms


def solution(mesh):
    in_specs = (
        P(("member", "lon"), None),
        P("lon", None),
        P("lon", None),
        P("lon", None),
        P("lon", None),
        P("lon", None, None),
        P(),
        P(),
        P(),
    )
    out_specs = (P(("member", "lon"), None), P(("member", "lon"), None), P("member"))
    return jax.shard_map(on_device, mesh=mesh, in_specs=in_specs, out_specs=out_specs, check_vma=False)
```

```python
import functools

import jax
import jax.numpy as jnp
from jax import lax
from jax.experimental import pallas as pl
from jax.experimental.pallas import tpu as pltpu
from jax.sharding import PartitionSpec as P

ITERS = 4
LANES = 128
SUBS = 8
F32 = jnp.float32
MIB = 2**20


def lane_blocks(rows):
    return rows // LANES


def roll(x, shift, axis):
    return pltpu.roll(x, shift % x.shape[axis], axis)


def repeat_row(row, times):
    return jnp.concatenate([row] * times, axis=1)


def gather_index():
    lane = lax.broadcasted_iota(jnp.int32, (SUBS, LANES), 1)
    sub = lax.broadcasted_iota(jnp.int32, (SUBS, LANES), 0)
    return (lane // SUBS) * SUBS + sub


def expand(field, block, index):
    part = field[:, block * LANES : (block + 1) * LANES]
    rows = [
        jnp.take_along_axis(jnp.broadcast_to(part[a : a + 1], (SUBS, LANES)), index, axis=1)
        for a in range(part.shape[0])
    ]
    return jnp.concatenate(rows, axis=0)


def fold(parts):
    sub = lax.broadcasted_iota(jnp.int32, (SUBS, LANES), 0)
    half = SUBS // 2
    while half:
        upper = (sub & half) == 0
        parts = [
            jnp.where(upper, low, high) + jnp.where(upper, roll(low, -half, 0), roll(high, half, 0))
            for low, high in zip(parts[:half], parts[half:])
        ]
        half //= 2
    return parts[0]


def row_sums(product):
    return functools.reduce(jnp.add, [product[i : i + SUBS] for i in range(0, product.shape[0], SUBS)])


def blocks_product(bt_ref, field, out_ref):
    index = gather_index()
    columns, rows = field.shape
    for block in range(lane_blocks(rows)):
        spread = expand(field, block, index)
        for first in range(0, columns, SUBS):
            parts = [row_sums(bt_ref[block, a] * spread) for a in range(first, first + SUBS)]
            out_ref[first : first + SUBS, block * LANES : (block + 1) * LANES] = fold(parts)


def even_device():
    return lax.rem(lax.axis_index("lon"), 2) == 0


def store_edges(inner_ref, outer_ref, row, even, first, last):
    inner_ref[row : row + 1] = jnp.where(even, last, first)
    outer_ref[row : row + 1] = jnp.where(even, first, last)


def halo_rows(inner_ref, outer_ref, row, even):
    inner, outer = inner_ref[row : row + 1], outer_ref[row : row + 1]
    return jnp.where(even, outer, inner), jnp.where(even, inner, outer)


def low_device():
    return lax.rem(lax.axis_index("lon"), 4) < 2


def lane_partial(squares):
    total = jnp.sum(squares, axis=0, keepdims=True)
    parts = [total[:, i * LANES : (i + 1) * LANES] for i in range(total.shape[1] // LANES)]
    return functools.reduce(jnp.add, parts)


def tile_flags(active_ref, first, tiles):
    active = active_ref[...]
    before = jnp.sum((active < first).astype(jnp.int32))
    row = jnp.minimum(before // LANES, active_ref.shape[0] - 2)
    lane = lax.broadcasted_iota(jnp.int32, (LANES, tiles), 1) + first
    found = jnp.zeros((LANES, tiles), jnp.int32)
    for step in range(2):
        entries = jnp.broadcast_to(active_ref[pl.ds(row + step, 1), :], (LANES, LANES))
        found = found + (entries.T == lane).astype(jnp.int32)
    return (jnp.sum(found, axis=0, keepdims=True) > 0).astype(F32)


def transpose_kernel(blocks_hbm, bt_ref, raw, sems):
    count, columns = bt_ref.shape[:2]
    step = blocks_hbm.shape[0] // count

    def fetch(i):
        part = pl.ds(i * step, step)
        return pltpu.make_async_copy(blocks_hbm.at[part], raw.at[part], sems.at[i])

    for i in range(count):
        fetch(i).start()
    for i in range(count):
        fetch(i).wait()
        for a in range(columns):
            bt_ref[i, a] = raw[i * step : (i + 1) * step, a * SUBS : (a + 1) * SUBS, :].reshape(LANES, LANES).T


PAIR_SEARCH, PAIR_FLOW, PAIR_FACE, PAIR_BACK_SEARCH, PAIR_BACK_FACE, PAIR_OWN, PAIR_OPPOSITE, PAIR_ROWS = 0, 1, 2, 3, 4, 8, 16, 24


def edge_products(bt_ref, field):
    columns, rows = field.shape
    index = gather_index()
    first, last = [], []
    for block in range(lane_blocks(rows)):
        spread = expand(field, block, index)
        first.append(jnp.sum(bt_ref[block, 0] * spread, axis=0, keepdims=True))
        last.append(jnp.sum(bt_ref[block, columns - 1] * spread, axis=0, keepdims=True))
    return jnp.concatenate(first, axis=1), jnp.concatenate(last, axis=1)


def first_kernel(
    active_ref, right_ref, east_ref, north_ref, surface_ref, mask_ref, bt_ref,
    residual_ref, search_ref, diag_ref, east_face_ref, north_face_ref, ocean_ref, east_end_ref, flow_ref, inner_ref, outer_ref, near_ref, far_ref,
):
    columns, rows = right_ref.shape
    count = lane_blocks(rows)
    tiles = rows // SUBS
    even = even_device()
    flags = tile_flags(active_ref, lax.axis_index("lon") * tiles, tiles)
    right = right_ref[...] * mask_ref[...].astype(F32)
    blocks_product(bt_ref, right, search_ref)
    lane = lax.broadcasted_iota(jnp.int32, (SUBS, LANES), 1)
    spread = [
        jnp.take_along_axis(jnp.broadcast_to(flags, (SUBS, tiles)), i * (LANES // SUBS) + lane // SUBS, axis=1)
        for i in range(count)
    ]
    flag_lat = jnp.concatenate(spread, axis=1)[0:1]
    ocean = mask_ref[...].astype(F32) * flag_lat
    ocean_ref[...] = ocean
    lat = lax.broadcasted_iota(jnp.int32, (columns, rows), 1)
    lon = lax.broadcasted_iota(jnp.int32, (columns, rows), 0)
    east_ocean = east_ref[...] * ocean
    east_face = jnp.where(lon < columns - 1, east_ocean * roll(ocean, -1, 0), 0.0)
    north_face = jnp.where(lat < rows - 1, north_ref[...] * ocean * roll(ocean, -1, 1), 0.0)
    east_face_ref[...] = east_face
    north_face_ref[...] = north_face
    diag = surface_ref[...] * ocean + east_face + roll(east_face, 1, 0) + north_face + roll(north_face, 1, 1)
    diag_ref[...] = diag
    residual = right_ref[...] * ocean
    residual_ref[...] = residual
    east_end = east_ocean[columns - 1 :]
    east_end_ref[...] = east_end
    search = search_ref[...] * ocean
    search_ref[...] = search
    nothing = jnp.zeros_like(east_end)
    flow = apply_operator(jnp.zeros_like(search), -search, diag, east_face, north_face, nothing, nothing)
    flow_ref[...] = flow
    edges = edge_products(bt_ref, flow)
    fields = (
        (PAIR_SEARCH, search[0:1], search[columns - 1 :]),
        (PAIR_FLOW, edges[0] * ocean[0:1], edges[1] * ocean[columns - 1 :]),
        (PAIR_FACE, ocean[0:1], east_end),
        (PAIR_BACK_SEARCH, search[columns - 1 :], search[0:1]),
        (PAIR_BACK_FACE, east_end, ocean[0:1]),
    )
    for row, west, east in fields:
        store_edges(inner_ref, outer_ref, row, even, west, east)
    for ref, edge in ((inner_ref, jnp.where(even, columns - 1, 0)), (outer_ref, jnp.where(even, 0, columns - 1))):
        ref[len(fields) : SUBS] = jnp.zeros((SUBS - len(fields), rows), F32)
        for i in range(count):
            lanes = slice(i * LANES, (i + 1) * LANES)
            ref[PAIR_OWN : PAIR_OWN + SUBS, lanes] = bt_ref[i, edge, pl.ds(pl.multiple_of(edge * SUBS, SUBS), SUBS), :]
            back = columns - 1 - edge
            ref[PAIR_OPPOSITE : PAIR_OPPOSITE + SUBS, lanes] = bt_ref[i, edge, pl.ds(pl.multiple_of(back * SUBS, SUBS), SUBS), :]
    low = low_device()
    for row, west, east in ((0, search[0:1], search[columns - 1 :]), (1, ocean[0:1], east_end)):
        near_ref[row : row + 1] = jnp.where(low, east, west)
        far_ref[row : row + 1] = jnp.where(low, west, east)


def apply_operator(residual, direction, diag, east_face, north_face, west_term, east_term):
    flow = diag * direction
    flow = flow - east_face * roll(direction, -1, 0) - roll(east_face, 1, 0) * roll(direction, 1, 0)
    flow = flow - north_face * roll(direction, -1, 1) - roll(north_face, 1, 1) * roll(direction, 1, 1)
    lon = lax.broadcasted_iota(jnp.int32, residual.shape, 0)
    flow = jnp.where(lon == 0, flow - west_term, flow)
    flow = jnp.where(lon == residual.shape[0] - 1, flow - east_term, flow)
    return residual - flow


def search_step(bt_ref, residual, direction, ocean, coef_ref, k, search_ref):
    count = lane_blocks(residual.shape[1])
    blocks_product(bt_ref, residual, search_ref)
    keep = repeat_row(coef_ref[2 * k : 2 * k + 1], count)
    gain = repeat_row(coef_ref[2 * k + 1 : 2 * k + 2], count)
    return keep * direction + gain * (ocean * search_ref[...])


def store_coefficients(low_ref, high_ref, coef_ref):
    low = jnp.full((1, LANES), low_ref[0], F32)
    high = jnp.full((1, LANES), high_ref[0], F32)
    center = (high + low) / 2.0
    radius = (high - low) / 2.0
    ratio = center / radius
    weight_prev = 1.0 / ratio
    coef_ref[0:1] = 1.0 / center
    for k in range(1, ITERS):
        weight = 1.0 / (2.0 * ratio - weight_prev)
        coef_ref[2 * k : 2 * k + 1] = weight * weight_prev
        coef_ref[2 * k + 1 : 2 * k + 2] = 2.0 * weight / radius
        weight_prev = weight


def neighbour_direction(own, opposite, search, flow, own_push, opposite_push, coef_ref):
    rows = search.shape[1]
    count = lane_blocks(rows)
    index = gather_index()
    parts = []
    for block in range(count):
        lanes = slice(block * LANES, (block + 1) * LANES)
        product = own[:, lanes] * expand(own_push, block, index) + opposite[:, lanes] * expand(opposite_push, block, index)
        parts.append(jnp.sum(product, axis=0, keepdims=True))
    scale, keep, gain = (repeat_row(coef_ref[n : n + 1], count) for n in (0, 2, 3))
    return keep * (scale * search) + gain * (search - scale * flow + jnp.concatenate(parts, axis=1))


def side_products(bt_ref, first, last):
    count, columns = bt_ref.shape[:2]
    index = gather_index()
    blocks = []
    for block in range(count):
        west, east = expand(first, block, index), expand(last, block, index)
        parts = [bt_ref[block, a, :SUBS] * west + bt_ref[block, a, LANES - SUBS :] * east for a in range(columns)]
        rows = [fold(parts[a : a + SUBS]) for a in range(0, columns, SUBS)]
        blocks.append(jnp.concatenate(rows, axis=0))
    return jnp.concatenate(blocks, axis=1)


def add_sides(field, first, last):
    lon = lax.broadcasted_iota(jnp.int32, field.shape, 0)
    field = jnp.where(lon == 0, field + first, field)
    return jnp.where(lon == field.shape[0] - 1, field + last, field)


def product_kernel(bt_ref, field_ref, out_ref):
    blocks_product(bt_ref, field_ref[...], out_ref)


def second_kernel(
    low_ref, high_ref, far_ref, outer_ref, near_ref, inner_ref, residual_ref, search_ref, flow_ref, product_ref, diag_ref, east_face_ref, north_face_ref, ocean_ref, east_end_ref, bt_ref,
    residual_out, direction_out, diag_out, faces_out, norms_out, coef_out, inner_out, outer_out,
):
    store_coefficients(low_ref, high_ref, coef_out)
    ocean = ocean_ref[...]
    columns, rows = ocean.shape
    count = lane_blocks(rows)
    scale, keep, gain, keep_next, gain_next = (repeat_row(coef_out[n : n + 1], count) for n in (0, 2, 3, 4, 5))
    search = search_ref[...]
    even, low = even_device(), low_device()
    sides = [halo_rows(inner_ref, outer_ref, row, even) for row in range(PAIR_BACK_FACE + 1)]
    beyond = [
        (jnp.where(low, far, near), jnp.where(low, near, far))
        for near, far in ((near_ref[row : row + 1], far_ref[row : row + 1]) for row in range(2))
    ]
    here = (search[0:1], search[columns - 1 :])
    static = (ocean[0:1], east_end_ref[...])
    faces, pushes, later_halos = [], [], []
    for side in range(2):
        there, flow, face, back, back_face = (pair[side] for pair in sides)
        face = static[side] * face
        own_push = face * (scale * (here[side] - there))
        opposite_push = back_face * beyond[1][side] * (scale * (beyond[0][side] - back))
        from_inner = even if side == 1 else jnp.logical_not(even)
        own, opposite = (
            jnp.where(from_inner, inner_ref[row : row + SUBS], outer_ref[row : row + SUBS]) for row in (PAIR_OWN, PAIR_OPPOSITE)
        )
        faces.append(face)
        pushes.append(-own_push)
        later_halos.append(face * neighbour_direction(own, opposite, there, flow, own_push, opposite_push, coef_out))
    faces_out[0:1] = faces[0]
    faces_out[1:2] = faces[1]
    diag = add_sides(diag_ref[...], faces[0], faces[1])
    diag_out[...] = diag
    residual = add_sides(residual_ref[...] - scale * flow_ref[...], pushes[0], pushes[1])
    norms_out[...] = jnp.zeros_like(norms_out)
    norms_out[0:1, 0:LANES] = lane_partial(residual * residual)
    product = side_products(bt_ref, pushes[0], pushes[1]) - scale * product_ref[...]
    direction = keep * (scale * search) + gain * (search + ocean * product)
    direction_out[...] = direction
    residual = apply_operator(residual, direction, diag, east_face_ref[...], north_face_ref[...], later_halos[0], later_halos[1])
    residual_out[...] = residual
    first, last = edge_products(bt_ref, residual)
    store_edges(
        inner_out, outer_out, 0, even,
        keep_next * direction[0:1] + gain_next * (ocean[0:1] * first),
        keep_next * direction[columns - 1 :] + gain_next * (ocean[columns - 1 :] * last),
    )


def store_norm(norms_out, norms_ref, k, squares):
    norms_out[...] = norms_ref[...]
    norms_out[0:1, k * LANES : (k + 1) * LANES] = lane_partial(squares)


def ahead_kernel(
    residual_ref, direction_ref, search_ref, diag_ref, east_face_ref, north_face_ref, ocean_ref, coef_ref, norms_ref, bt_ref,
    residual_out, direction_out, solution_out, product_out, norms_out,
):
    residual = residual_ref[...]
    direction = direction_ref[...]
    store_norm(norms_out, norms_ref, 1, residual * residual)
    later = search_step(bt_ref, residual, direction, ocean_ref[...], coef_ref, 2, product_out)
    direction_out[...] = later
    scale = repeat_row(coef_ref[0:1], lane_blocks(residual.shape[1]))
    solution_out[...] = scale * search_ref[...] + direction + later
    nothing = jnp.zeros((1, residual.shape[1]), F32)
    residual = apply_operator(residual, later, diag_ref[...], east_face_ref[...], north_face_ref[...], nothing, nothing)
    residual_out[...] = residual
    blocks_product(bt_ref, residual, product_out)


FIRST_RES, FIRST_PUSH, LAST_RES, LAST_PUSH, SUMS, PACK_PARTS = 0, 1, 2, 3, 4, 5


def store_row(pack_ref, part, row):
    for i in range(pack_ref.shape[1]):
        pack_ref[part, i : i + 1, :] = row[:, i * LANES : (i + 1) * LANES]


def closing_kernel(
    outer_ref, inner_ref, residual_ref, direction_ref, solution_ref, product_ref, diag_ref, east_face_ref, north_face_ref, ocean_ref, faces_ref, coef_ref, norms_ref, bt_ref,
    residual_out, solution_out, pack_out,
):
    west, east = halo_rows(inner_ref, outer_ref, 0, even_device())
    west, east = faces_ref[0:1] * west, faces_ref[1:2] * east
    residual = add_sides(residual_ref[...], west, east)
    keep, gain = (repeat_row(coef_ref[n : n + 1], lane_blocks(residual.shape[1])) for n in (2 * ITERS - 2, 2 * ITERS - 1))
    product = product_ref[...] + side_products(bt_ref, west, east)
    later = keep * direction_ref[...] + gain * (ocean_ref[...] * product)
    solution_out[...] = solution_ref[...] + later
    columns = residual.shape[0]
    pack_out[SUMS] = jnp.zeros(pack_out.shape[1:], F32)
    for k in range(ITERS - 2):
        pack_out[SUMS, k : k + 1, :] = norms_ref[0:1, k * LANES : (k + 1) * LANES]
    pack_out[SUMS, ITERS - 2 : ITERS - 1, :] = lane_partial(residual * residual)
    nothing = jnp.zeros_like(west)
    residual = apply_operator(residual, later, diag_ref[...], east_face_ref[...], north_face_ref[...], nothing, nothing)
    residual_out[...] = residual
    lon = lax.broadcasted_iota(jnp.int32, residual.shape, 0)
    inside = jnp.where((lon > 0) & (lon < columns - 1), residual, 0.0)
    pack_out[SUMS, ITERS - 1 : ITERS, :] = lane_partial(inside * inside)
    store_row(pack_out, FIRST_RES, residual[0:1])
    store_row(pack_out, FIRST_PUSH, faces_ref[0:1] * later[0:1])
    store_row(pack_out, LAST_RES, residual[columns - 1 :])
    store_row(pack_out, LAST_PUSH, faces_ref[1:2] * later[columns - 1 :])


def swap_order(size, radix):
    return (1,) if radix == 2 else (1, 2, 3) if size == 1 else (1, 3, 2)


def join_packs(size, radix, is_last, pack_ref, others, halo, packs):
    me = lax.axis_index("lon")
    mine = lax.rem(me // size, radix)
    packs[mine] = pack_ref[...]
    for s, other in zip(swap_order(size, radix), others):
        packs[mine ^ s] = other[...]

    def part(run, name):
        return packs[run % radix, name]

    sums = functools.reduce(jnp.add, [part(run, SUMS) for run in range(radix)])
    squares = []
    for run in range(radix if is_last else radix - 1):
        left = part(run, LAST_RES) + part(run + 1, FIRST_PUSH)
        right = part(run + 1, FIRST_RES) + part(run, LAST_PUSH)
        squares.append(left * left + right * right)
    total = jnp.sum(functools.reduce(jnp.add, squares), axis=0, keepdims=True)
    sub = lax.broadcasted_iota(jnp.int32, sums.shape, 0)
    sums = jnp.where(sub == ITERS - 1, sums + total, sums)
    before = packs[lax.rem(mine + radix - 1, radix), LAST_PUSH]
    after = packs[lax.rem(mine + 1, radix), FIRST_PUSH]
    place = lax.rem(me, size)
    west_now = place == 0
    east_now = place == size - 1
    if not is_last:
        west_now = west_now & (mine > 0)
        east_now = east_now & (mine < radix - 1)
    west, east = halo
    return sums, jnp.where(west_now, before, west), jnp.where(east_now, after, east)


def stage_kernel(size, radix, *refs):
    pack_ref, others, halo_ref = refs[0], refs[1:radix], refs[radix] if size > 1 else None
    pack_out, halo_out, packs = refs[-3:]
    nothing = jnp.zeros(pack_ref.shape[1:], F32)
    halo = (nothing, nothing) if halo_ref is None else (halo_ref[0], halo_ref[1])
    sums, west, east = join_packs(size, radix, False, pack_ref, others, halo, packs)
    pack_out[...] = packs[0]
    for name in (LAST_RES, LAST_PUSH):
        pack_out[name] = packs[radix - 1, name]
    pack_out[SUMS] = sums
    halo_out[0] = west
    halo_out[1] = east


def copy_kernel(field_ref, out_ref):
    out_ref[...] = field_ref[...]


def finish_kernel(size, radix, cells_all, *refs):
    pack_ref, others, halo_ref = refs[0], refs[1:radix], refs[radix]
    residual_ref = refs[radix + 1]
    residual_out, norms_out, packs = refs[radix + 2 :]
    sums, *pushes = join_packs(size, radix, True, pack_ref, others, (halo_ref[0], halo_ref[1]), packs)
    west, east = (
        jnp.concatenate([push[i : i + 1] for i in range(push.shape[0])], axis=1) for push in pushes
    )
    residual_out[...] = add_sides(residual_ref[...], west, east)
    for k in range(ITERS):
        norms_out[k] = jnp.sum(sums[k : k + 1]) / cells_all


def vmem():
    return pl.BlockSpec(memory_space=pltpu.VMEM)


def shape(*dims):
    return jax.ShapeDtypeStruct(dims, F32)


def smem():
    return pl.BlockSpec(memory_space=pltpu.SMEM)


def call(body, in_specs, outs, scratch, limit, cost=None, out_specs=None):
    return pl.pallas_call(
        body,
        in_specs=in_specs,
        out_specs=out_specs or [vmem()] * len(outs),
        out_shape=outs,
        scratch_shapes=scratch,
        compiler_params=pltpu.CompilerParams(vmem_limit_bytes=limit),
        cost_estimate=cost,
    )


def exchange(inner, outer):
    devices = lax.axis_size("lon")
    pairs = [(i, i ^ 1) for i in range(devices)]
    across = [(i, (i + 1 if i % 2 else i - 1) % devices) for i in range(devices)]
    return lax.ppermute(inner, "lon", pairs), lax.ppermute(outer, "lon", across)


def exchange_beyond(near, far):
    devices = lax.axis_size("lon")
    within = [(i, i ^ 2) for i in range(devices)]
    across = [(i, (i + 2 if i % 4 >= 2 else i - 2) % devices) for i in range(devices)]
    return lax.ppermute(near, "lon", within), lax.ppermute(far, "lon", across)


def swap_runs(pack, size, radix):
    devices = lax.axis_size("lon")
    return [
        lax.ppermute(pack, "lon", [(i, i ^ (s * size)) for i in range(devices)]) for s in swap_order(size, radix)
    ]


def on_device(
    right_side, east_coef, north_coef, surface_term, cell_mask, inverse_blocks, active_tiles, low_bound, high_bound
):
    columns, rows = right_side.shape
    tiles = inverse_blocks.shape[0]
    count = lane_blocks(rows)
    field = shape(columns, rows)
    row = shape(1, rows)
    two = shape(2, rows)
    bt_shape = shape(count, columns, LANES, LANES)
    (bt,) = call(
        transpose_kernel,
        [pl.BlockSpec(memory_space=pl.ANY)],
        [bt_shape],
        [pltpu.VMEM(inverse_blocks.shape, F32), pltpu.SemaphoreType.DMA((count,))],
        40 * MIB,
        pl.CostEstimate(flops=10**9, bytes_accessed=2 * inverse_blocks.size * 4, transcendentals=0),
    )(inverse_blocks)
    pair_shape = shape(PAIR_ROWS, rows)
    residual, search, diag, east_face, north_face, ocean, east_end, flow, inner, outer, near, far = call(
        first_kernel,
        [vmem()] * 7,
        [field, field, field, field, field, field, row, field, pair_shape, pair_shape, two, two],
        [],
        24 * MIB,
    )(active_tiles.reshape(-1, LANES), right_side, east_coef, north_coef, surface_term, cell_mask, bt)
    low_bound, high_bound, outer = lax.optimization_barrier((low_bound, high_bound, outer))
    inner, outer = exchange(inner, outer)
    near, far = exchange_beyond(near, far)
    work = pl.CostEstimate(flops=2 * bt.size, bytes_accessed=4 * bt.size, transcendentals=0)
    (product,) = call(product_kernel, [vmem()] * 2, [field], [], 24 * MIB, work)(bt, flow)
    residual, direction, diag, faces, norms, coef, inner, outer = call(
        second_kernel,
        [smem()] * 2 + [vmem()] * 14,
        [field, field, field, two, row, shape(SUBS, LANES), row, row],
        [],
        24 * MIB,
    )(
        low_bound, high_bound, far, outer, near, inner, residual, search, flow, product, diag, east_face, north_face,
        ocean, east_end, bt,
    )
    inner, outer = exchange(inner, outer)
    residual, direction, answer, product, norms = call(
        ahead_kernel,
        [vmem()] * 10,
        [field, field, field, field, row],
        [],
        24 * MIB,
        work,
    )(residual, direction, search, diag, east_face, north_face, ocean, coef, norms, bt)
    pack_shape = shape(PACK_PARTS, count, LANES)
    residual, answer, pack = call(closing_kernel, [vmem()] * 14, [field, field, pack_shape], [], 24 * MIB)(
        outer, inner, residual, direction, answer, product, diag, east_face, north_face, ocean, faces, coef, norms, bt
    )
    (answer,) = call(copy_kernel, [vmem()], [field], [], 24 * MIB, work)(answer)
    devices = lax.axis_size("lon")
    size, halo = 1, []
    while True:
        radix = 4 if (devices // size) % 4 == 0 else 2
        others = swap_runs(pack, size, radix)
        packs = [pltpu.VMEM((radix, PACK_PARTS, count, LANES), F32)]
        if size * radix == devices:
            break
        pack, *halo = call(
            functools.partial(stage_kernel, size, radix),
            [vmem()] * (radix + len(halo)),
            [pack_shape, shape(2, count, LANES)],
            packs,
            24 * MIB,
        )(pack, *others, *halo)
        size *= radix
    residual, norms = call(
        functools.partial(finish_kernel, size, radix, float(columns * devices * rows)),
        [vmem()] * (radix + 2),
        [field, shape(ITERS)],
        packs,
        24 * MIB,
        out_specs=[vmem(), smem()],
    )(pack, *others, *halo, residual)
    return answer, residual, norms


def solution(mesh):
    in_specs = (
        P(("member", "lon"), None),
        P("lon", None),
        P("lon", None),
        P("lon", None),
        P("lon", None),
        P("lon", None, None),
        P(),
        P(),
        P(),
    )
    out_specs = (P(("member", "lon"), None), P(("member", "lon"), None), P("member"))
    return jax.shard_map(on_device, mesh=mesh, in_specs=in_specs, out_specs=out_specs, check_vma=False)
```
